32 devices in a mesh: dp: 8 (over y, x, core), seq: 4 (over z).
Axes of the slice: x: 2, y: 2, z: 4, core: 2. Of those that a mesh axis runs over, the one named last changes fastest.
Arguments:
- inputs: bfloat16 [512, 32, 1024], P('seq', 'dp'), may hold values from -6 to 6
- memory: bfloat16 [512, 32, 1024], P('seq', 'dp'), may hold values from -6 to 6
- compressed: bfloat16 [512, 32, 1024], P('seq', 'dp'), may hold values from -6 to 6
- seg_len: int32 [32], P('dp'), may hold values from 128 to 512, as said below
- gain_first: float32 [1024], replicated, may hold values from 0.5 to 1.5
- shift_first: float32 [1024], replicated, may hold values from -1.75 to 1.75
- w_query: bfloat16 [1024, 1024], replicated, may hold values from -0.1875 to 0.1875
- w_key: bfloat16 [1024, 1024], replicated, may hold values from -0.1875 to 0.1875
- w_value: bfloat16 [1024, 1024], replicated, may hold values from -0.1875 to 0.1875
- w_rel: bfloat16 [1024, 1024], replicated, may hold values from -0.1875 to 0.1875
- bias_content: float32 [1024], replicated, may hold values from -3 to 3
- bias_position: float32 [1024], replicated, may hold values from -3 to 3
- w_out: bfloat16 [1024, 1024], replicated, may hold values from -0.75 to 0.75
- gain_second: float32 [1024], replicated, may hold values from 0.5 to 1.5
- shift_second: float32 [1024], replicated, may hold values from -1.75 to 1.75
- w_up: bfloat16 [1024, 4096], P(None, 'seq'), may hold values from -0.1875 to 0.1875
- bias_up: bfloat16 [4096], P('seq'), may hold values from -3 to 3
- w_down: bfloat16 [4096, 1024], P('seq'), may hold values from -0.09375 to 0.09375
- bias_down: float32 [1024], replicated, may hold values from -1.75 to 1.75
- w_comp: bfloat16 [3, 1024, 1024], P(None, None, 'seq'), may hold values from -0.109375 to 0.109375
- comp_bias: float32 [1024], P('seq'), may hold values from -1.75 to 1.75
- grad_out: bfloat16 [512, 32, 1024], P('seq', 'dp'), may hold values from -6 to 6
- grad_comp: bfloat16 [170, 32, 1024], P(None, 'dp', 'seq'), may hold values from -6 to 6
Outputs:
- output: bfloat16 [512, 32, 1024], P('seq', 'dp')
- grad_inputs: bfloat16 [512, 32, 1024], P('seq', 'dp')
- new_compressed: bfloat16 [170, 32, 1024], P(None, 'dp', 'seq')
- grad_gain_first: float32 [1024], replicated
- grad_shift_first: float32 [1024], replicated
- grad_w_query: float32 [1024, 1024], replicated
- grad_w_key: float32 [1024, 1024], replicated
- grad_w_value: float32 [1024, 1024], replicated
- grad_w_rel: float32 [1024, 1024], replicated
- grad_bias_content: float32 [1024], replicated
- grad_bias_position: float32 [1024], replicated
- grad_w_out: float32 [1024, 1024], replicated
- grad_gain_second: float32 [1024], replicated
- grad_shift_second: float32 [1024], replicated
- grad_w_up: float32 [1024, 4096], P(None, 'seq')
- grad_bias_up: float32 [4096], P('seq')
- grad_w_down: float32 [4096, 1024], P('seq')
- grad_bias_down: float32 [1024], replicated
- grad_w_comp: float32 [3, 1024, 1024], P(None, None, 'seq')
- grad_comp_bias: float32 [1024], P('seq')
The draws below stay inside these ranges and needn't reach their ends.
Inputs may be any that keep to these rules, and one draw needn't show every extreme that they name: `seg_len`: each stream's true length is a quarter of 512, half of 512 or 512; among the 4 streams of each index of dp at least one has length 512.
All inputs are finite; a program needn't handle non-finite values.
Results may differ from the reference program's by a relative error of at most 0.017.
Values may be sent and summed in bfloat16 or wider, within the bound.
No kernel may reach another device: no remote copies, remote signals or barrier semaphores. Data moves between devices by JAX's collectives and lax.ppermute only.
A program may use at most 320 MiB of HBM per device.

```python
import math
import jax
import jax.numpy as jnp
from jax import lax

D = 1024
H = 8
DH = 128
FF = 4096
SDEV = 4
SEG = 512
MEM = 512
CMEM = 512
RATE = 3
STREAMS = 32
CTX = 1536
CNEW = 170


def draw_seg_len(key, part):
    key = jax.random.fold_in(key, 7)
    level_key, pick_key = jax.random.split(key)
    levels = jax.random.randint(level_key, (STREAMS,), 0, 3)
    lengths = jnp.where(levels == 0, SEG // 4, jnp.where(levels == 1, SEG // 2, SEG))
    chosen = jax.random.randint(pick_key, (STREAMS // SDEV,), 0, SDEV)
    stream_ids = jnp.arange(STREAMS, dtype=jnp.int32)
    longest = stream_ids % SDEV == chosen[stream_ids // SDEV]
    return jnp.where(longest, SEG, lengths).astype(jnp.int32)


def block_scale(own_key, dims, cuts, least, high):
    level, own = 1.0, jax.random.fold_in(own_key, 6)
    for position, blocks in cuts:
        draws = jnp.exp(jax.random.uniform(jax.random.fold_in(own, position), (blocks,), jnp.float32, least / len(cuts), high / len(cuts)))
        level = level * jnp.repeat(draws, dims[position] // blocks).reshape([-1 if axis == position else 1 for axis in range(len(dims))])
    return level


def scatter_about(stream_key, dims, scale, bound, cuts=(), held_as=jnp.bfloat16):
    level = block_scale(stream_key, dims, cuts, -0.22, 0.18) if cuts else 1.0
    entries = jax.random.normal(stream_key, dims, jnp.float32) * scale * level
    return jnp.minimum(jnp.maximum(entries, -bound), bound).astype(held_as)


def setup_inputs(seed: int = 0) -> dict:
    splits = jax.random.split(jax.random.key(seed), 24)
    inputs = scatter_about(splits[0], (SEG, STREAMS, D), 1.0, 6.0, ((0, 4), (1, 8)))
    memory = scatter_about(splits[1], (MEM, STREAMS, D), 1.0, 6.0, ((0, 4), (1, 8)))
    compressed = scatter_about(splits[2], (CMEM, STREAMS, D), 1.0, 6.0, ((0, 4), (1, 8)))
    seg_len = draw_seg_len(jax.random.fold_in(splits[23], 71), 0)
    gain_first = jnp.clip(1.0 + 0.1 * jax.random.normal(splits[4], (D,), jnp.float32), 0.5, 1.5)
    shift_first = scatter_about(splits[5], (D,), 0.3, 1.75, (), jnp.float32)
    w_query = scatter_about(splits[6], (D, D), D ** -0.5, 0.1875)
    w_key = scatter_about(splits[7], (D, D), D ** -0.5, 0.1875)
    w_value = scatter_about(splits[8], (D, D), D ** -0.5, 0.1875)
    w_rel = scatter_about(splits[9], (D, D), D ** -0.5, 0.1875)
    bias_content = scatter_about(splits[10], (D,), 0.5, 3.0, (), jnp.float32)
    bias_position = scatter_about(splits[11], (D,), 0.5, 3.0, (), jnp.float32)
    w_out = scatter_about(splits[12], (D, D), (D // 16) ** -0.5, 0.75)
    gain_second = jnp.clip(1.0 + 0.1 * jax.random.normal(splits[13], (D,), jnp.float32), 0.5, 1.5)
    shift_second = scatter_about(splits[14], (D,), 0.3, 1.75, (), jnp.float32)
    w_up = scatter_about(splits[15], (D, FF), D ** -0.5, 0.1875, ((1, 4),))
    bias_up = scatter_about(splits[16], (FF,), 0.5, 3.0, ((0, 4),))
    w_down = scatter_about(splits[17], (FF, D), FF ** -0.5, 0.09375, ((0, 4),))
    bias_down = scatter_about(splits[18], (D,), 0.3, 1.75, (), jnp.float32)
    w_comp = scatter_about(splits[19], (RATE, D, D), (RATE * D) ** -0.5, 0.109375, ((2, 4),))
    comp_bias = scatter_about(splits[20], (D,), 0.3, 1.75, ((0, 4),), jnp.float32)
    grad_out = scatter_about(splits[21], (SEG, STREAMS, D), 1.0, 6.0, ((0, 4), (1, 8)))
    grad_comp = scatter_about(splits[22], (CNEW, STREAMS, D), 1.0, 6.0, ((1, 8), (2, 4)))
    return {"inputs": inputs, "memory": memory, "compressed": compressed, "seg_len": seg_len, "gain_first": gain_first, "shift_first": shift_first, "w_query": w_query, "w_key": w_key, "w_value": w_value, "w_rel": w_rel, "bias_content": bias_content, "bias_position": bias_position, "w_out": w_out, "gain_second": gain_second, "shift_second": shift_second, "w_up": w_up, "bias_up": bias_up, "w_down": w_down, "bias_down": bias_down, "w_comp": w_comp, "comp_bias": comp_bias, "grad_out": grad_out, "grad_comp": grad_comp}


@jax.custom_vjp
def low(v):
    return lax.optimization_barrier(v.astype(jnp.bfloat16)).astype(jnp.float32)

@jax.custom_vjp
def low_back(v):
    return v

def low_keep(v):
    return (low(v), None)

def low_pass(kept, grad):
    return (grad,)

def back_keep(v):
    return (v, None)

def back_low(kept, grad):
    return (low(grad),)
low.defvjp(low_keep, low_pass)
low_back.defvjp(back_keep, back_low)

def layer_norm(values, gain, shift):
    center = values - lax.optimization_barrier(jnp.mean(values, -1, keepdims=True))
    spread = lax.optimization_barrier(jnp.mean(center * center, -1, keepdims=True))
    return center * lax.rsqrt(spread + 1e-05) * gain + shift

def gelu_tanh(values):
    return jax.nn.gelu(values, approximate=True)

def sinusoids(positions):
    half_width = D // 2
    frequency = jnp.exp(jnp.arange(half_width, dtype=jnp.float32) * (-2.0 * math.log(10000.0) / D))
    angles = positions.astype(jnp.float32)[:, None] * frequency[None, :]
    return (jnp.cos(angles), jnp.sin(angles))

def reference(inputs, memory, compressed, seg_len, gain_first, shift_first, w_query, w_key, w_value, w_rel, bias_content, bias_position, w_out, gain_second, shift_second, w_up, bias_up, w_down, bias_down, w_comp, comp_bias, grad_out, grad_comp):
    highest = lax.Precision.HIGHEST
    score_scale = 1.0 / math.sqrt(DH)
    half_width = D // 2
    key_cos, key_sin = sinusoids(jnp.arange(CTX, dtype=jnp.int32))
    pos_table = low(jnp.concatenate([key_cos, key_sin], -1))
    query_cos, query_sin = sinusoids(CMEM + MEM + jnp.arange(SEG, dtype=jnp.int32))
    query_cos = query_cos[:, None, :]
    query_sin = query_sin[:, None, :]
    key_seg = jnp.arange(CTX, dtype=jnp.int32) - (CMEM + MEM)
    query_seg = jnp.arange(SEG, dtype=jnp.int32)
    memory_f = memory.astype(jnp.float32)
    mem_streams = jnp.moveaxis(memory_f, 1, 0)
    cmem_streams = jnp.moveaxis(compressed.astype(jnp.float32), 1, 0)

    def stream_fn(params, pieces):
        gain_one, shift_one, query_w, key_w, value_w, rel_w, content_b, position_b, out_w, gain_two, shift_two, up_w, up_b, down_w, down_b = params
        x_rows, mem_rows, cmem_rows, length = pieces
        context = jnp.concatenate([cmem_rows, mem_rows, x_rows], 0)
        normed = low(layer_norm(context, gain_one, shift_one))
        queries = low_back(jnp.dot(normed[CMEM + MEM:], query_w, precision=highest))
        keys_h = low(low_back(jnp.dot(normed, key_w, precision=highest))).reshape(CTX, H, DH)
        values_h = low(low_back(jnp.dot(normed, value_w, precision=highest))).reshape(CTX, H, DH)
        query_content = low(queries + content_b).reshape(SEG, H, DH)
        query_position = low(queries + position_b).reshape(SEG, H, DH)
        mixed = low_back(jnp.einsum('qhd,fhd->qhf', query_position, rel_w.reshape(D, H, DH), precision=highest))
        first_half = mixed[..., :half_width]
        second_half = mixed[..., half_width:]
        rotated = low(jnp.concatenate([first_half * query_sin + second_half * query_cos, second_half * query_sin - first_half * query_cos], -1))
        content = jnp.einsum('qhd,khd->hqk', query_content, keys_h, precision=highest)
        placed = jnp.einsum('qhf,kf->hqk', rotated, pos_table, precision=highest)
        scores = low_back((content + placed) * score_scale)
        visible = (key_seg[None, :] < 0) | (key_seg[None, :] <= query_seg[:, None]) & (key_seg[None, :] < length)
        scores = jnp.where(visible[None], scores, -1e+30)
        attn_prob = low(jax.nn.softmax(scores, -1))
        attended = jnp.einsum('hqk,khd->qhd', attn_prob, values_h, precision=highest).reshape(SEG, D)
        attn_out = low_back(low(attended))
        branch = low_back(jnp.dot(attn_out, out_w, precision=highest))
        hidden = x_rows + branch
        normed_two = low(layer_norm(hidden, gain_two, shift_two))
        pre_act = low_back(jnp.dot(normed_two, up_w, precision=highest) + up_b)
        activated = low(gelu_tanh(pre_act))
        return hidden + jnp.dot(activated, down_w, precision=highest) + down_b

    def forward(x_all, params, comp_weight, comp_shift):

        def stream_step(carry, pieces):
            return (carry, jax.checkpoint(stream_fn)(params, pieces))
        _, results = lax.scan(stream_step, None, (jnp.moveaxis(x_all, 1, 0), mem_streams, cmem_streams, seg_len))
        windows = memory_f[:CNEW * RATE].reshape(CNEW, RATE, STREAMS, D)
        new_comp = jnp.einsum('rtsd,tde->rse', windows, comp_weight, precision=highest) + comp_shift
        return (jnp.moveaxis(results, 0, 1), new_comp)
    params = (gain_first, shift_first, w_query.astype(jnp.float32), w_key.astype(jnp.float32), w_value.astype(jnp.float32), w_rel.astype(jnp.float32), bias_content, bias_position, w_out.astype(jnp.float32), gain_second, shift_second, w_up.astype(jnp.float32), bias_up.astype(jnp.float32), w_down.astype(jnp.float32), bias_down)
    primal, pullback = jax.vjp(forward, inputs.astype(jnp.float32), params, w_comp.astype(jnp.float32), comp_bias)
    grad_x, grad_params, grad_wc, grad_bc = pullback((grad_out.astype(jnp.float32), grad_comp.astype(jnp.float32)))
    result_rows, new_comp = primal
    return (result_rows.astype(jnp.bfloat16), grad_x.astype(jnp.bfloat16), new_comp.astype(jnp.bfloat16), grad_params[0], grad_params[1], grad_params[2], grad_params[3], grad_params[4], grad_params[5], grad_params[6], grad_params[7], grad_params[8], grad_params[9], grad_params[10], grad_params[11], grad_params[12], grad_params[13], grad_params[14], grad_wc, grad_bc)
```

```python
import functools
import math

import jax
import jax.numpy as jnp
from jax import lax
from jax.experimental import pallas as pl
from jax.experimental.pallas import tpu as pltpu
from jax.sharding import PartitionSpec as P

D = 1024
H = 8
DH = 128
MEM = 512
CMEM = 512
RATE = 3


def layer_norm(values, gain, shift):
    center = values - jnp.mean(values, -1, keepdims=True)
    spread = jnp.mean(center * center, -1, keepdims=True)
    return center * lax.rsqrt(spread + 1e-05) * gain + shift


def gelu_tanh(values):
    return jax.nn.gelu(values, approximate=True)


def sinusoids(positions):
    half_width = D // 2
    frequency = jnp.exp(jnp.arange(half_width, dtype=jnp.float32) * (-2.0 * math.log(10000.0) / D))
    angles = positions.astype(jnp.float32)[:, None] * frequency[None, :]
    return (jnp.cos(angles), jnp.sin(angles))


def key_positions(seq_parts, cmem_dev, mem_dev, seg_dev):
    ctx_dev = cmem_dev + mem_dev + seg_dev
    row_ids = jnp.arange(ctx_dev * seq_parts, dtype=jnp.int32)
    device_ids = row_ids // ctx_dev
    local_ids = row_ids % ctx_dev
    in_cmem = device_ids * cmem_dev + local_ids
    in_mem = CMEM + device_ids * mem_dev + (local_ids - cmem_dev)
    in_seg = CMEM + MEM + device_ids * seg_dev + (local_ids - cmem_dev - mem_dev)
    return jnp.where(
        local_ids < cmem_dev, in_cmem, jnp.where(local_ids < cmem_dev + mem_dev, in_mem, in_seg)
    )


def rotate_rows(position_rows, rel_heads, row_sin, row_cos, half_width):
    mixed = jnp.einsum(
        "qshd,fhd->qshf", position_rows, rel_heads, preferred_element_type=jnp.float32
    )
    first_half = mixed[..., :half_width]
    second_half = mixed[..., half_width:]
    return jnp.concatenate(
        [
            first_half * row_sin + second_half * row_cos,
            second_half * row_sin - first_half * row_cos,
        ],
        -1,
    ).astype(jnp.bfloat16)


def split_rows_plan(
    inputs,
    memory,
    compressed,
    seg_len,
    gain_first,
    shift_first,
    w_query,
    w_key,
    w_value,
    w_rel,
    bias_content,
    bias_position,
    w_out,
    gain_second,
    shift_second,
    w_up,
    bias_up,
    w_down,
    bias_down,
    w_comp,
    comp_bias,
    grad_out,
    grad_comp,
):
    seq_parts = lax.axis_size("seq")
    my_index = lax.axis_index("seq")
    seg_dev, streams, model_width = inputs.shape
    mem_dev = memory.shape[0]
    cmem_dev = compressed.shape[0]
    split_at = cmem_dev + mem_dev
    ctx_dev = split_at + seg_dev
    total_keys = ctx_dev * seq_parts
    half_width = model_width // 2
    score_scale = 1.0 / math.sqrt(DH)
    key_pos = key_positions(seq_parts, cmem_dev, mem_dev, seg_dev)
    key_cos, key_sin = sinusoids(key_pos)
    pos_table = jnp.concatenate([key_cos, key_sin], -1).astype(jnp.bfloat16)
    query_rows = my_index * seg_dev + jnp.arange(seg_dev, dtype=jnp.int32)
    query_cos, query_sin = sinusoids(CMEM + MEM + query_rows)
    query_cos = query_cos[:, None, None, :]
    query_sin = query_sin[:, None, None, :]
    key_seg = key_pos - (CMEM + MEM)
    visible = (key_seg[None, None, :] < 0) | (
        key_seg[None, None, :] <= query_rows[None, :, None]
    ) & (key_seg[None, None, :] < seg_len[:, None, None])
    x_in = inputs.astype(jnp.float32)
    context = jnp.concatenate([compressed, memory, inputs], 0).astype(jnp.float32)
    normed = layer_norm(context, gain_first, shift_first)
    normed_low = normed.astype(jnp.bfloat16)
    seg_normed = normed_low[split_at:]
    queries = jnp.dot(seg_normed, w_query, preferred_element_type=jnp.float32)
    keys_low = jnp.dot(normed_low, w_key, preferred_element_type=jnp.float32).astype(jnp.bfloat16)
    values_low = jnp.dot(normed_low, w_value, preferred_element_type=jnp.float32).astype(
        jnp.bfloat16
    )
    query_content = (queries + bias_content).astype(jnp.bfloat16).reshape(seg_dev, streams, H, DH)
    query_position = (queries + bias_position).astype(jnp.bfloat16).reshape(seg_dev, streams, H, DH)
    rel_heads = w_rel.reshape(model_width, H, DH)
    rotated = rotate_rows(query_position, rel_heads, query_sin, query_cos, half_width)
    keys_all, values_all, memory_all = (
        lax.all_gather(keys_low, "seq", axis=0, tiled=True),
        lax.all_gather(values_low, "seq", axis=0, tiled=True),
        lax.all_gather(memory, "seq", axis=0, tiled=True),
    )

    def scores_of(keys_gathered):
        content = jnp.einsum(
            "qshd,kshd->shqk",
            query_content,
            keys_gathered.reshape(total_keys, streams, H, DH),
            preferred_element_type=jnp.float32,
        )
        placed = jnp.einsum("qshf,kf->shqk", rotated, pos_table, preferred_element_type=jnp.float32)
        return jnp.where(visible[:, None], (content + placed) * score_scale, -1e30)

    scores = scores_of(keys_all)
    row_max = jnp.max(scores, -1, keepdims=True)
    exp_scores = jnp.exp(scores - row_max)
    row_total = jnp.sum(exp_scores, -1, keepdims=True)
    attn_prob = (exp_scores / row_total).astype(jnp.bfloat16)
    log_total = row_max + jnp.log(row_total)
    attended = jnp.einsum(
        "shqk,kshd->qshd",
        attn_prob,
        values_all.reshape(total_keys, streams, H, DH),
        preferred_element_type=jnp.float32,
    )
    attn_out = attended.reshape(seg_dev, streams, model_width).astype(jnp.bfloat16)
    hidden = x_in + jnp.dot(attn_out, w_out, preferred_element_type=jnp.float32)
    normed_two = layer_norm(hidden, gain_second, shift_second).astype(jnp.bfloat16)
    normed_all = lax.all_gather(normed_two, "seq", axis=0, tiled=True)
    pre_act = jnp.dot(normed_all, w_up, preferred_element_type=jnp.float32) + bias_up.astype(
        jnp.float32
    )
    activated = gelu_tanh(pre_act).astype(jnp.bfloat16)
    row_piece = activated
    ffn_result = lax.psum_scatter(
        jnp.dot(row_piece, w_down, preferred_element_type=jnp.float32).astype(jnp.bfloat16),
        "seq",
        scatter_dimension=0,
        tiled=True,
    ).astype(jnp.float32)
    output = (hidden + ffn_result + bias_down).astype(jnp.bfloat16)
    grad_all = lax.all_gather(grad_out, "seq", axis=0, tiled=True)
    d_activated = jnp.einsum("rsd,fd->rsf", grad_all, w_down, preferred_element_type=jnp.float32)
    _, gelu_back = jax.vjp(gelu_tanh, pre_act)
    d_pre = gelu_back(d_activated)[0].astype(jnp.bfloat16)
    grad_w_down = jnp.einsum("rsf,rsd->fd", activated, grad_all, preferred_element_type=jnp.float32)
    grad_w_up = jnp.einsum("rsd,rsf->df", normed_all, d_pre, preferred_element_type=jnp.float32)
    grad_bias_up = jnp.sum(d_pre.astype(jnp.float32), (0, 1))
    row_piece = d_pre
    d_normed_two = lax.psum_scatter(
        jnp.einsum("rsf,df->rsd", row_piece, w_up, preferred_element_type=jnp.float32).astype(
            jnp.bfloat16
        ),
        "seq",
        scatter_dimension=0,
        tiled=True,
    ).astype(jnp.float32)
    _, norm_two_back = jax.vjp(layer_norm, hidden, gain_second, shift_second)
    d_hidden_ffn, grad_gain_second, grad_shift_second = norm_two_back(d_normed_two)
    grad_rows_f = grad_out.astype(jnp.float32)
    d_hidden = grad_rows_f + d_hidden_ffn
    grad_bias_down = jnp.sum(grad_rows_f, (0, 1))
    d_branch = d_hidden.astype(jnp.bfloat16)
    grad_w_out = jnp.einsum("rsd,rse->de", attn_out, d_branch, preferred_element_type=jnp.float32)
    d_attn = (
        jnp.einsum("rse,de->rsd", d_branch, w_out, preferred_element_type=jnp.float32)
        .astype(jnp.bfloat16)
        .reshape(seg_dev, streams, H, DH)
    )
    keys_back, values_back = (
        lax.all_gather(keys_low, "seq", axis=0, tiled=True),
        lax.all_gather(values_low, "seq", axis=0, tiled=True),
    )
    keys_heads = keys_back.reshape(total_keys, streams, H, DH)
    values_heads = values_back.reshape(total_keys, streams, H, DH)
    prob_full = jnp.exp(scores_of(keys_back) - log_total)
    prob_low = prob_full.astype(jnp.bfloat16)
    d_prob = jnp.einsum("qshd,kshd->shqk", d_attn, values_heads, preferred_element_type=jnp.float32)
    inner_sum = jnp.sum(d_prob * prob_full, -1, keepdims=True)
    d_scores = (prob_full * (d_prob - inner_sum)).astype(jnp.bfloat16)
    key_part = (
        jnp.einsum("shqk,qshd->kshd", d_scores, query_content, preferred_element_type=jnp.float32)
        * score_scale
    )
    value_part = jnp.einsum("shqk,qshd->kshd", prob_low, d_attn, preferred_element_type=jnp.float32)
    key_sums = lax.psum_scatter(
        jnp.concatenate(
            [
                key_part.reshape(ctx_dev * lax.axis_size("seq"), streams, model_width),
                value_part.reshape(ctx_dev * lax.axis_size("seq"), streams, model_width),
            ],
            -1,
        ).astype(jnp.bfloat16),
        "seq",
        scatter_dimension=0,
        tiled=True,
    ).astype(jnp.float32)
    d_keys = key_sums[..., :model_width].astype(jnp.bfloat16)
    d_values = key_sums[..., model_width:].astype(jnp.bfloat16)
    d_content = (
        jnp.einsum("shqk,kshd->qshd", d_scores, keys_heads, preferred_element_type=jnp.float32)
        * score_scale
    )
    d_rotated = (
        jnp.einsum("shqk,kf->qshf", d_scores, pos_table, preferred_element_type=jnp.float32)
        * score_scale
    )
    lead_part = d_rotated[..., :half_width]
    tail_part = d_rotated[..., half_width:]
    d_mixed = jnp.concatenate(
        [
            lead_part * query_sin - tail_part * query_cos,
            lead_part * query_cos + tail_part * query_sin,
        ],
        -1,
    ).astype(jnp.bfloat16)
    d_query_pos = jnp.einsum(
        "qshf,fhd->qshd", d_mixed, rel_heads, preferred_element_type=jnp.float32
    )
    grad_w_rel = jnp.einsum(
        "qshf,qshd->fhd", d_mixed, query_position, preferred_element_type=jnp.float32
    ).reshape(model_width, model_width)
    grad_bias_content = jnp.sum(d_content, (0, 1)).reshape(model_width)
    grad_bias_position = jnp.sum(d_query_pos, (0, 1)).reshape(model_width)
    d_queries = (
        (d_content + d_query_pos).reshape(seg_dev, streams, model_width).astype(jnp.bfloat16)
    )
    grad_w_query = jnp.einsum(
        "rsd,rse->de", seg_normed, d_queries, preferred_element_type=jnp.float32
    )
    grad_w_key = jnp.einsum("rsd,rse->de", normed_low, d_keys, preferred_element_type=jnp.float32)
    grad_w_value = jnp.einsum(
        "rsd,rse->de", normed_low, d_values, preferred_element_type=jnp.float32
    )
    d_from_kv = jnp.einsum(
        "rse,de->rsd", d_keys, w_key, preferred_element_type=jnp.float32
    ) + jnp.einsum("rse,de->rsd", d_values, w_value, preferred_element_type=jnp.float32)
    d_from_query = jnp.einsum("rse,de->rsd", d_queries, w_query, preferred_element_type=jnp.float32)
    d_normed = jnp.concatenate([d_from_kv[:split_at], d_from_kv[split_at:] + d_from_query], 0)
    _, norm_one_back = jax.vjp(layer_norm, context, gain_first, shift_first)
    d_context, grad_gain_first, grad_shift_first = norm_one_back(d_normed)
    grad_inputs = (d_hidden + d_context[split_at:]).astype(jnp.bfloat16)
    new_rows = memory_all.shape[0] // RATE
    windows = memory_all[: new_rows * RATE].reshape(new_rows, RATE, streams, model_width)
    new_compressed = (
        jnp.einsum("rtsd,tde->rse", windows, w_comp, preferred_element_type=jnp.float32) + comp_bias
    ).astype(jnp.bfloat16)
    grad_w_comp = jnp.einsum(
        "rtsd,rse->tde", windows, grad_comp, preferred_element_type=jnp.float32
    )
    grad_comp_bias = jnp.sum(grad_comp.astype(jnp.float32), (0, 1))
    (
        grad_w_query,
        grad_w_key,
        grad_w_value,
        grad_w_rel,
        grad_w_out,
        grad_bias_content,
        grad_bias_position,
        grad_gain_first,
        grad_shift_first,
        grad_gain_second,
        grad_shift_second,
        grad_bias_down,
    ) = lax.psum(
        (
            grad_w_query,
            grad_w_key,
            grad_w_value,
            grad_w_rel,
            grad_w_out,
            grad_bias_content,
            grad_bias_position,
            grad_gain_first,
            grad_shift_first,
            grad_gain_second,
            grad_shift_second,
            grad_bias_down,
        ),
        ("dp", "seq"),
    )
    grad_w_up, grad_bias_up, grad_w_down, grad_w_comp, grad_comp_bias = (
        lax.psum(grad_w_up.astype(jnp.bfloat16), "dp").astype(jnp.float32),
        lax.psum(grad_bias_up.astype(jnp.bfloat16), "dp").astype(jnp.float32),
        lax.psum(grad_w_down.astype(jnp.bfloat16), "dp").astype(jnp.float32),
        lax.psum(grad_w_comp.astype(jnp.bfloat16), "dp").astype(jnp.float32),
        lax.psum(grad_comp_bias.astype(jnp.bfloat16), "dp").astype(jnp.float32),
    )
    return (
        output,
        grad_inputs,
        new_compressed,
        grad_gain_first,
        grad_shift_first,
        grad_w_query,
        grad_w_key,
        grad_w_value,
        grad_w_rel,
        grad_bias_content,
        grad_bias_position,
        grad_w_out,
        grad_gain_second,
        grad_shift_second,
        grad_w_up,
        grad_bias_up,
        grad_w_down,
        grad_bias_down,
        grad_w_comp,
        grad_comp_bias,
    )


BF16 = jnp.bfloat16
F32 = jnp.float32
QUERY_BLOCK = 256
HEADS_A_CALL = 2
VMEM_LIMIT = 48 * 1024 * 1024
SHORT = pl.CostEstimate(flops=1024, bytes_accessed=1024, transcendentals=0)


def contract(left, right, left_dim, right_dim):
    return lax.dot_general(
        left, right, (((left_dim,), (right_dim,)), ((), ())), preferred_element_type=F32
    )


def bit_of(axis, distance):
    return (lax.axis_index(axis) // distance) % 2


def swap(rows, axis, distance):
    count = lax.axis_size(axis)
    return lax.ppermute(rows, axis, [(i, i ^ distance) for i in range(count)])


def after(value, *others):
    return lax.optimization_barrier((value, *others))[0]


def pick(rows, which, dim):
    return lax.dynamic_index_in_dim(rows, which, dim, keepdims=False)


def halve(rows, step, dim=0):
    bit = bit_of(*step)
    got = swap(pick(rows, 1 - bit, dim).astype(BF16), *step)
    return pick(rows, bit, dim).astype(F32) + got.astype(F32)


def double(rows, step, dim=0):
    got = swap(rows, *step)
    second = bit_of(*step) == 1
    return jnp.stack([jnp.where(second, got, rows), jnp.where(second, rows, got)], dim)


def bits_below(count):
    return [1 << i for i in range(count.bit_length() - 1)]


def token(value):
    return (value[(0,) * value.ndim].astype(F32) * 0.0).astype(jnp.int32)


def to_streams(rows, count, order=0):
    me = lax.axis_index("seq")
    block = rows.shape[1]
    whole = jnp.zeros((count * block, rows.shape[2]), rows.dtype)
    for shift in range(count):
        part = pick(rows, (me + shift) % count + order, 0)
        if shift:
            part = lax.ppermute(part, "seq", [(i, (i + shift) % count) for i in range(count)])
        whole = lax.dynamic_update_slice_in_dim(whole, part, (me - shift) % count * block, 0)
    return whole


def by_stream(rows):
    return jnp.swapaxes(rows, 0, 1)


def attend_kernel(
    len_ref, qc_ref, qp_ref, k_ref, v_ref, rel_ref, table_ref, cos_ref, sin_ref, *rest
):
    p_ref, o_ref = rest[-2:]
    rows = qc_ref.shape[0]
    keys = k_ref.shape[0]
    half = cos_ref.shape[1]
    split = CMEM + MEM
    mixed = contract(qp_ref[...], rel_ref[...], 1, 1)
    lead, tail = mixed[:, :half], mixed[:, half:]
    cos, sin = cos_ref[...], sin_ref[...]
    rotated = jnp.concatenate(
        [(lead * sin + tail * cos).astype(BF16), (tail * sin - lead * cos).astype(BF16)], 1
    )
    scores = contract(qc_ref[...], k_ref[...], 1, 1) + contract(rotated, table_ref[...], 1, 1)
    scores = scores * (1.0 / math.sqrt(DH))
    row_ids = pl.program_id(1) * rows + lax.broadcasted_iota(jnp.int32, (rows, keys - split), 0)
    col_ids = lax.broadcasted_iota(jnp.int32, (rows, keys - split), 1)
    visible = (col_ids <= row_ids) & (col_ids < len_ref[0])
    past = scores[:, :split]
    own = jnp.where(visible, scores[:, split:], -1e30)
    top = jnp.maximum(jnp.max(past, 1, keepdims=True), jnp.max(own, 1, keepdims=True))
    past = jnp.exp(past - top)
    own = jnp.exp(own - top)
    total = jnp.sum(past, 1, keepdims=True) + jnp.sum(own, 1, keepdims=True)
    scale = 1.0 / total
    prob = jnp.concatenate([(past * scale).astype(BF16), (own * scale).astype(BF16)], 1)
    p_ref[0] = prob
    o_ref[...] = jnp.dot(prob, v_ref[...], preferred_element_type=F32).astype(BF16)


def attend(heads, length, content, position, keys, values, w_rel, table, cos, sin, first=(), into=()):
    seg, width = content.shape
    total = keys.shape[0]
    block = QUERY_BLOCK
    start, count = heads.start, len(heads)
    head = lambda h, q: (0, start + h)
    rows = lambda h, q: (q, start + h)
    whole = pl.BlockSpec(memory_space=pl.ANY)
    operands = [length, content, position, keys, values, w_rel, table, cos, sin]
    aliases = {len(operands) + i: i for i in range(len(into))}
    operands += [*into, *first]
    return pl.pallas_call(
        attend_kernel,
        grid=(count, seg // block),
        in_specs=[
            pl.BlockSpec(memory_space=pltpu.SMEM),
            pl.BlockSpec((block, DH), rows),
            pl.BlockSpec((block, DH), rows),
            pl.BlockSpec((total, DH), head),
            pl.BlockSpec((total, DH), head),
            pl.BlockSpec((width, DH), head),
            pl.BlockSpec((total, width), lambda h, q: (0, 0)),
            pl.BlockSpec((block, width // 2), lambda h, q: (q, 0)),
            pl.BlockSpec((block, width // 2), lambda h, q: (q, 0)),
        ]
        + [whole] * (len(into) + len(first)),
        out_specs=[
            pl.BlockSpec((1, block, total), lambda h, q: (start + h, q, 0)),
            pl.BlockSpec((block, DH), rows),
        ],
        out_shape=[
            jax.ShapeDtypeStruct((H, seg, total), BF16),
            jax.ShapeDtypeStruct((seg, width), BF16),
        ],
        input_output_aliases=aliases,
        compiler_params=pltpu.CompilerParams(vmem_limit_bytes=VMEM_LIMIT),
        cost_estimate=SHORT,
        name="attend",
    )(*operands)


def attend_back_kernel(
    with_sums,
    bits_ref,
    p_ref,
    da_ref,
    qc_ref,
    qp_ref,
    k_ref,
    v_ref,
    rel_ref,
    wq_ref,
    wk_ref,
    wv_ref,
    normed_ref,
    table_ref,
    cos_ref,
    sin_ref,
    *rest,
):
    keep_ref, give_ref, rows_ref, along_ref, shift_ref, bias_ref = rest[-10:-4]
    dk_sum, dv_sum, drel_sum, dq_all = rest[-4:]
    head, step = pl.program_id(0), pl.program_id(1)
    scale = 1.0 / math.sqrt(DH)
    half = cos_ref.shape[1]
    block = da_ref.shape[0]
    seg = dq_all.shape[0]

    @pl.when(step == 0)
    def _():
        dk_sum[...] = jnp.zeros_like(dk_sum)
        dv_sum[...] = jnp.zeros_like(dv_sum)
        drel_sum[...] = jnp.zeros_like(drel_sum)
        bias_ref[...] = jnp.zeros_like(bias_ref)

    prob = p_ref[0]
    d_attn = da_ref[...]
    dv_sum[...] += contract(prob, d_attn, 0, 0)
    d_prob = contract(d_attn, v_ref[...], 1, 1)
    prob_f = prob.astype(F32)
    weighted = prob_f * d_prob
    inner = jnp.sum(weighted, 1, keepdims=True)
    d_scores = (weighted - prob_f * inner).astype(BF16)
    dk_sum[...] += contract(d_scores, qc_ref[...], 0, 0)
    d_content = jnp.dot(d_scores, k_ref[...], preferred_element_type=F32) * scale
    d_rotated = jnp.dot(d_scores, table_ref[...], preferred_element_type=F32) * scale
    lead, tail = d_rotated[:, :half], d_rotated[:, half:]
    cos, sin = cos_ref[...], sin_ref[...]
    d_mixed = jnp.concatenate(
        [(lead * sin - tail * cos).astype(BF16), (lead * cos + tail * sin).astype(BF16)], 1
    )
    d_position = jnp.dot(d_mixed, rel_ref[...], preferred_element_type=F32)
    drel_sum[...] += contract(d_mixed, qp_ref[...], 0, 0)
    dq_all[pl.ds(pl.multiple_of(step * block, block), block), :] = (d_content + d_position).astype(
        BF16
    )
    bias_ref[...] += jnp.concatenate(
        [jnp.sum(d_content, 0, keepdims=True), jnp.sum(d_position, 0, keepdims=True)], 0
    )

    @pl.when(step == pl.num_programs(1) - 1)
    def _():
        d_key = (dk_sum[...] * scale).astype(BF16)
        d_value = dv_sum[...].astype(BF16)
        d_query = dq_all[...]
        past = d_key.shape[0] - seg
        of_kv = jnp.dot(
            normed_ref[...], jnp.concatenate([d_key, d_value], 1), preferred_element_type=F32
        )
        of_query = jnp.dot(normed_ref[:, past:], d_query, preferred_element_type=F32)
        mine = bits_ref[0] == 1
        for i, grad in enumerate((of_query, drel_sum[...], of_kv[:, :DH], of_kv[:, DH:])):
            middle = grad.shape[0] // 2
            low, high = grad[:middle].astype(BF16), grad[middle:].astype(BF16)
            keep_ref[i] = jnp.where(mine, high, low)
            give_ref[i] = jnp.where(mine, low, high)
        own_rows = (
            contract(d_query, wq_ref[...], 1, 1)
            + contract(d_key[past:], wk_ref[...], 1, 1)
            + contract(d_value[past:], wv_ref[...], 1, 1)
        )
        wq = wq_ref[...].astype(F32)
        wk = wk_ref[...].astype(F32)
        wv = wv_ref[...].astype(F32)
        own_along = of_query * wq + of_kv[:, :DH] * wk + of_kv[:, DH:] * wv
        own_shift = (
            jnp.sum(d_query.astype(F32), 0, keepdims=True) * wq
            + jnp.sum(d_key.astype(F32), 0, keepdims=True) * wk
            + jnp.sum(d_value.astype(F32), 0, keepdims=True) * wv
        )

        @pl.when(head == 0)
        def _():
            before = rest[:3] if with_sums else None
            rows_ref[...] = own_rows + before[0][...] if with_sums else own_rows
            along_ref[...] = own_along + before[1][...] if with_sums else own_along
            shift_ref[...] = own_shift + before[2][...] if with_sums else own_shift

        @pl.when(head > 0)
        def _():
            rows_ref[...] += own_rows
            along_ref[...] += own_along
            shift_ref[...] += own_shift


def attend_back(
    start,
    count,
    heads,
    bits,
    prob,
    d_attn,
    content,
    position,
    keys,
    values,
    w_rel,
    w_query,
    w_key,
    w_value,
    normed_t,
    table,
    cos,
    sin,
    sums=(),
    into=(),
    first=(),
):
    seg, width = content.shape
    total = keys.shape[0]
    block = QUERY_BLOCK
    column = lambda h, q: (0, start + h)
    rows = lambda h, q: (q, start + h)
    fixed = lambda h, q: (0, 0)
    whole = pl.BlockSpec(memory_space=pl.ANY)
    operands = [bits, prob, d_attn, content, position, keys, values, w_rel]
    operands += [w_query, w_key, w_value, normed_t, table, cos, sin]
    aliases = {}
    sum_specs = [
        pl.BlockSpec((seg, width), fixed),
        pl.BlockSpec((width, DH), fixed),
        pl.BlockSpec((width, DH), fixed),
    ]
    for i in range(len(sums)):
        aliases[len(operands) + i] = 2 + i
    operands += [*sums]
    for i in range(len(into)):
        aliases[len(operands) + i] = i
    operands += [*into, *first]
    half = jax.ShapeDtypeStruct(into[0].shape if into else (4, width // 2, len(heads) * DH), BF16)
    half_spec = pl.BlockSpec((4, width // 2, DH), lambda h, q: (0, 0, start - heads.start + h))
    return pl.pallas_call(
        functools.partial(attend_back_kernel, bool(sums)),
        grid=(count, seg // block),
        in_specs=[
            pl.BlockSpec(memory_space=pltpu.SMEM),
            pl.BlockSpec((1, block, total), lambda h, q: (start + h, q, 0)),
            pl.BlockSpec((block, DH), rows),
            pl.BlockSpec((block, DH), rows),
            pl.BlockSpec((block, DH), rows),
            pl.BlockSpec((total, DH), column),
            pl.BlockSpec((total, DH), column),
            pl.BlockSpec((width, DH), column),
            pl.BlockSpec((width, DH), column),
            pl.BlockSpec((width, DH), column),
            pl.BlockSpec((width, DH), column),
            pl.BlockSpec((width, total), fixed),
            pl.BlockSpec((total, width), fixed),
            pl.BlockSpec((block, width // 2), rows_of_block),
            pl.BlockSpec((block, width // 2), rows_of_block),
        ]
        + sum_specs[: len(sums)]
        + [whole] * (len(into) + len(first)),
        out_specs=[half_spec, half_spec] + sum_specs + [pl.BlockSpec((2, DH), lambda h, q: (0, h))],
        out_shape=[
            half,
            half,
            jax.ShapeDtypeStruct((seg, width), F32),
            jax.ShapeDtypeStruct((width, DH), F32),
            jax.ShapeDtypeStruct((width, DH), F32),
            jax.ShapeDtypeStruct((2, count * DH), F32),
        ],
        scratch_shapes=[
            pltpu.VMEM((total, DH), F32),
            pltpu.VMEM((total, DH), F32),
            pltpu.VMEM((width, DH), F32),
            pltpu.VMEM((seg, DH), BF16),
        ],
        input_output_aliases=aliases,
        compiler_params=pltpu.CompilerParams(vmem_limit_bytes=VMEM_LIMIT),
        cost_estimate=SHORT,
        name="attend_back",
    )(*operands)


def rows_of_block(h, q):
    return (q, 0)


def in_vmem():
    return pl.BlockSpec(memory_space=pltpu.VMEM)


def norm_kernel(count, owners_ref, *refs):
    parts, (gain_ref, shift_ref), (normed_ref, rows_ref) = refs[:count], refs[count : count + 2], refs[-2:]
    block = rows_ref.shape[1]
    for i, part in enumerate(parts):
        owner = owners_ref[i]
        for kind in range(3):
            low = part[kind * block : (kind + 1) * block]
            values = low.astype(F32)
            center = values - jnp.mean(values, -1, keepdims=True)
            spread = jnp.mean(center * center, -1, keepdims=True)
            normed = center * lax.rsqrt(spread + 1e-05) * gain_ref[...] + shift_ref[...]
            normed_ref[kind, owner] = normed.astype(BF16)
            if kind == 2:
                rows_ref[owner] = low


def norm_context(parts, owners, gain, shift, after=()):
    rows, width = parts[0].shape
    block = rows // 3
    normed, inputs = pl.pallas_call(
        functools.partial(norm_kernel, len(parts)),
        in_specs=[pl.BlockSpec(memory_space=pltpu.SMEM)] + [in_vmem()] * (len(parts) + 2)
        + [pl.BlockSpec(memory_space=pl.ANY)] * len(after),
        out_specs=[in_vmem(), in_vmem()],
        out_shape=[
            jax.ShapeDtypeStruct((3, len(parts), block, width), BF16),
            jax.ShapeDtypeStruct((len(parts), block, width), BF16),
        ],
        compiler_params=pltpu.CompilerParams(vmem_limit_bytes=VMEM_LIMIT),
        cost_estimate=SHORT,
        name="norm_context",
    )(owners, *parts, gain.reshape(1, -1), shift.reshape(1, -1), *after)
    return normed.reshape(-1, width), inputs.reshape(-1, width)


def place_kernel(count, owners_ref, *refs):
    for i, part in enumerate(refs[:count]):
        refs[-1][owners_ref[i]] = part[...]


def place_rows(parts, owners, after=()):
    rows, width = parts[0].shape
    return pl.pallas_call(
        functools.partial(place_kernel, len(parts)),
        in_specs=[pl.BlockSpec(memory_space=pltpu.SMEM)]
        + [in_vmem()] * len(parts)
        + [pl.BlockSpec(memory_space=pl.ANY)] * len(after),
        out_specs=in_vmem(),
        out_shape=jax.ShapeDtypeStruct((len(parts), rows, width), parts[0].dtype),
        cost_estimate=SHORT,
        name="place_rows",
    )(owners, *parts, *after)


def copy_kernel(rows_ref, *refs):
    refs[-1][...] = rows_ref[...]


def copy_after(rows, *others):
    return pl.pallas_call(
        copy_kernel,
        in_specs=[in_vmem()] + [pl.BlockSpec(memory_space=pl.ANY)] * len(others),
        out_specs=in_vmem(),
        out_shape=jax.ShapeDtypeStruct(rows.shape, rows.dtype),
        cost_estimate=SHORT,
        name="copy_after",
    )(rows, *others)


def flip_kernel(rows_ref, *refs):
    refs[-1][...] = rows_ref[...].T


def flip_after(rows, *others):
    count, width = rows.shape
    block = width // 2
    return pl.pallas_call(
        flip_kernel,
        grid=(count // block,),
        in_specs=[pl.BlockSpec((block, width), lambda i: (i, 0))]
        + [pl.BlockSpec(memory_space=pl.ANY)] * len(others),
        out_specs=pl.BlockSpec((width, block), lambda i: (0, i)),
        out_shape=jax.ShapeDtypeStruct((width, count), rows.dtype),
        cost_estimate=SHORT,
        name="flip_after",
    )(rows, *others)


def half_grad_kernel(bits_ref, left_ref, right_ref, out_ref):
    out_ref[...] = contract(left_ref[...], right_ref[...], 0, 0).astype(BF16)


def half_grad(bits, which, pre, left, right, give):
    rows, units = left.shape
    width = right.shape[1]
    cells = 1 << max(pre.bit_length(), 2)
    run = cells // (2 * pre)

    def column(i, bits):
        side = 1 - bits[which] if give else bits[which]
        return (0, (i // run * 2 + side) * run + i % run)

    return pl.pallas_call(
        half_grad_kernel,
        grid_spec=pltpu.PrefetchScalarGridSpec(
            num_scalar_prefetch=1,
            grid=(cells // 2,),
            in_specs=[
                pl.BlockSpec((rows, units // cells), column),
                pl.BlockSpec((rows, width), lambda i, bits: (0, 0)),
            ],
            out_specs=pl.BlockSpec((units // cells, width), lambda i, bits: (i, 0)),
        ),
        out_shape=jax.ShapeDtypeStruct((units // 2, width), BF16),
        compiler_params=pltpu.CompilerParams(vmem_limit_bytes=VMEM_LIMIT),
        cost_estimate=SHORT,
        name="half_grad",
    )(bits, left, right)[None]


def out_grad_kernel(bits_ref, left_ref, right_ref, keep_ref, give_ref):
    mine = bits_ref[0] == 1
    grad = contract(left_ref[...], right_ref[...], 0, 0)
    middle, columns = keep_ref.shape[1:]
    for i in range(2):
        part = grad[:, i * columns : (i + 1) * columns]
        low, high = part[:middle].astype(BF16), part[middle:].astype(BF16)
        keep_ref[i] = jnp.where(mine, high, low)
        give_ref[i] = jnp.where(mine, low, high)


def out_grad(bits, left, right):
    width = right.shape[1]
    half = jax.ShapeDtypeStruct((6, width // 2, width // 2), BF16)
    spec = pl.BlockSpec((2, width // 2, width // 2), lambda i: (2, 0, 0))
    whole = pl.BlockSpec(left.shape, lambda i: (0, 0))
    return pl.pallas_call(
        out_grad_kernel,
        grid=(1,),
        in_specs=[pl.BlockSpec(memory_space=pltpu.SMEM), whole, whole],
        out_specs=[spec, spec],
        out_shape=[half, half],
        compiler_params=pltpu.CompilerParams(vmem_limit_bytes=VMEM_LIMIT),
        cost_estimate=SHORT,
        name="out_grad",
    )(bits, left, right)


def finish_kernel(bits_ref, own_ref, got_ref, *refs):
    outs = refs[-5:]
    own = pl.program_id(0) == bits_ref[0]

    def write(ref):
        for i in range(4):
            outs[i][...] = ref[i].astype(F32)
        if ref.shape[0] > 4:
            half = ref.shape[2]
            outs[4][:, :half] = ref[4].astype(F32)
            outs[4][:, half:] = ref[5].astype(F32)

    pl.when(own)(lambda: write(own_ref))
    pl.when(jnp.logical_not(own))(lambda: write(got_ref))


def finish(bits, column, columns, own, got, results):
    count, rows, width = own.shape
    fixed = pl.BlockSpec(own.shape, lambda i: (0, 0, 0))
    block = pl.BlockSpec((rows, width), lambda i: (i, column))
    last = pl.BlockSpec((rows, columns * width), lambda i: (i, 0))
    out = jax.ShapeDtypeStruct((2 * rows, columns * width), F32)
    if count == 4:
        out_specs, before = [block] * 4, results[:4]
    else:
        out_specs, before = [block] * 4 + [last], results
    sums = pl.pallas_call(
        finish_kernel if count > 4 else lambda *refs: finish_kernel(*refs, None),
        grid=(2,),
        in_specs=[pl.BlockSpec(memory_space=pltpu.SMEM), fixed, fixed]
        + [pl.BlockSpec(memory_space=pl.ANY)] * len(before),
        out_specs=out_specs,
        out_shape=[out] * len(out_specs),
        input_output_aliases={3 + i: i for i in range(len(before))},
        compiler_params=pltpu.CompilerParams(vmem_limit_bytes=VMEM_LIMIT),
        cost_estimate=SHORT,
        name="finish",
    )(bits, own, got, *before)
    return list(sums) + list(results[len(sums) :])


class Chain:
    def __init__(self, moves, keeps, gives):
        self.moves, self.keeps, self.gives = list(moves), keeps, gives
        self.join = False


def parts_of(move):
    return len(move[1])


def split_rows(rows, pre):
    lead, count, columns = rows.shape
    return rows.reshape(lead, pre, 2, count // (2 * pre), columns)


def first_halves(rows, move):
    keeps, gives = [], []
    size = rows.shape[0] // parts_of(move)
    for i, (step, pre) in enumerate(move[1]):
        cells = split_rows(rows[i * size : (i + 1) * size], pre)
        bit = bit_of(*step)
        flat = (size, -1, rows.shape[2])
        keeps.append(pick(cells, bit, 2).reshape(flat))
        gives.append(pick(cells, 1 - bit, 2).reshape(flat))
    return keeps, gives


def round_of(chains, bits, bit_names, after=()):
    operands, plans, out_shape = [], [], []
    for chain in chains:
        kind, cuts = chain.moves.pop(0)
        nexts = chain.moves[0] if chain.moves else None
        got = [swap(give, *step) for give, (step, _) in zip(chain.gives, cuts)]
        held = chain.keeps if kind == "halve" else chain.gives
        leads, columns = [h.shape[0] for h in held], held[0].shape[2]
        total = sum(leads)
        next_kind, next_cuts = nexts if nexts else ("end", [None])
        size = total // len(next_cuts)
        ins, views = [], []
        for i, (h, g) in enumerate(zip(held, got)):
            base = sum(leads[:i])
            if kind == "double":
                cells = max(pre for _, pre in cuts)
                view = (h.shape[0], cells, h.shape[1] // cells, columns)
                bit = (bit_names.index(cuts[i][0]), cuts[i][1])
            elif next_kind == "halve":
                cells = max(2 * pre for _, pre in next_cuts)
                view = (h.shape[0], cells, h.shape[1] // cells, columns)
                bit = None
            else:
                view = h.shape
                bit = None
            ins.append((len(operands), base, bit, view))
            operands += [h.reshape(view), g.reshape(view)]
        rows = held[0].shape[1]
        outs = []
        for j, cut in enumerate(next_cuts):
            if next_kind == "halve":
                cells = ins[0][3][1]
                shape = (size, cells // 2, rows // cells, columns)
                outs.append((len(out_shape), bit_names.index(cut[0]), cut[1]))
                out_shape += [jax.ShapeDtypeStruct(shape, BF16)] * 2
            else:
                if kind == "double":
                    cells = ins[0][3][1]
                    shape = (size, cells * 2, rows // cells, columns)
                    if chain.join and next_kind == "end":
                        shape = (1, cells * 2, rows // cells, size * columns)
                else:
                    shape = (size, rows, columns)
                outs.append((len(out_shape), None, None))
                out_shape += [jax.ShapeDtypeStruct(shape, held[0].dtype)]
        plans.append((kind, next_kind, size, ins, outs))

    def kernel(bits_ref, *refs):
        inputs, results = refs[: len(operands)], refs[-len(out_shape) :]
        for kind, next_kind, size, ins, outs in plans:
            for at, base, bit, view in ins:
                held_ref, got_ref = inputs[at], inputs[at + 1]
                for i in range(view[0]):
                    where, which = divmod(base + i, size)
                    out, out_bit, out_pre = outs[where]
                    if kind == "double":
                        mine = bits_ref[bit[0]]
                        run = view[1] // bit[1]
                        for cell in range(view[1]):
                            for side, ref in ((mine, held_ref), (1 - mine, got_ref)):
                                place = (cell // run * 2 + side) * run + cell % run
                                if results[out].shape[3] == ref.shape[3]:
                                    results[out][which, place] = ref[i, cell]
                                else:
                                    wide = slice(which * ref.shape[3], (which + 1) * ref.shape[3])
                                    results[out][0, place, :, wide] = ref[i, cell]
                    elif next_kind == "halve":
                        mine = bits_ref[out_bit]
                        run = view[1] // (2 * out_pre)
                        for cell in range(view[1] // 2):
                            for side, slot in ((mine, out), (1 - mine, out + 1)):
                                place = (cell // run * 2 + side) * run + cell % run
                                results[slot][which, cell] = (
                                    held_ref[i, place].astype(F32) + got_ref[i, place].astype(F32)
                                ).astype(BF16)
                    else:
                        results[out][which] = (held_ref[i].astype(F32) + got_ref[i].astype(F32)).astype(
                            results[out].dtype
                        )

    in_vmem = pl.BlockSpec(memory_space=pltpu.VMEM)
    results = pl.pallas_call(
        kernel,
        in_specs=[pl.BlockSpec(memory_space=pltpu.SMEM)]
        + [in_vmem] * len(operands)
        + [pl.BlockSpec(memory_space=pl.ANY)] * len(after),
        out_specs=[in_vmem] * len(out_shape),
        out_shape=out_shape,
        compiler_params=pltpu.CompilerParams(vmem_limit_bytes=VMEM_LIMIT),
        cost_estimate=SHORT,
        name="add_and_split",
    )(bits, *operands, *after)
    for chain, (kind, next_kind, size, ins, outs) in zip(chains, plans):
        flat = lambda r: r.reshape(r.shape[0], -1, r.shape[-1])
        if next_kind == "halve":
            chain.keeps = [flat(results[o]) for o, _, _ in outs]
            chain.gives = [flat(results[o + 1]) for o, _, _ in outs]
        else:
            chain.keeps = []
            chain.gives = [flat(results[o]) for o, _, _ in outs]


def gather_wide(rows, wide, order):
    have = []
    for i in order:
        rows = double(rows, wide[i], sum(j < i for j in have))
        have.append(i)
    return rows


def own_streams_plan(
    inputs,
    memory,
    compressed,
    seg_len,
    gain_first,
    shift_first,
    w_query,
    w_key,
    w_value,
    w_rel,
    bias_content,
    bias_position,
    w_out,
    gain_second,
    shift_second,
    w_up,
    bias_up,
    w_down,
    bias_down,
    w_comp,
    comp_bias,
    grad_out,
    grad_comp,
):
    seq_parts = lax.axis_size("seq")
    dp_parts = lax.axis_size("dp")
    me = lax.axis_index("seq")
    seg_dev, streams, width = inputs.shape
    seg = seg_dev * seq_parts
    split = CMEM + MEM
    hidden_dev = w_down.shape[0]

    core = ("dp", 1)
    wide = [("dp", d) for d in bits_below(dp_parts)[1:]]
    line = [("seq", d) for d in bits_below(seq_parts)]
    there = list(range(len(wide)))
    back = there[::-1]
    core_bit = bit_of(*core)

    bit_names = [core] + wide + line
    bits = jnp.stack([bit_of(*name) for name in bit_names]).astype(jnp.int32)
    wide_in = [[(wide[i], 1), (wide[j], 1 << j)] for i, j in zip(there, back)]
    core_cut, line_cuts, wide_cuts = [(core, 1)], [[(s, 1)] for s in line], [[(s, 1)] for s in wide]

    def moves_of(cuts, collected):
        return [("halve", c) for c in cuts] + [("double", c) for c in reversed(collected)]

    piece = hidden_dev // 2 >> len(wide)
    place = core_bit
    for step in wide:
        place = place * 2 + bit_of(*step)

    def gathered(rows):
        rows = jnp.swapaxes(rows.reshape(piece, 2, width // 2), 0, 1)
        chain = Chain(moves_of([], wide_in + line_cuts), [], [rows])
        chain.join = True
        return chain

    up_piece = lax.dynamic_slice_in_dim(w_up, place * piece, piece, 1).T
    up_chain = gathered(up_piece)
    round_of([up_chain], bits, bit_names)
    order = token(up_chain.gives[0])
    for step in line[:-1]:
        round_of([up_chain], bits, bit_names)
    order_two = token(up_chain.gives[0])

    key_cos, key_sin = sinusoids(jnp.arange(split + seg, dtype=jnp.int32))
    table = jnp.concatenate([key_cos, key_sin], -1).astype(BF16)
    cos, sin = key_cos[split:], key_sin[split:]

    owners = jnp.stack([(me - shift) % seq_parts for shift in range(seq_parts)]).astype(jnp.int32)

    def send(parts):
        return [parts[0]] + [
            lax.ppermute(part, "seq", [(i, (i + shift) % seq_parts) for i in range(seq_parts)])
            for shift, part in enumerate(parts)
            if shift
        ]

    def parts_for(rows, order=0):
        return [pick(rows, (me + shift) % seq_parts + order, 0) for shift in range(seq_parts)]

    def from_streams(parts):
        return by_stream(place_rows(send(parts), owners))

    blocks = [by_stream(rows) for rows in (compressed, memory, inputs)]
    parts = send(parts_for(jnp.concatenate(blocks, 1), order))
    down_piece = lax.dynamic_slice_in_dim(w_down, place * piece + order_two, piece, 0)
    down_chain = gathered(down_piece)
    round_of([up_chain], bits, bit_names)
    normed, x_rows = norm_context(
        parts, owners, gain_first, shift_first, [*up_chain.gives, *down_chain.gives, table, cos, sin]
    )
    length = lax.dynamic_slice_in_dim(seg_len, me, 1)
    order = token(normed)
    go_parts = parts_for(by_stream(grad_out), order)
    bias_all = lax.dynamic_slice_in_dim(bias_up.reshape(2, -1), core_bit + order, 1, 0)

    seg_normed = normed[split:]
    queries = jnp.dot(seg_normed, w_query, preferred_element_type=F32)
    keys = jnp.dot(normed, w_key, preferred_element_type=F32).astype(BF16)
    values = jnp.dot(normed, w_value, preferred_element_type=F32).astype(BF16)
    content = (queries + bias_content).astype(BF16)
    position = (queries + bias_position).astype(BF16)
    given = (length, content, position, keys, values, w_rel, table, cos, sin)
    round_of([down_chain], bits, bit_names, [normed])
    round_of([down_chain], bits, bit_names, [values])
    go_rows = send(go_parts)
    prob, attn_out = attend(range(H // 2), *given, first=down_chain.gives + go_parts[1:])
    go_rows = place_rows(go_rows, owners, [attn_out]).reshape(seg, width)
    round_of([down_chain], bits, bit_names, [attn_out])
    while up_chain.moves:
        round_of([up_chain], bits, bit_names, [attn_out])
    up_half = up_chain.gives[0][0]
    bias_all = double(bias_all, line[-1], 0)
    prob, attn_out = attend(
        range(H // 2, H),
        *given,
        first=down_chain.gives + [go_rows, bias_all, up_half],
        into=[prob, attn_out],
    )
    while down_chain.moves:
        round_of([down_chain], bits, bit_names, [attn_out])
    down_half = down_chain.gives[0][0]
    for step in line[-2::-1]:
        bias_all = double(bias_all, step, 0)
    bias_half = jnp.swapaxes(bias_all.reshape(seq_parts, -1, piece), 0, 1).reshape(-1).astype(F32)
    memory_rows = copy_after(by_stream(memory), attn_out)
    memory_all = lax.all_gather(memory_rows, "seq", axis=1, tiled=True)
    x_f = x_rows.astype(F32)
    hidden = x_f + jnp.dot(attn_out, w_out, preferred_element_type=F32)
    normed_two = layer_norm(hidden, gain_second, shift_second).astype(BF16)

    pair_normed = double(normed_two, core).reshape(-1, width)
    pair_grad = double(go_rows, core).reshape(-1, width)
    pre_act = contract(pair_normed, up_half, 1, 1) + bias_half
    activated = gelu_tanh(pre_act).astype(BF16)
    ffn_rows = jnp.dot(activated, down_half, preferred_element_type=F32)
    ffn_rows = halve(ffn_rows.reshape(2, seg, width), core)
    output = (hidden + ffn_rows + bias_down).astype(BF16)
    output_parts = parts_for(output.reshape(seq_parts, seg_dev, width))
    down_grad = functools.partial(half_grad, bits, 1, 1, activated, pair_grad)
    down_give = down_grad(True)
    d_activated = contract(pair_grad, down_half, 1, 1)
    _, gelu_back = jax.vjp(gelu_tanh, pre_act)
    d_pre = gelu_back(d_activated)[0].astype(BF16)
    up_grad = functools.partial(half_grad, bits, len(wide), 1 << (len(wide) - 1), d_pre, pair_normed)
    up_give = up_grad(True)
    d_normed_two = jnp.dot(d_pre, up_half, preferred_element_type=F32)
    d_normed_two = halve(d_normed_two.reshape(2, seg, width), core)
    grad_bias_half = jnp.sum(d_pre.astype(F32), 0)
    ffn = Chain(
        moves_of(wide_in + line_cuts, [core_cut] + wide_in),
        [down_grad(False), up_grad(False)],
        [down_give, up_give],
    )

    go_f = go_rows.astype(F32)
    _, norm_two_back = jax.vjp(layer_norm, hidden, gain_second, shift_second)
    d_hidden_ffn, grad_gain_second, grad_shift_second = norm_two_back(d_normed_two)
    d_hidden = go_f + d_hidden_ffn
    grad_bias_down = jnp.sum(go_f, 0)
    d_branch = d_hidden.astype(BF16)
    d_attn = contract(d_branch, w_out, 1, 1).astype(BF16)

    new_rows = memory_all.shape[1] // RATE
    windows = memory_all[:, : new_rows * RATE].reshape(streams, new_rows, RATE, width)
    new_compressed = (
        jnp.einsum("srtd,tde->rse", windows, w_comp, preferred_element_type=F32) + comp_bias
    ).astype(BF16)
    grad_w_comp = jnp.einsum("srtd,rse->tde", windows, grad_comp, preferred_element_type=F32)
    grad_comp_bias = jnp.sum(grad_comp.astype(F32), (0, 1))
    comp_moves = moves_of([core_cut] + wide_cuts, [core_cut] + wide_cuts)
    comp_shape = grad_w_comp.shape
    comp = Chain(
        comp_moves, *first_halves(grad_w_comp.astype(BF16).reshape(1, -1, comp_shape[2]), comp_moves[0])
    )

    normed_t = flip_after(normed, normed_two)
    half_heads = H // 2
    group_moves = moves_of([core_cut] + wide_in + line_cuts, [core_cut] + wide_in + line_cuts)
    groups, biases, head_sums = [], [], []
    output_rows = send(output_parts)
    first = ffn.gives + output_parts[1:] + [memory_rows]
    beside = [[], [], [ffn, comp], [ffn, comp]]
    for start in range(0, H, HEADS_A_CALL):
        base = start // half_heads * half_heads
        group_heads = range(base, base + half_heads)
        if start == 0:
            halves = out_grad(bits, attn_out, d_branch)
        elif start == base:
            halves = []
        *halves, d_rows, along, shift_part, bias_part = attend_back(
            start, HEADS_A_CALL, group_heads, bits, prob, d_attn, content, position, keys, values,
            w_rel, w_query, w_key, w_value, normed_t, table, cos, sin, head_sums, halves, first,
        )
        head_sums = [d_rows, along, shift_part]
        biases.append(bias_part)
        active = beside[start // HEADS_A_CALL] + groups
        if active:
            round_of(active, bits, bit_names, [bias_part])
        first = [g for c in active for g in c.gives]
        if start == 0:
            output_rows = place_rows(output_rows, owners, [bias_part])
            first += [output_rows]
        if start + HEADS_A_CALL == group_heads.stop:
            groups.append(Chain(group_moves, [halves[0]], [halves[1]]))
            first += groups[-1].gives
            if start + HEADS_A_CALL == half_heads:
                first += comp.gives + ffn.keeps
    output = by_stream(output_rows)
    d_normed = d_rows
    _, norm_one_back = jax.vjp(lambda v: layer_norm(v, gain_first, shift_first), x_f)
    (d_context,) = norm_one_back(d_normed)
    grad_inputs = (d_hidden + d_context).astype(BF16).reshape(seq_parts, seg_dev, width)
    input_parts = parts_for(grad_inputs)
    input_rows = send(input_parts)

    grad_shift_first = jnp.sum(shift_part, 1)
    grad_gain_first = (jnp.sum(along, 1) - shift_first * grad_shift_first) / gain_first
    vectors = jnp.concatenate(
        [
            jnp.concatenate(biases, 1).reshape(-1),
            grad_gain_first,
            grad_shift_first,
            grad_gain_second,
            grad_shift_second,
            grad_bias_down,
        ]
    )
    count = vectors.shape[0]
    hidden_sums = jnp.zeros((2, grad_bias_half.shape[0]), F32)
    hidden_sums = lax.dynamic_update_slice(hidden_sums, grad_bias_half[None], (core_bit, 0))
    comp_sums = jnp.zeros((seq_parts, grad_comp_bias.shape[0]), F32)
    comp_sums = lax.dynamic_update_slice(comp_sums, grad_comp_bias[None], (me, 0))
    vectors = jnp.concatenate([vectors, hidden_sums.reshape(-1), comp_sums.reshape(-1)])
    vector = Chain([("add", [(name, 1)]) for name in bit_names], [], [vectors.reshape(1, -1, DH)])

    one, two = groups
    rounds = [
        [ffn, one, two, vector],
        [ffn, one, two, vector],
        [ffn, one, two],
        [ffn, one, two, vector, comp],
        [ffn, one, two, vector, comp],
        [one, two, vector, comp],
        [one, two, comp],
    ]
    turn = 0
    while len(two.moves) > 1 or vector.moves or comp.moves or ffn.moves:
        active = rounds[turn] if turn < len(rounds) else [ffn, one, two, vector, comp]
        active = [c for c in active if len(c.moves) > (c in groups)]
        if turn == 5:
            fence = input_parts
        elif turn == 8:
            input_rows = place_rows(input_rows, owners)
            fence = [input_rows]
        else:
            fence = []
        round_of(active, bits, bit_names, fence)
        turn += 1
    grad_inputs = by_stream(input_rows)
    vectors = vector.gives[0].reshape(-1)

    grad_w_down = ffn.gives[0][0].astype(F32)
    grad_w_up = ffn.gives[0][1].astype(F32).T
    grad_w_comp = comp.gives[0].astype(F32).reshape(comp_shape)
    results = []
    for column, group in enumerate(groups):
        own = group.gives[0]
        results = finish(bits, column, len(groups), own, swap(own, *core), results)
    grad_w_query, grad_w_rel, grad_w_key, grad_w_value, grad_w_out = results

    totals = vectors[:count].reshape(-1, width)
    hidden_sums = vectors[count : count + hidden_sums.size].reshape(
        [2, 1 << len(wide)] + [2] * len(line) + [piece]
    )
    for step in line:
        hidden_sums = pick(hidden_sums, bit_of(*step), 2)
    grad_bias_up = hidden_sums.reshape(-1)
    comp_sums = vectors[count + grad_bias_half.size * 2 :].reshape(comp_sums.shape)
    grad_comp_bias = pick(comp_sums, me, 0)

    return (
        output,
        grad_inputs,
        new_compressed,
        totals[2],
        totals[3],
        grad_w_query,
        grad_w_key,
        grad_w_value,
        grad_w_rel,
        totals[0],
        totals[1],
        grad_w_out,
        totals[4],
        totals[5],
        grad_w_up,
        grad_bias_up,
        grad_w_down,
        totals[6],
        grad_w_comp,
        grad_comp_bias,
    )


def on_device(*arrays):
    streams = arrays[0].shape[1]
    dp_parts, seq_parts = lax.axis_size("dp"), lax.axis_size("seq")
    fits = streams == seq_parts and seq_parts > 1 and dp_parts >= 4
    powers = (seq_parts & (seq_parts - 1)) == 0 and (dp_parts & (dp_parts - 1)) == 0
    plan = own_streams_plan if fits and powers else split_rows_plan
    return plan(*arrays)


def solution(mesh):
    in_specs = (
        P("seq", "dp", None),
        P("seq", "dp", None),
        P("seq", "dp", None),
        P("dp"),
        P(),
        P(),
        P(),
        P(),
        P(),
        P(),
        P(),
        P(),
        P(),
        P(),
        P(),
        P(None, "seq"),
        P("seq"),
        P("seq", None),
        P(),
        P(None, None, "seq"),
        P("seq"),
        P("seq", "dp", None),
        P(None, "dp", "seq"),
    )
    out_specs = (
        P("seq", "dp", None),
        P("seq", "dp", None),
        P(None, "dp", "seq"),
        P(),
        P(),
        P(),
        P(),
        P(),
        P(),
        P(),
        P(),
        P(),
        P(),
        P(),
        P(None, "seq"),
        P("seq"),
        P("seq", None),
        P(),
        P(None, None, "seq"),
        P("seq"),
    )
    return jax.shard_map(
        on_device, mesh=mesh, in_specs=in_specs, out_specs=out_specs, check_vma=False
    )
```

```python
import functools
import math

import jax
import jax.numpy as jnp
from jax import lax
from jax.experimental import pallas as pl
from jax.experimental.pallas import tpu as pltpu
from jax.sharding import PartitionSpec as P

D = 1024
H = 8
DH = 128
MEM = 512
CMEM = 512
RATE = 3


def layer_norm(values, gain, shift):
    center = values - jnp.mean(values, -1, keepdims=True)
    spread = jnp.mean(center * center, -1, keepdims=True)
    return center * lax.rsqrt(spread + 1e-05) * gain + shift


def gelu_tanh(values):
    return jax.nn.gelu(values, approximate=True)


def sinusoids(positions):
    half_width = D // 2
    frequency = jnp.exp(jnp.arange(half_width, dtype=jnp.float32) * (-2.0 * math.log(10000.0) / D))
    angles = positions.astype(jnp.float32)[:, None] * frequency[None, :]
    return (jnp.cos(angles), jnp.sin(angles))


def key_positions(seq_parts, cmem_dev, mem_dev, seg_dev):
    ctx_dev = cmem_dev + mem_dev + seg_dev
    row_ids = jnp.arange(ctx_dev * seq_parts, dtype=jnp.int32)
    device_ids = row_ids // ctx_dev
    local_ids = row_ids % ctx_dev
    in_cmem = device_ids * cmem_dev + local_ids
    in_mem = CMEM + device_ids * mem_dev + (local_ids - cmem_dev)
    in_seg = CMEM + MEM + device_ids * seg_dev + (local_ids - cmem_dev - mem_dev)
    return jnp.where(
        local_ids < cmem_dev, in_cmem, jnp.where(local_ids < cmem_dev + mem_dev, in_mem, in_seg)
    )


def rotate_rows(position_rows, rel_heads, row_sin, row_cos, half_width):
    mixed = jnp.einsum(
        "qshd,fhd->qshf", position_rows, rel_heads, preferred_element_type=jnp.float32
    )
    first_half = mixed[..., :half_width]
    second_half = mixed[..., half_width:]
    return jnp.concatenate(
        [
            first_half * row_sin + second_half * row_cos,
            second_half * row_sin - first_half * row_cos,
        ],
        -1,
    ).astype(jnp.bfloat16)


def split_rows_plan(
    inputs,
    memory,
    compressed,
    seg_len,
    gain_first,
    shift_first,
    w_query,
    w_key,
    w_value,
    w_rel,
    bias_content,
    bias_position,
    w_out,
    gain_second,
    shift_second,
    w_up,
    bias_up,
    w_down,
    bias_down,
    w_comp,
    comp_bias,
    grad_out,
    grad_comp,
):
    seq_parts = lax.axis_size("seq")
    my_index = lax.axis_index("seq")
    seg_dev, streams, model_width = inputs.shape
    mem_dev = memory.shape[0]
    cmem_dev = compressed.shape[0]
    split_at = cmem_dev + mem_dev
    ctx_dev = split_at + seg_dev
    total_keys = ctx_dev * seq_parts
    half_width = model_width // 2
    score_scale = 1.0 / math.sqrt(DH)
    key_pos = key_positions(seq_parts, cmem_dev, mem_dev, seg_dev)
    key_cos, key_sin = sinusoids(key_pos)
    pos_table = jnp.concatenate([key_cos, key_sin], -1).astype(jnp.bfloat16)
    query_rows = my_index * seg_dev + jnp.arange(seg_dev, dtype=jnp.int32)
    query_cos, query_sin = sinusoids(CMEM + MEM + query_rows)
    query_cos = query_cos[:, None, None, :]
    query_sin = query_sin[:, None, None, :]
    key_seg = key_pos - (CMEM + MEM)
    visible = (key_seg[None, None, :] < 0) | (
        key_seg[None, None, :] <= query_rows[None, :, None]
    ) & (key_seg[None, None, :] < seg_len[:, None, None])
    x_in = inputs.astype(jnp.float32)
    context = jnp.concatenate([compressed, memory, inputs], 0).astype(jnp.float32)
    normed = layer_norm(context, gain_first, shift_first)
    normed_low = normed.astype(jnp.bfloat16)
    seg_normed = normed_low[split_at:]
    queries = jnp.dot(seg_normed, w_query, preferred_element_type=jnp.float32)
    keys_low = jnp.dot(normed_low, w_key, preferred_element_type=jnp.float32).astype(jnp.bfloat16)
    values_low = jnp.dot(normed_low, w_value, preferred_element_type=jnp.float32).astype(
        jnp.bfloat16
    )
    query_content = (queries + bias_content).astype(jnp.bfloat16).reshape(seg_dev, streams, H, DH)
    query_position = (queries + bias_position).astype(jnp.bfloat16).reshape(seg_dev, streams, H, DH)
    rel_heads = w_rel.reshape(model_width, H, DH)
    rotated = rotate_rows(query_position, rel_heads, query_sin, query_cos, half_width)
    keys_all, values_all, memory_all = (
        lax.all_gather(keys_low, "seq", axis=0, tiled=True),
        lax.all_gather(values_low, "seq", axis=0, tiled=True),
        lax.all_gather(memory, "seq", axis=0, tiled=True),
    )

    def scores_of(keys_gathered):
        content = jnp.einsum(
            "qshd,kshd->shqk",
            query_content,
            keys_gathered.reshape(total_keys, streams, H, DH),
            preferred_element_type=jnp.float32,
        )
        placed = jnp.einsum("qshf,kf->shqk", rotated, pos_table, preferred_element_type=jnp.float32)
        return jnp.where(visible[:, None], (content + placed) * score_scale, -1e30)

    scores = scores_of(keys_all)
    row_max = jnp.max(scores, -1, keepdims=True)
    exp_scores = jnp.exp(scores - row_max)
    row_total = jnp.sum(exp_scores, -1, keepdims=True)
    attn_prob = (exp_scores / row_total).astype(jnp.bfloat16)
    log_total = row_max + jnp.log(row_total)
    attended = jnp.einsum(
        "shqk,kshd->qshd",
        attn_prob,
        values_all.reshape(total_keys, streams, H, DH),
        preferred_element_type=jnp.float32,
    )
    attn_out = attended.reshape(seg_dev, streams, model_width).astype(jnp.bfloat16)
    hidden = x_in + jnp.dot(attn_out, w_out, preferred_element_type=jnp.float32)
    normed_two = layer_norm(hidden, gain_second, shift_second).astype(jnp.bfloat16)
    normed_all = lax.all_gather(normed_two, "seq", axis=0, tiled=True)
    pre_act = jnp.dot(normed_all, w_up, preferred_element_type=jnp.float32) + bias_up.astype(
        jnp.float32
    )
    activated = gelu_tanh(pre_act).astype(jnp.bfloat16)
    row_piece = activated
    ffn_result = lax.psum_scatter(
        jnp.dot(row_piece, w_down, preferred_element_type=jnp.float32).astype(jnp.bfloat16),
        "seq",
        scatter_dimension=0,
        tiled=True,
    ).astype(jnp.float32)
    output = (hidden + ffn_result + bias_down).astype(jnp.bfloat16)
    grad_all = lax.all_gather(grad_out, "seq", axis=0, tiled=True)
    d_activated = jnp.einsum("rsd,fd->rsf", grad_all, w_down, preferred_element_type=jnp.float32)
    _, gelu_back = jax.vjp(gelu_tanh, pre_act)
    d_pre = gelu_back(d_activated)[0].astype(jnp.bfloat16)
    grad_w_down = jnp.einsum("rsf,rsd->fd", activated, grad_all, preferred_element_type=jnp.float32)
    grad_w_up = jnp.einsum("rsd,rsf->df", normed_all, d_pre, preferred_element_type=jnp.float32)
    grad_bias_up = jnp.sum(d_pre.astype(jnp.float32), (0, 1))
    row_piece = d_pre
    d_normed_two = lax.psum_scatter(
        jnp.einsum("rsf,df->rsd", row_piece, w_up, preferred_element_type=jnp.float32).astype(
            jnp.bfloat16
        ),
        "seq",
        scatter_dimension=0,
        tiled=True,
    ).astype(jnp.float32)
    _, norm_two_back = jax.vjp(layer_norm, hidden, gain_second, shift_second)
    d_hidden_ffn, grad_gain_second, grad_shift_second = norm_two_back(d_normed_two)
    grad_rows_f = grad_out.astype(jnp.float32)
    d_hidden = grad_rows_f + d_hidden_ffn
    grad_bias_down = jnp.sum(grad_rows_f, (0, 1))
    d_branch = d_hidden.astype(jnp.bfloat16)
    grad_w_out = jnp.einsum("rsd,rse->de", attn_out, d_branch, preferred_element_type=jnp.float32)
    d_attn = (
        jnp.einsum("rse,de->rsd", d_branch, w_out, preferred_element_type=jnp.float32)
        .astype(jnp.bfloat16)
        .reshape(seg_dev, streams, H, DH)
    )
    keys_back, values_back = (
        lax.all_gather(keys_low, "seq", axis=0, tiled=True),
        lax.all_gather(values_low, "seq", axis=0, tiled=True),
    )
    keys_heads = keys_back.reshape(total_keys, streams, H, DH)
    values_heads = values_back.reshape(total_keys, streams, H, DH)
    prob_full = jnp.exp(scores_of(keys_back) - log_total)
    prob_low = prob_full.astype(jnp.bfloat16)
    d_prob = jnp.einsum("qshd,kshd->shqk", d_attn, values_heads, preferred_element_type=jnp.float32)
    inner_sum = jnp.sum(d_prob * prob_full, -1, keepdims=True)
    d_scores = (prob_full * (d_prob - inner_sum)).astype(jnp.bfloat16)
    key_part = (
        jnp.einsum("shqk,qshd->kshd", d_scores, query_content, preferred_element_type=jnp.float32)
        * score_scale
    )
    value_part = jnp.einsum("shqk,qshd->kshd", prob_low, d_attn, preferred_element_type=jnp.float32)
    key_sums = lax.psum_scatter(
        jnp.concatenate(
            [
                key_part.reshape(ctx_dev * lax.axis_size("seq"), streams, model_width),
                value_part.reshape(ctx_dev * lax.axis_size("seq"), streams, model_width),
            ],
            -1,
        ).astype(jnp.bfloat16),
        "seq",
        scatter_dimension=0,
        tiled=True,
    ).astype(jnp.float32)
    d_keys = key_sums[..., :model_width].astype(jnp.bfloat16)
    d_values = key_sums[..., model_width:].astype(jnp.bfloat16)
    d_content = (
        jnp.einsum("shqk,kshd->qshd", d_scores, keys_heads, preferred_element_type=jnp.float32)
        * score_scale
    )
    d_rotated = (
        jnp.einsum("shqk,kf->qshf", d_scores, pos_table, preferred_element_type=jnp.float32)
        * score_scale
    )
    lead_part = d_rotated[..., :half_width]
    tail_part = d_rotated[..., half_width:]
    d_mixed = jnp.concatenate(
        [
            lead_part * query_sin - tail_part * query_cos,
            lead_part * query_cos + tail_part * query_sin,
        ],
        -1,
    ).astype(jnp.bfloat16)
    d_query_pos = jnp.einsum(
        "qshf,fhd->qshd", d_mixed, rel_heads, preferred_element_type=jnp.float32
    )
    grad_w_rel = jnp.einsum(
        "qshf,qshd->fhd", d_mixed, query_position, preferred_element_type=jnp.float32
    ).reshape(model_width, model_width)
    grad_bias_content = jnp.sum(d_content, (0, 1)).reshape(model_width)
    grad_bias_position = jnp.sum(d_query_pos, (0, 1)).reshape(model_width)
    d_queries = (
        (d_content + d_query_pos).reshape(seg_dev, streams, model_width).astype(jnp.bfloat16)
    )
    grad_w_query = jnp.einsum(
        "rsd,rse->de", seg_normed, d_queries, preferred_element_type=jnp.float32
    )
    grad_w_key = jnp.einsum("rsd,rse->de", normed_low, d_keys, preferred_element_type=jnp.float32)
    grad_w_value = jnp.einsum(
        "rsd,rse->de", normed_low, d_values, preferred_element_type=jnp.float32
    )
    d_from_kv = jnp.einsum(
        "rse,de->rsd", d_keys, w_key, preferred_element_type=jnp.float32
    ) + jnp.einsum("rse,de->rsd", d_values, w_value, preferred_element_type=jnp.float32)
    d_from_query = jnp.einsum("rse,de->rsd", d_queries, w_query, preferred_element_type=jnp.float32)
    d_normed = jnp.concatenate([d_from_kv[:split_at], d_from_kv[split_at:] + d_from_query], 0)
    _, norm_one_back = jax.vjp(layer_norm, context, gain_first, shift_first)
    d_context, grad_gain_first, grad_shift_first = norm_one_back(d_normed)
    grad_inputs = (d_hidden + d_context[split_at:]).astype(jnp.bfloat16)
    new_rows = memory_all.shape[0] // RATE
    windows = memory_all[: new_rows * RATE].reshape(new_rows, RATE, streams, model_width)
    new_compressed = (
        jnp.einsum("rtsd,tde->rse", windows, w_comp, preferred_element_type=jnp.float32) + comp_bias
    ).astype(jnp.bfloat16)
    grad_w_comp = jnp.einsum(
        "rtsd,rse->tde", windows, grad_comp, preferred_element_type=jnp.float32
    )
    grad_comp_bias = jnp.sum(grad_comp.astype(jnp.float32), (0, 1))
    (
        grad_w_query,
        grad_w_key,
        grad_w_value,
        grad_w_rel,
        grad_w_out,
        grad_bias_content,
        grad_bias_position,
        grad_gain_first,
        grad_shift_first,
        grad_gain_second,
        grad_shift_second,
        grad_bias_down,
    ) = lax.psum(
        (
            grad_w_query,
            grad_w_key,
            grad_w_value,
            grad_w_rel,
            grad_w_out,
            grad_bias_content,
            grad_bias_position,
            grad_gain_first,
            grad_shift_first,
            grad_gain_second,
            grad_shift_second,
            grad_bias_down,
        ),
        ("dp", "seq"),
    )
    grad_w_up, grad_bias_up, grad_w_down, grad_w_comp, grad_comp_bias = (
        lax.psum(grad_w_up.astype(jnp.bfloat16), "dp").astype(jnp.float32),
        lax.psum(grad_bias_up.astype(jnp.bfloat16), "dp").astype(jnp.float32),
        lax.psum(grad_w_down.astype(jnp.bfloat16), "dp").astype(jnp.float32),
        lax.psum(grad_w_comp.astype(jnp.bfloat16), "dp").astype(jnp.float32),
        lax.psum(grad_comp_bias.astype(jnp.bfloat16), "dp").astype(jnp.float32),
    )
    return (
        output,
        grad_inputs,
        new_compressed,
        grad_gain_first,
        grad_shift_first,
        grad_w_query,
        grad_w_key,
        grad_w_value,
        grad_w_rel,
        grad_bias_content,
        grad_bias_position,
        grad_w_out,
        grad_gain_second,
        grad_shift_second,
        grad_w_up,
        grad_bias_up,
        grad_w_down,
        grad_bias_down,
        grad_w_comp,
        grad_comp_bias,
    )


BF16 = jnp.bfloat16
F32 = jnp.float32
ATTEND_PARTS = 2
BACK_PARTS = 1
CALLS = (2, 2, 2, 2)
MIB = 1024 * 1024
SHORT = pl.CostEstimate(flops=1024, bytes_accessed=1024, transcendentals=0)


def contract(left, right, left_dim, right_dim):
    return lax.dot_general(
        left, right, (((left_dim,), (right_dim,)), ((), ())), preferred_element_type=F32
    )


def bit_of(axis, distance):
    return (lax.axis_index(axis) // distance) % 2


def swap(rows, axis, distance):
    count = lax.axis_size(axis)
    return lax.ppermute(rows, axis, [(i, i ^ distance) for i in range(count)])


def after(value, *others):
    return lax.optimization_barrier((value, *others))[0]


def pick(rows, which, dim):
    return lax.dynamic_index_in_dim(rows, which, dim, keepdims=False)


def halve(rows, step, dim=0):
    bit = bit_of(*step)
    got = swap(pick(rows, 1 - bit, dim).astype(BF16), *step)
    return pick(rows, bit, dim).astype(F32) + got.astype(F32)


def double(rows, step, dim=0):
    got = swap(rows, *step)
    second = bit_of(*step) == 1
    return jnp.stack([jnp.where(second, got, rows), jnp.where(second, rows, got)], dim)


def bits_below(count):
    return [1 << i for i in range(count.bit_length() - 1)]


def token(value):
    return (value[(0,) * value.ndim].astype(F32) * 0.0).astype(jnp.int32)


def to_streams(rows, count, order=0):
    me = lax.axis_index("seq")
    block = rows.shape[1]
    whole = jnp.zeros((count * block, rows.shape[2]), rows.dtype)
    for shift in range(count):
        part = pick(rows, (me + shift) % count + order, 0)
        if shift:
            part = lax.ppermute(part, "seq", [(i, (i + shift) % count) for i in range(count)])
        whole = lax.dynamic_update_slice_in_dim(whole, part, (me - shift) % count * block, 0)
    return whole


def by_stream(rows):
    return jnp.swapaxes(rows, 0, 1)


def attend_kernel(
    len_ref, qc_ref, qp_ref, k_ref, v_ref, rel_ref, table_ref, cos_ref, sin_ref, *rest
):
    p_ref, o_ref = rest[-2:]
    rows = qc_ref.shape[0] // ATTEND_PARTS
    keys = k_ref.shape[0]
    half = cos_ref.shape[1]
    split = CMEM + MEM
    for part in range(ATTEND_PARTS):
        at = slice(part * rows, (part + 1) * rows)
        mixed = contract(qp_ref[at], rel_ref[...], 1, 1)
        lead, tail = mixed[:, :half], mixed[:, half:]
        cos, sin = cos_ref[at], sin_ref[at]
        rotated = jnp.concatenate(
            [(lead * sin + tail * cos).astype(BF16), (tail * sin - lead * cos).astype(BF16)], 1
        )
        scores = contract(qc_ref[at], k_ref[...], 1, 1) + contract(rotated, table_ref[...], 1, 1)
        row_ids = part * rows + lax.broadcasted_iota(jnp.int32, (rows, keys - split), 0)
        col_ids = lax.broadcasted_iota(jnp.int32, (rows, keys - split), 1)
        visible = (col_ids <= row_ids) & (col_ids < len_ref[0])
        past = scores[:, :split]
        own = jnp.where(visible, scores[:, split:], -1e30)
        top = jnp.maximum(jnp.max(past, 1, keepdims=True), jnp.max(own, 1, keepdims=True))
        factor = math.log2(math.e) / math.sqrt(DH)
        past = jnp.exp2((past - top) * factor)
        own = jnp.exp2((own - top) * factor)
        total = jnp.sum(past, 1, keepdims=True) + jnp.sum(own, 1, keepdims=True)
        scale = 1.0 / total
        prob = jnp.concatenate([(past * scale).astype(BF16), (own * scale).astype(BF16)], 1)
        p_ref[0, at] = prob
        o_ref[at] = jnp.dot(prob, v_ref[...], preferred_element_type=F32).astype(BF16)


def attend(heads, length, content, position, keys, values, w_rel, table, cos, sin, first=(), into=()):
    seg, width = content.shape
    total = keys.shape[0]
    block = seg
    start, count = heads.start, len(heads)
    head = lambda h, q: (0, start + h)
    rows = lambda h, q: (q, start + h)
    whole = pl.BlockSpec(memory_space=pl.ANY)
    operands = [length, content, position, keys, values, w_rel, table, cos, sin]
    aliases = {len(operands) + i: i for i in range(len(into))}
    operands += [*into, *first]
    return pl.pallas_call(
        attend_kernel,
        grid=(count, seg // block),
        in_specs=[
            pl.BlockSpec(memory_space=pltpu.SMEM),
            pl.BlockSpec((block, DH), rows),
            pl.BlockSpec((block, DH), rows),
            pl.BlockSpec((total, DH), head),
            pl.BlockSpec((total, DH), head),
            pl.BlockSpec((width, DH), head),
            pl.BlockSpec((total, width), lambda h, q: (0, 0)),
            pl.BlockSpec((block, width // 2), lambda h, q: (q, 0)),
            pl.BlockSpec((block, width // 2), lambda h, q: (q, 0)),
        ]
        + [whole] * (len(into) + len(first)),
        out_specs=[
            pl.BlockSpec((1, block, total), lambda h, q: (start + h, q, 0)),
            pl.BlockSpec((block, DH), rows),
        ],
        out_shape=[
            jax.ShapeDtypeStruct((H, seg, total), BF16),
            jax.ShapeDtypeStruct((seg, width), BF16),
        ],
        input_output_aliases=aliases,
        compiler_params=pltpu.CompilerParams(vmem_limit_bytes=52 * MIB),
        cost_estimate=SHORT,
        name="attend",
    )(*operands)


def attend_back_kernel(
    with_sums,
    bits_ref,
    p_ref,
    da_ref,
    qc_ref,
    qp_ref,
    k_ref,
    v_ref,
    rel_ref,
    wq_ref,
    wk_ref,
    wv_ref,
    normed_ref,
    table_ref,
    cos_ref,
    sin_ref,
    *rest,
):
    keep_ref, give_ref, rows_ref, along_ref, shift_ref, bias_ref = rest[-6:]
    head = pl.program_id(0)
    scale = 1.0 / math.sqrt(DH)
    half = cos_ref.shape[1]
    seg = da_ref.shape[0]
    past = k_ref.shape[0] - seg
    block = seg // BACK_PARTS
    dk_t = dv_t = drel_t = 0.0
    d_content_sum = d_position_sum = 0.0
    d_queries = []
    for part in range(BACK_PARTS):
        at = slice(part * block, (part + 1) * block)
        prob = p_ref[0, at]
        d_attn = da_ref[at]
        dv_t = dv_t + contract(d_attn, prob, 0, 0)
        d_prob = contract(d_attn, v_ref[...], 1, 1)
        prob_f = prob.astype(F32)
        weighted = prob_f * d_prob
        inner = jnp.sum(weighted, 1, keepdims=True)
        d_scores = (weighted - prob_f * inner).astype(BF16)
        dk_t = dk_t + contract(qc_ref[at], d_scores, 0, 0)
        d_content = jnp.dot(d_scores, k_ref[...], preferred_element_type=F32) * scale
        d_rotated = jnp.dot(d_scores, table_ref[...], preferred_element_type=F32)
        lead, tail = d_rotated[:, :half], d_rotated[:, half:]
        cos, sin = cos_ref[at] * scale, sin_ref[at] * scale
        d_mixed = jnp.concatenate(
            [(lead * sin - tail * cos).astype(BF16), (lead * cos + tail * sin).astype(BF16)], 1
        )
        d_position = jnp.dot(d_mixed, rel_ref[...], preferred_element_type=F32)
        drel_t = drel_t + contract(qp_ref[at], d_mixed, 0, 0)
        d_queries.append((d_content + d_position).astype(BF16))
        d_content_sum = d_content_sum + jnp.sum(d_content, 0, keepdims=True)
        d_position_sum = d_position_sum + jnp.sum(d_position, 0, keepdims=True)
    bias_ref[...] = jnp.concatenate([d_content_sum, d_position_sum], 0)

    d_query = jnp.concatenate(d_queries, 0)
    d_kv_t = jnp.concatenate([(dk_t * scale).astype(BF16), dv_t.astype(BF16)], 0)
    d_kv = d_kv_t[:, past:].T
    of_kv_t = jnp.dot(d_kv_t, normed_ref[...], preferred_element_type=F32)
    of_query_t = contract(d_query, normed_ref[past:, :], 0, 0)
    of_query, of_key, of_value = of_query_t.T, of_kv_t[:DH].T, of_kv_t[DH:].T
    mine = bits_ref[0] == 1
    for i, grad in enumerate((of_query, drel_t.T, of_key, of_value)):
        middle = grad.shape[0] // 2
        low, high = grad[:middle].astype(BF16), grad[middle:].astype(BF16)
        keep_ref[i] = jnp.where(mine, high, low)
        give_ref[i] = jnp.where(mine, low, high)
    own_rows = (
        contract(d_query, wq_ref[...], 1, 1)
        + contract(d_kv[:, :DH], wk_ref[...], 1, 1)
        + contract(d_kv[:, DH:], wv_ref[...], 1, 1)
    )
    wq = wq_ref[...].astype(F32)
    wk = wk_ref[...].astype(F32)
    wv = wv_ref[...].astype(F32)
    sums = jnp.sum(d_kv_t.astype(F32), 1, keepdims=True).T
    own_along = of_query * wq + of_key * wk + of_value * wv
    own_shift = (
        jnp.sum(d_query.astype(F32), 0, keepdims=True) * wq + sums[:, :DH] * wk + sums[:, DH:] * wv
    )

    @pl.when(head == 0)
    def _():
        before = rest[:3] if with_sums else None
        rows_ref[...] = own_rows + before[0][...] if with_sums else own_rows
        along_ref[...] = own_along + before[1][...] if with_sums else own_along
        shift_ref[...] = own_shift + before[2][...] if with_sums else own_shift

    @pl.when(head > 0)
    def _():
        rows_ref[...] += own_rows
        along_ref[...] += own_along
        shift_ref[...] += own_shift


def attend_back(
    start,
    count,
    heads,
    bits,
    prob,
    d_attn,
    content,
    position,
    keys,
    values,
    w_rel,
    w_query,
    w_key,
    w_value,
    normed,
    table,
    cos,
    sin,
    sums=(),
    into=(),
    first=(),
):
    seg, width = content.shape
    total = keys.shape[0]
    block = seg
    column = lambda h: (0, start + h)
    rows = lambda h: (0, start + h)
    fixed = lambda h: (0, 0)
    whole = pl.BlockSpec(memory_space=pl.ANY)
    operands = [bits, prob, d_attn, content, position, keys, values, w_rel]
    operands += [w_query, w_key, w_value, normed, table, cos, sin]
    aliases = {}
    sum_specs = [
        pl.BlockSpec((seg, width), fixed),
        pl.BlockSpec((width, DH), fixed),
        pl.BlockSpec((width, DH), fixed),
    ]
    for i in range(len(sums)):
        aliases[len(operands) + i] = 2 + i
    operands += [*sums]
    for i in range(len(into)):
        aliases[len(operands) + i] = i
    operands += [*into, *first]
    half = jax.ShapeDtypeStruct(into[0].shape if into else (4, width // 2, len(heads) * DH), BF16)
    half_spec = pl.BlockSpec((4, width // 2, DH), lambda h: (0, 0, start - heads.start + h))
    return pl.pallas_call(
        functools.partial(attend_back_kernel, bool(sums)),
        grid=(count,),
        in_specs=[
            pl.BlockSpec(memory_space=pltpu.SMEM),
            pl.BlockSpec((1, block, total), lambda h: (start + h, 0, 0)),
            pl.BlockSpec((block, DH), rows),
            pl.BlockSpec((block, DH), rows),
            pl.BlockSpec((block, DH), rows),
            pl.BlockSpec((total, DH), column),
            pl.BlockSpec((total, DH), column),
            pl.BlockSpec((width, DH), column),
            pl.BlockSpec((width, DH), column),
            pl.BlockSpec((width, DH), column),
            pl.BlockSpec((width, DH), column),
            pl.BlockSpec(memory_space=pltpu.VMEM),
            pl.BlockSpec(memory_space=pltpu.VMEM),
            pl.BlockSpec(memory_space=pltpu.VMEM),
            pl.BlockSpec(memory_space=pltpu.VMEM),
        ]
        + sum_specs[: len(sums)]
        + [whole] * (len(into) + len(first)),
        out_specs=[half_spec, half_spec] + sum_specs + [pl.BlockSpec((2, DH), lambda h: (0, h))],
        out_shape=[
            half,
            half,
            jax.ShapeDtypeStruct((seg, width), F32),
            jax.ShapeDtypeStruct((width, DH), F32),
            jax.ShapeDtypeStruct((width, DH), F32),
            jax.ShapeDtypeStruct((2, count * DH), F32),
        ],
        input_output_aliases=aliases,
        compiler_params=pltpu.CompilerParams(vmem_limit_bytes=52 * MIB),
        cost_estimate=SHORT,
        name="attend_back",
    )(*operands)


def in_vmem():
    return pl.BlockSpec(memory_space=pltpu.VMEM)


def norm_kernel(count, owners_ref, *refs):
    parts, (gain_ref, shift_ref), (normed_ref, rows_ref) = refs[:count], refs[count : count + 2], refs[-2:]
    block = rows_ref.shape[1]
    for i, part in enumerate(parts):
        owner = owners_ref[i]
        for kind in range(3):
            low = part[kind * block : (kind + 1) * block]
            values = low.astype(F32)
            center = values - jnp.mean(values, -1, keepdims=True)
            spread = jnp.mean(center * center, -1, keepdims=True)
            normed = center * lax.rsqrt(spread + 1e-05) * gain_ref[...] + shift_ref[...]
            normed_ref[kind, owner] = normed.astype(BF16)
            if kind == 2:
                rows_ref[owner] = low


def norm_context(parts, owners, gain, shift, after=()):
    rows, width = parts[0].shape
    block = rows // 3
    normed, inputs = pl.pallas_call(
        functools.partial(norm_kernel, len(parts)),
        in_specs=[pl.BlockSpec(memory_space=pltpu.SMEM)] + [in_vmem()] * (len(parts) + 2)
        + [pl.BlockSpec(memory_space=pl.ANY)] * len(after),
        out_specs=[in_vmem(), in_vmem()],
        out_shape=[
            jax.ShapeDtypeStruct((3, len(parts), block, width), BF16),
            jax.ShapeDtypeStruct((len(parts), block, width), BF16),
        ],
        compiler_params=pltpu.CompilerParams(vmem_limit_bytes=48 * MIB),
        cost_estimate=SHORT,
        name="norm_context",
    )(owners, *parts, gain.reshape(1, -1), shift.reshape(1, -1), *after)
    return normed.reshape(-1, width), inputs.reshape(-1, width)


def place_kernel(count, owners_ref, *refs):
    for i, part in enumerate(refs[:count]):
        refs[-1][owners_ref[i]] = part[...]


def place_rows(parts, owners, after=()):
    rows, width = parts[0].shape
    return pl.pallas_call(
        functools.partial(place_kernel, len(parts)),
        in_specs=[pl.BlockSpec(memory_space=pltpu.SMEM)]
        + [in_vmem()] * len(parts)
        + [pl.BlockSpec(memory_space=pl.ANY)] * len(after),
        out_specs=in_vmem(),
        out_shape=jax.ShapeDtypeStruct((len(parts), rows, width), parts[0].dtype),
        cost_estimate=SHORT,
        name="place_rows",
    )(owners, *parts, *after)


def hold(values, *others):
    whole = pl.BlockSpec(memory_space=pl.ANY)
    return pl.pallas_call(
        lambda *refs: None,
        in_specs=[whole] * (len(values) + len(others)),
        out_specs=[whole] * len(values),
        out_shape=[jax.ShapeDtypeStruct(v.shape, v.dtype) for v in values],
        input_output_aliases={i: i for i in range(len(values))},
        cost_estimate=SHORT,
        name="hold",
    )(*values, *others)


def copy_kernel(rows_ref, *refs):
    refs[-1][...] = rows_ref[...]


def copy_after(rows, *others):
    return pl.pallas_call(
        copy_kernel,
        in_specs=[in_vmem()] + [pl.BlockSpec(memory_space=pl.ANY)] * len(others),
        out_specs=in_vmem(),
        out_shape=jax.ShapeDtypeStruct(rows.shape, rows.dtype),
        cost_estimate=SHORT,
        name="copy_after",
    )(rows, *others)


def out_grad_kernel(bits_ref, left_ref, right_ref, keep_ref, give_ref):
    mine = bits_ref[0] == 1
    grad = contract(left_ref[...], right_ref[...], 0, 0)
    middle, columns = keep_ref.shape[1:]
    for i in range(2):
        part = grad[:, i * columns : (i + 1) * columns]
        low, high = part[:middle].astype(BF16), part[middle:].astype(BF16)
        keep_ref[i] = jnp.where(mine, high, low)
        give_ref[i] = jnp.where(mine, low, high)


def out_grad(bits, left, right):
    width = right.shape[1]
    half = jax.ShapeDtypeStruct((6, width // 2, width // 2), BF16)
    spec = pl.BlockSpec((2, width // 2, width // 2), lambda i: (2, 0, 0))
    whole = pl.BlockSpec(left.shape, lambda i: (0, 0))
    return pl.pallas_call(
        out_grad_kernel,
        grid=(1,),
        in_specs=[pl.BlockSpec(memory_space=pltpu.SMEM), whole, whole],
        out_specs=[spec, spec],
        out_shape=[half, half],
        compiler_params=pltpu.CompilerParams(vmem_limit_bytes=48 * MIB),
        cost_estimate=SHORT,
        name="out_grad",
    )(bits, left, right)


def finish_kernel(bits_ref, own_ref, got_ref, *refs):
    outs = refs[-5:]
    own = pl.program_id(0) == bits_ref[0]

    def write(ref):
        for i in range(4):
            outs[i][...] = ref[i].astype(F32)
        if ref.shape[0] > 4:
            half = ref.shape[2]
            outs[4][:, :half] = ref[4].astype(F32)
            outs[4][:, half:] = ref[5].astype(F32)

    pl.when(own)(lambda: write(own_ref))
    pl.when(jnp.logical_not(own))(lambda: write(got_ref))


def finish(bits, column, columns, own, got, results):
    count, rows, width = own.shape
    fixed = pl.BlockSpec(own.shape, lambda i: (0, 0, 0))
    block = pl.BlockSpec((rows, width), lambda i: (i, column))
    last = pl.BlockSpec((rows, columns * width), lambda i: (i, 0))
    out = jax.ShapeDtypeStruct((2 * rows, columns * width), F32)
    if count == 4:
        out_specs, before = [block] * 4, results[:4]
    else:
        out_specs, before = [block] * 4 + [last], results
    sums = pl.pallas_call(
        finish_kernel if count > 4 else lambda *refs: finish_kernel(*refs, None),
        grid=(2,),
        in_specs=[pl.BlockSpec(memory_space=pltpu.SMEM), fixed, fixed]
        + [pl.BlockSpec(memory_space=pl.ANY)] * len(before),
        out_specs=out_specs,
        out_shape=[out] * len(out_specs),
        input_output_aliases={3 + i: i for i in range(len(before))},
        compiler_params=pltpu.CompilerParams(vmem_limit_bytes=48 * MIB),
        cost_estimate=SHORT,
        name="finish",
    )(bits, own, got, *before)
    return list(sums) + list(results[len(sums) :])


class Chain:
    def __init__(self, moves, keeps, gives):
        self.moves, self.keeps, self.gives = list(moves), keeps, gives
        self.join = False
        self.got = None


def parts_of(move):
    return len(move[1])


def split_rows(rows, pre):
    lead, count, columns = rows.shape
    return rows.reshape(lead, pre, 2, count // (2 * pre), columns)


def first_halves(rows, move):
    keeps, gives = [], []
    size = rows.shape[0] // parts_of(move)
    for i, (step, pre) in enumerate(move[1]):
        cells = split_rows(rows[i * size : (i + 1) * size], pre)
        bit = bit_of(*step)
        flat = (size, -1, rows.shape[2])
        keeps.append(pick(cells, bit, 2).reshape(flat))
        gives.append(pick(cells, 1 - bit, 2).reshape(flat))
    return keeps, gives


def round_of(chains, bits, bit_names, after=(), through=()):
    operands, plans, out_shape = [], [], []
    for chain in chains:
        kind, cuts = chain.moves.pop(0)
        nexts = chain.moves[0] if chain.moves else None
        got = chain.got or [[swap(give, *step)] for give, (step, _) in zip(chain.gives, cuts)]
        chain.got = None
        held = chain.keeps if kind == "halve" else chain.gives
        leads, columns = [h.shape[0] for h in held], held[0].shape[2]
        total = sum(leads)
        next_kind, next_cuts = nexts if nexts else ("end", [None])
        size = total // len(next_cuts)
        ins, views = [], []
        for i, (h, g) in enumerate(zip(held, got)):
            base = sum(leads[:i])
            if kind == "double":
                cells = max(pre for _, pre in cuts)
                view = (h.shape[0], cells, h.shape[1] // cells, columns)
                bit = (bit_names.index(cuts[i][0]), cuts[i][1])
            elif next_kind == "halve":
                cells = max([2 * pre for _, pre in next_cuts] + [len(g) for g in got])
                view = (h.shape[0], cells, h.shape[1] // cells, columns)
                bit = None
            else:
                view = h.shape
                bit = None
            ins.append((len(operands), base, bit, view, len(g)))
            operands += [h.reshape(view)]
            operands += [r.reshape(view[0], -1, *view[2:]) if len(g) > 1 else r.reshape(view) for r in g]
        rows = held[0].shape[1]
        outs = []
        for j, cut in enumerate(next_cuts):
            if next_kind == "halve":
                cells = ins[0][3][1]
                shape = (size, cells // 2, rows // cells, columns)
                outs.append((len(out_shape), bit_names.index(cut[0]), cut[1]))
                out_shape += [jax.ShapeDtypeStruct(shape, BF16)] * 2
            else:
                if kind == "double":
                    cells = ins[0][3][1]
                    shape = (size, cells * 2, rows // cells, columns)
                    if chain.join and next_kind == "end":
                        shape = (1, cells * 2, rows // cells, size * columns)
                else:
                    shape = (size, rows, columns)
                outs.append((len(out_shape), None, None))
                out_shape += [jax.ShapeDtypeStruct(shape, held[0].dtype)]
        plans.append((kind, next_kind, size, ins, outs))

    def kernel(bits_ref, *refs):
        inputs, results = refs[: len(operands)], refs[len(refs) - len(out_shape) - len(through) :]
        for kind, next_kind, size, ins, outs in plans:
            for at, base, bit, view, count in ins:
                held_ref, got_ref = inputs[at], inputs[at + 1]
                got_refs = inputs[at + 1 : at + 1 + count]
                for i in range(view[0]):
                    where, which = divmod(base + i, size)
                    out, out_bit, out_pre = outs[where]
                    if kind == "double":
                        mine = bits_ref[bit[0]]
                        run = view[1] // bit[1]
                        for cell in range(view[1]):
                            for side, ref in ((mine, held_ref), (1 - mine, got_ref)):
                                place = (cell // run * 2 + side) * run + cell % run
                                if results[out].shape[3] == ref.shape[3]:
                                    results[out][which, place] = ref[i, cell]
                                else:
                                    wide = slice(which * ref.shape[3], (which + 1) * ref.shape[3])
                                    results[out][0, place, :, wide] = ref[i, cell]
                    elif next_kind == "halve":
                        mine = bits_ref[out_bit]
                        run = view[1] // (2 * out_pre)
                        for cell in range(view[1] // 2):
                            if count > 1:
                                sums = []
                                for side in range(2):
                                    place = (cell // run * 2 + side) * run + cell % run
                                    piece, rest = divmod(place * count, view[1])
                                    more = got_refs[piece][i, rest // count].astype(F32)
                                    sums.append(held_ref[i, place].astype(F32) + more)
                                high = mine == 1
                                results[out][which, cell] = jnp.where(high, sums[1], sums[0]).astype(BF16)
                                results[out + 1][which, cell] = jnp.where(high, *sums).astype(BF16)
                                continue
                            for side, slot in ((mine, out), (1 - mine, out + 1)):
                                place = (cell // run * 2 + side) * run + cell % run
                                results[slot][which, cell] = (
                                    held_ref[i, place].astype(F32) + got_ref[i, place].astype(F32)
                                ).astype(BF16)
                    else:
                        results[out][which] = (held_ref[i].astype(F32) + got_ref[i].astype(F32)).astype(
                            results[out].dtype
                        )

    in_vmem = pl.BlockSpec(memory_space=pltpu.VMEM)
    results = pl.pallas_call(
        kernel,
        in_specs=[pl.BlockSpec(memory_space=pltpu.SMEM)]
        + [in_vmem] * len(operands)
        + [pl.BlockSpec(memory_space=pl.ANY)] * (len(through) + len(after)),
        out_specs=[in_vmem] * len(out_shape) + [pl.BlockSpec(memory_space=pl.ANY)] * len(through),
        out_shape=out_shape + [jax.ShapeDtypeStruct(r.shape, r.dtype) for r in through],
        input_output_aliases={
            1 + len(operands) + i: len(out_shape) + i for i in range(len(through))
        },
        compiler_params=pltpu.CompilerParams(vmem_limit_bytes=48 * MIB),
        cost_estimate=SHORT,
        name="add_and_split",
    )(bits, *operands, *through, *after)
    for chain, (kind, next_kind, size, ins, outs) in zip(chains, plans):
        flat = lambda r: r.reshape(r.shape[0], -1, r.shape[-1])
        if next_kind == "halve":
            chain.keeps = [flat(results[o]) for o, _, _ in outs]
            chain.gives = [flat(results[o + 1]) for o, _, _ in outs]
        else:
            chain.keeps = []
            chain.gives = [flat(results[o]) for o, _, _ in outs]
    return results[len(out_shape) :]


def own_streams_plan(
    inputs,
    memory,
    compressed,
    seg_len,
    gain_first,
    shift_first,
    w_query,
    w_key,
    w_value,
    w_rel,
    bias_content,
    bias_position,
    w_out,
    gain_second,
    shift_second,
    w_up,
    bias_up,
    w_down,
    bias_down,
    w_comp,
    comp_bias,
    grad_out,
    grad_comp,
):
    seq_parts = lax.axis_size("seq")
    dp_parts = lax.axis_size("dp")
    me = lax.axis_index("seq")
    seg_dev, streams, width = inputs.shape
    seg = seg_dev * seq_parts
    split = CMEM + MEM
    hidden_dev = w_down.shape[0]

    core = ("dp", 1)
    wide = [("dp", d) for d in reversed(bits_below(dp_parts)[1:])]
    line = [("seq", d) for d in bits_below(seq_parts)]
    there = list(range(len(wide)))
    back = there[::-1]
    core_bit = bit_of(*core)

    bit_names = [core] + wide + line
    bits = jnp.stack([bit_of(*name) for name in bit_names]).astype(jnp.int32)
    wide_in = [[(wide[i], 1), (wide[j], 1 << j)] for i, j in zip(there, back)]
    line_in = [[(step, 1 << i)] for i, step in enumerate(reversed(line))][::-1]
    core_cut, line_cuts, wide_cuts = [(core, 1)], [[(s, 1)] for s in line], [[(s, 1)] for s in wide]

    def moves_of(cuts, collected):
        return [("halve", c) for c in cuts] + [("double", c) for c in reversed(collected)]

    piece = hidden_dev // dp_parts
    place = lax.axis_index("dp")

    def gathered(rows):
        rows = jnp.swapaxes(rows.reshape(piece, 2, width // 2), 0, 1)
        chain = Chain(moves_of([], wide_in + line_in), [], [rows])
        chain.join = True
        return chain

    up_piece = lax.dynamic_slice_in_dim(w_up, place * piece, piece, 1).T
    up_chain = gathered(up_piece)
    round_of([up_chain], bits, bit_names)
    for step in line[:-1]:
        round_of([up_chain], bits, bit_names)
    order_two = token(up_chain.gives[0])

    key_cos, key_sin = sinusoids(jnp.arange(split + seg, dtype=jnp.int32))
    table = jnp.concatenate([key_cos, key_sin], -1).astype(BF16)
    cos, sin = key_cos[split:], key_sin[split:]

    owners = jnp.stack([(me - shift) % seq_parts for shift in range(seq_parts)]).astype(jnp.int32)

    def send(parts):
        return [parts[0]] + [
            lax.ppermute(part, "seq", [(i, (i + shift) % seq_parts) for i in range(seq_parts)])
            for shift, part in enumerate(parts)
            if shift
        ]

    def parts_for(rows, order=0):
        return [pick(rows, (me + shift) % seq_parts + order, 0) for shift in range(seq_parts)]

    def from_streams(parts):
        return by_stream(place_rows(send(parts), owners))

    blocks = [by_stream(rows) for rows in (compressed, memory, inputs)]
    parts = send(parts_for(jnp.concatenate(blocks, 1)))
    down_piece = lax.dynamic_slice_in_dim(w_down, place * piece + order_two, piece, 0)
    down_chain = gathered(down_piece)
    round_of([up_chain], bits, bit_names)
    go_parts = parts_for(by_stream(grad_out))
    memory_rows = by_stream(memory)
    idle = [*up_chain.gives, *down_chain.gives, table, cos, sin, *go_parts, memory_rows]
    normed, x_rows = norm_context(parts, owners, gain_first, shift_first, idle)
    length = lax.dynamic_slice_in_dim(seg_len, me, 1)
    order = token(normed)
    bias_all = lax.dynamic_slice_in_dim(bias_up.reshape(-1, 2, piece), core_bit + order, 1, 1)
    bias_all = bias_all.reshape(1, -1)

    seg_normed = normed[split:]
    queries = jnp.dot(seg_normed, w_query, preferred_element_type=F32)
    keys = jnp.dot(normed, w_key, preferred_element_type=F32).astype(BF16)
    values = jnp.dot(normed, w_value, preferred_element_type=F32).astype(BF16)
    content = (queries + bias_content).astype(BF16)
    position = (queries + bias_position).astype(BF16)
    memory_rows = copy_after(memory_rows, keys)
    memory_all = lax.all_gather(memory_rows, "seq", axis=1, tiled=True)
    given = (length, content, position, keys, values, w_rel, table, cos, sin)
    round_of([down_chain], bits, bit_names, [normed])
    round_of([down_chain], bits, bit_names, [values])
    prob, attn_out = attend(range(H // 2), *given, first=down_chain.gives)
    prob, attn_out = round_of([up_chain, down_chain], bits, bit_names, [], [prob, attn_out])
    while up_chain.moves:
        round_of([up_chain], bits, bit_names, [attn_out])
    up_half = up_chain.gives[0][0]
    bias_all = double(bias_all, line[-1], 0)
    prob, attn_out = attend(
        range(H // 2, H), *given, first=down_chain.gives + [bias_all], into=[prob, attn_out]
    )
    (attn_out,) = round_of([down_chain], bits, bit_names, [], [attn_out])
    while down_chain.moves:
        round_of([down_chain], bits, bit_names)
    down_half = down_chain.gives[0][0]
    for i, step in enumerate(line[-2::-1]):
        bias_all = double(bias_all, step, i + 1)
    bias_half = jnp.swapaxes(bias_all.reshape(seq_parts, -1, piece), 0, 1).reshape(-1).astype(F32)
    x_f = x_rows.astype(F32)
    hidden = x_f + jnp.dot(attn_out, w_out, preferred_element_type=F32)
    normed_two = layer_norm(hidden, gain_second, shift_second).astype(BF16)

    pair_normed = double(normed_two, core).reshape(-1, width)
    pre_act = contract(pair_normed, up_half, 1, 1) + bias_half
    activated = gelu_tanh(pre_act).astype(BF16)
    go_rows = place_rows(send(go_parts), owners, [activated, memory_all]).reshape(seg, width)
    pair_grad = double(go_rows, core).reshape(-1, width)
    ffn_rows = jnp.dot(activated, down_half, preferred_element_type=F32)
    ffn_rows = halve(ffn_rows.reshape(2, seg, width), core)
    output = (hidden + ffn_rows + bias_down).astype(BF16)
    output_parts = parts_for(output.reshape(seq_parts, seg_dev, width))
    groups_of = [list(range(c, dp_parts, 2)) for c in range(2)]

    def over_rows(grad):
        return lax.psum_scatter(grad, "dp", axis_index_groups=groups_of, tiled=True)

    down_sum = over_rows(contract(activated, pair_grad, 0, 0).astype(BF16))
    d_activated = contract(pair_grad, down_half, 1, 1)
    _, gelu_back = jax.vjp(gelu_tanh, pre_act)
    d_pre = gelu_back(d_activated)[0].astype(BF16)
    d_normed_two = jnp.dot(d_pre, up_half, preferred_element_type=F32)
    d_normed_two = halve(d_normed_two.reshape(2, seg, width), core)
    up_sum = over_rows(contract(d_pre, pair_normed, 0, 0).astype(BF16))
    grad_bias_half = jnp.sum(d_pre.astype(F32), 0)

    go_f = go_rows.astype(F32)
    _, norm_two_back = jax.vjp(layer_norm, hidden, gain_second, shift_second)
    d_hidden_ffn, grad_gain_second, grad_shift_second = norm_two_back(d_normed_two)
    d_hidden = go_f + d_hidden_ffn
    grad_bias_down = jnp.sum(go_f, 0)
    d_branch = d_hidden.astype(BF16)
    d_attn = contract(d_branch, w_out, 1, 1).astype(BF16)

    half_heads = H // 2
    group_moves = moves_of([core_cut] + wide_in + line_cuts, [core_cut] + wide_in + line_cuts)
    groups, biases, head_sums = [], [], []
    output_rows = send(output_parts)

    first, start = [], 0
    for call, heads in enumerate(CALLS):
        base = start // half_heads * half_heads
        group_heads = range(base, base + half_heads)
        if start == 0:
            halves = out_grad(bits, attn_out, d_branch)
        elif start == base:
            halves = []
        *halves, d_rows, along, shift_part, bias_part = attend_back(
            start, heads, group_heads, bits, prob, d_attn, content, position, keys, values,
            w_rel, w_query, w_key, w_value, normed, table, cos, sin, head_sums, halves, first,
        )
        start += heads
        passing = [*halves, d_rows, along, shift_part, bias_part]
        if call == 0:
            down_sum, *passing = hold([down_sum, *passing])
            down_sum = lax.psum_scatter(down_sum, "seq", tiled=True)
            first = output_parts[1:]
        elif call == 1:
            output_rows = place_rows(output_rows, owners, [bias_part])
            up_sum, *passing = hold([up_sum, *passing], output_rows)
            up_sum = lax.psum_scatter(up_sum, "seq", tiled=True)
            first = []
        elif call == 2:
            down_sum, *passing = round_of(groups, bits, bit_names, [], [down_sum, *passing])
            down_sum = lax.all_gather(down_sum, "dp", tiled=True)
            first = [g for c in groups for g in c.gives]
        else:
            memory_all, *passing = round_of(groups, bits, bit_names, [], [memory_all, *passing])
        *halves, d_rows, along, shift_part, bias_part = passing
        head_sums = [d_rows, along, shift_part]
        biases.append(bias_part)
        if start == group_heads.stop:
            groups.append(Chain(group_moves, [halves[0]], [halves[1]]))
            first += [halves[1]]
    output = by_stream(output_rows)

    new_rows = memory_all.shape[1] // RATE
    windows = memory_all[:, : new_rows * RATE].reshape(streams, new_rows, RATE, width)
    new_compressed = (
        jnp.einsum("srtd,tde->rse", windows, w_comp, preferred_element_type=F32) + comp_bias
    ).astype(BF16)
    grad_w_comp = jnp.einsum("srtd,rse->tde", windows, grad_comp, preferred_element_type=F32)
    grad_comp_bias = jnp.sum(grad_comp.astype(F32), (0, 1))
    comp_moves = moves_of([core_cut] + wide_cuts, [core_cut] + wide_cuts)
    comp_shape = grad_w_comp.shape
    comp = Chain(
        comp_moves, *first_halves(grad_w_comp.astype(BF16).reshape(1, -1, comp_shape[2]), comp_moves[0])
    )

    d_normed = d_rows
    _, norm_one_back = jax.vjp(lambda v: layer_norm(v, gain_first, shift_first), x_f)
    (d_context,) = norm_one_back(d_normed)
    grad_inputs = (d_hidden + d_context).astype(BF16).reshape(seq_parts, seg_dev, width)
    input_parts = parts_for(grad_inputs)
    input_rows = send(input_parts)

    grad_shift_first = jnp.sum(shift_part, 1)
    grad_gain_first = (jnp.sum(along, 1) - shift_first * grad_shift_first) / gain_first
    vectors = jnp.concatenate(
        [
            jnp.concatenate(biases, 1).reshape(-1),
            grad_gain_first,
            grad_shift_first,
            grad_gain_second,
            grad_shift_second,
            grad_bias_down,
        ]
    )
    count = vectors.shape[0]
    hidden_sums = jnp.zeros((2, grad_bias_half.shape[0]), F32)
    hidden_sums = lax.dynamic_update_slice(hidden_sums, grad_bias_half[None], (core_bit, 0))
    comp_sums = jnp.zeros((seq_parts, grad_comp_bias.shape[0]), F32)
    comp_sums = lax.dynamic_update_slice(comp_sums, grad_comp_bias[None], (me, 0))
    vectors = jnp.concatenate([vectors, hidden_sums.reshape(-1), comp_sums.reshape(-1)])
    vector = Chain([("add", [(name, 1)]) for name in bit_names], [], [vectors.reshape(1, -1, DH)])

    one, two = groups
    def finished(column, group, results):
        own = group.gives[0]
        return finish(bits, column, len(groups), own, swap(own, *core), results)

    turn, results = 0, []
    pinned = {
        1: input_parts,
        2: [input_rows[1]],
        3: [new_compressed],
        5: [*input_rows[2:-1]],
        6: [input_rows[-1]],
    }
    while len(two.moves) > 1 or vector.moves or comp.moves:
        active = [one, two] + [comp] * (turn > 0) + [vector] * (turn > 2)
        active = [c for c in active if len(c.moves) > (c in groups)]
        fence = pinned.get(turn, [])
        if turn == 7:
            grad_inputs = by_stream(place_rows(input_rows, owners))
            fence = [grad_inputs]
        if not results and len(one.moves) == 1:
            results = finished(0, one, results)
            fence = [*fence, *results]
        through = [up_sum] if turn == 0 else []
        through = round_of(active, bits, bit_names, fence, through)
        if turn == 0:
            up_sum = lax.all_gather(through[0], "dp", tiled=True)
            grad_w_down, grad_w_up = down_sum.astype(F32), up_sum.astype(F32).T
            pinned[4] = [grad_w_down]
            pinned[5] = [*pinned[5], grad_w_up]
        turn += 1
    vectors = vector.gives[0].reshape(-1)

    grad_w_comp = comp.gives[0].astype(F32).reshape(comp_shape)
    results = finished(1, two, results)
    grad_w_query, grad_w_rel, grad_w_key, grad_w_value, grad_w_out = results

    totals = vectors[:count].reshape(-1, width)
    hidden_sums = vectors[count : count + hidden_sums.size].reshape(
        [2, 1 << len(wide)] + [2] * len(line) + [piece]
    )
    for step in reversed(line):
        hidden_sums = pick(hidden_sums, bit_of(*step), 2)
    grad_bias_up = jnp.swapaxes(hidden_sums, 0, 1).reshape(-1)
    comp_sums = vectors[count + grad_bias_half.size * 2 :].reshape(comp_sums.shape)
    grad_comp_bias = pick(comp_sums, me, 0)

    return (
        output,
        grad_inputs,
        new_compressed,
        totals[2],
        totals[3],
        grad_w_query,
        grad_w_key,
        grad_w_value,
        grad_w_rel,
        totals[0],
        totals[1],
        grad_w_out,
        totals[4],
        totals[5],
        grad_w_up,
        grad_bias_up,
        grad_w_down,
        totals[6],
        grad_w_comp,
        grad_comp_bias,
    )


def on_device(*arrays):
    streams = arrays[0].shape[1]
    dp_parts, seq_parts = lax.axis_size("dp"), lax.axis_size("seq")
    fits = streams == seq_parts and seq_parts > 1 and dp_parts >= 4
    powers = (seq_parts & (seq_parts - 1)) == 0 and (dp_parts & (dp_parts - 1)) == 0
    plan = own_streams_plan if fits and powers else split_rows_plan
    return plan(*arrays)


def solution(mesh):
    in_specs = (
        P("seq", "dp", None),
        P("seq", "dp", None),
        P("seq", "dp", None),
        P("dp"),
        P(),
        P(),
        P(),
        P(),
        P(),
        P(),
        P(),
        P(),
        P(),
        P(),
        P(),
        P(None, "seq"),
        P("seq"),
        P("seq", None),
        P(),
        P(None, None, "seq"),
        P("seq"),
        P("seq", "dp", None),
        P(None, "dp", "seq"),
    )
    out_specs = (
        P("seq", "dp", None),
        P("seq", "dp", None),
        P(None, "dp", "seq"),
        P(),
        P(),
        P(),
        P(),
        P(),
        P(),
        P(),
        P(),
        P(),
        P(),
        P(),
        P(None, "seq"),
        P("seq"),
        P("seq", None),
        P(),
        P(None, None, "seq"),
        P("seq"),
    )
    return jax.shard_map(
        on_device, mesh=mesh, in_specs=in_specs, out_specs=out_specs, check_vma=False
    )
```

```python
import functools
import math

import jax
import jax.numpy as jnp
from jax import lax
from jax.experimental import pallas as pl
from jax.experimental.pallas import tpu as pltpu
from jax.sharding import PartitionSpec as P

D = 1024
H = 8
DH = 128
MEM = 512
CMEM = 512
RATE = 3


def layer_norm(values, gain, shift):
    center = values - jnp.mean(values, -1, keepdims=True)
    spread = jnp.mean(center * center, -1, keepdims=True)
    return center * lax.rsqrt(spread + 1e-05) * gain + shift


def gelu_tanh(values):
    return jax.nn.gelu(values, approximate=True)


def sinusoids(positions):
    half_width = D // 2
    frequency = jnp.exp(jnp.arange(half_width, dtype=jnp.float32) * (-2.0 * math.log(10000.0) / D))
    angles = positions.astype(jnp.float32)[:, None] * frequency[None, :]
    return (jnp.cos(angles), jnp.sin(angles))


def key_positions(seq_parts, cmem_dev, mem_dev, seg_dev):
    ctx_dev = cmem_dev + mem_dev + seg_dev
    row_ids = jnp.arange(ctx_dev * seq_parts, dtype=jnp.int32)
    device_ids = row_ids // ctx_dev
    local_ids = row_ids % ctx_dev
    in_cmem = device_ids * cmem_dev + local_ids
    in_mem = CMEM + device_ids * mem_dev + (local_ids - cmem_dev)
    in_seg = CMEM + MEM + device_ids * seg_dev + (local_ids - cmem_dev - mem_dev)
    return jnp.where(
        local_ids < cmem_dev, in_cmem, jnp.where(local_ids < cmem_dev + mem_dev, in_mem, in_seg)
    )


def rotate_rows(position_rows, rel_heads, row_sin, row_cos, half_width):
    mixed = jnp.einsum(
        "qshd,fhd->qshf", position_rows, rel_heads, preferred_element_type=jnp.float32
    )
    first_half = mixed[..., :half_width]
    second_half = mixed[..., half_width:]
    return jnp.concatenate(
        [
            first_half * row_sin + second_half * row_cos,
            second_half * row_sin - first_half * row_cos,
        ],
        -1,
    ).astype(jnp.bfloat16)


def split_rows_plan(
    inputs,
    memory,
    compressed,
    seg_len,
    gain_first,
    shift_first,
    w_query,
    w_key,
    w_value,
    w_rel,
    bias_content,
    bias_position,
    w_out,
    gain_second,
    shift_second,
    w_up,
    bias_up,
    w_down,
    bias_down,
    w_comp,
    comp_bias,
    grad_out,
    grad_comp,
):
    seq_parts = lax.axis_size("seq")
    my_index = lax.axis_index("seq")
    seg_dev, streams, model_width = inputs.shape
    mem_dev = memory.shape[0]
    cmem_dev = compressed.shape[0]
    split_at = cmem_dev + mem_dev
    ctx_dev = split_at + seg_dev
    total_keys = ctx_dev * seq_parts
    half_width = model_width // 2
    score_scale = 1.0 / math.sqrt(DH)
    key_pos = key_positions(seq_parts, cmem_dev, mem_dev, seg_dev)
    key_cos, key_sin = sinusoids(key_pos)
    pos_table = jnp.concatenate([key_cos, key_sin], -1).astype(jnp.bfloat16)
    query_rows = my_index * seg_dev + jnp.arange(seg_dev, dtype=jnp.int32)
    query_cos, query_sin = sinusoids(CMEM + MEM + query_rows)
    query_cos = query_cos[:, None, None, :]
    query_sin = query_sin[:, None, None, :]
    key_seg = key_pos - (CMEM + MEM)
    visible = (key_seg[None, None, :] < 0) | (
        key_seg[None, None, :] <= query_rows[None, :, None]
    ) & (key_seg[None, None, :] < seg_len[:, None, None])
    x_in = inputs.astype(jnp.float32)
    context = jnp.concatenate([compressed, memory, inputs], 0).astype(jnp.float32)
    normed = layer_norm(context, gain_first, shift_first)
    normed_low = normed.astype(jnp.bfloat16)
    seg_normed = normed_low[split_at:]
    queries = jnp.dot(seg_normed, w_query, preferred_element_type=jnp.float32)
    keys_low = jnp.dot(normed_low, w_key, preferred_element_type=jnp.float32).astype(jnp.bfloat16)
    values_low = jnp.dot(normed_low, w_value, preferred_element_type=jnp.float32).astype(
        jnp.bfloat16
    )
    query_content = (queries + bias_content).astype(jnp.bfloat16).reshape(seg_dev, streams, H, DH)
    query_position = (queries + bias_position).astype(jnp.bfloat16).reshape(seg_dev, streams, H, DH)
    rel_heads = w_rel.reshape(model_width, H, DH)
    rotated = rotate_rows(query_position, rel_heads, query_sin, query_cos, half_width)
    keys_all, values_all, memory_all = (
        lax.all_gather(keys_low, "seq", axis=0, tiled=True),
        lax.all_gather(values_low, "seq", axis=0, tiled=True),
        lax.all_gather(memory, "seq", axis=0, tiled=True),
    )

    def scores_of(keys_gathered):
        content = jnp.einsum(
            "qshd,kshd->shqk",
            query_content,
            keys_gathered.reshape(total_keys, streams, H, DH),
            preferred_element_type=jnp.float32,
        )
        placed = jnp.einsum("qshf,kf->shqk", rotated, pos_table, preferred_element_type=jnp.float32)
        return jnp.where(visible[:, None], (content + placed) * score_scale, -1e30)

    scores = scores_of(keys_all)
    row_max = jnp.max(scores, -1, keepdims=True)
    exp_scores = jnp.exp(scores - row_max)
    row_total = jnp.sum(exp_scores, -1, keepdims=True)
    attn_prob = (exp_scores / row_total).astype(jnp.bfloat16)
    log_total = row_max + jnp.log(row_total)
    attended = jnp.einsum(
        "shqk,kshd->qshd",
        attn_prob,
        values_all.reshape(total_keys, streams, H, DH),
        preferred_element_type=jnp.float32,
    )
    attn_out = attended.reshape(seg_dev, streams, model_width).astype(jnp.bfloat16)
    hidden = x_in + jnp.dot(attn_out, w_out, preferred_element_type=jnp.float32)
    normed_two = layer_norm(hidden, gain_second, shift_second).astype(jnp.bfloat16)
    normed_all = lax.all_gather(normed_two, "seq", axis=0, tiled=True)
    pre_act = jnp.dot(normed_all, w_up, preferred_element_type=jnp.float32) + bias_up.astype(
        jnp.float32
    )
    activated = gelu_tanh(pre_act).astype(jnp.bfloat16)
    row_piece = activated
    ffn_result = lax.psum_scatter(
        jnp.dot(row_piece, w_down, preferred_element_type=jnp.float32).astype(jnp.bfloat16),
        "seq",
        scatter_dimension=0,
        tiled=True,
    ).astype(jnp.float32)
    output = (hidden + ffn_result + bias_down).astype(jnp.bfloat16)
    grad_all = lax.all_gather(grad_out, "seq", axis=0, tiled=True)
    d_activated = jnp.einsum("rsd,fd->rsf", grad_all, w_down, preferred_element_type=jnp.float32)
    _, gelu_back = jax.vjp(gelu_tanh, pre_act)
    d_pre = gelu_back(d_activated)[0].astype(jnp.bfloat16)
    grad_w_down = jnp.einsum("rsf,rsd->fd", activated, grad_all, preferred_element_type=jnp.float32)
    grad_w_up = jnp.einsum("rsd,rsf->df", normed_all, d_pre, preferred_element_type=jnp.float32)
    grad_bias_up = jnp.sum(d_pre.astype(jnp.float32), (0, 1))
    row_piece = d_pre
    d_normed_two = lax.psum_scatter(
        jnp.einsum("rsf,df->rsd", row_piece, w_up, preferred_element_type=jnp.float32).astype(
            jnp.bfloat16
        ),
        "seq",
        scatter_dimension=0,
        tiled=True,
    ).astype(jnp.float32)
    _, norm_two_back = jax.vjp(layer_norm, hidden, gain_second, shift_second)
    d_hidden_ffn, grad_gain_second, grad_shift_second = norm_two_back(d_normed_two)
    grad_rows_f = grad_out.astype(jnp.float32)
    d_hidden = grad_rows_f + d_hidden_ffn
    grad_bias_down = jnp.sum(grad_rows_f, (0, 1))
    d_branch = d_hidden.astype(jnp.bfloat16)
    grad_w_out = jnp.einsum("rsd,rse->de", attn_out, d_branch, preferred_element_type=jnp.float32)
    d_attn = (
        jnp.einsum("rse,de->rsd", d_branch, w_out, preferred_element_type=jnp.float32)
        .astype(jnp.bfloat16)
        .reshape(seg_dev, streams, H, DH)
    )
    keys_back, values_back = (
        lax.all_gather(keys_low, "seq", axis=0, tiled=True),
        lax.all_gather(values_low, "seq", axis=0, tiled=True),
    )
    keys_heads = keys_back.reshape(total_keys, streams, H, DH)
    values_heads = values_back.reshape(total_keys, streams, H, DH)
    prob_full = jnp.exp(scores_of(keys_back) - log_total)
    prob_low = prob_full.astype(jnp.bfloat16)
    d_prob = jnp.einsum("qshd,kshd->shqk", d_attn, values_heads, preferred_element_type=jnp.float32)
    inner_sum = jnp.sum(d_prob * prob_full, -1, keepdims=True)
    d_scores = (prob_full * (d_prob - inner_sum)).astype(jnp.bfloat16)
    key_part = (
        jnp.einsum("shqk,qshd->kshd", d_scores, query_content, preferred_element_type=jnp.float32)
        * score_scale
    )
    value_part = jnp.einsum("shqk,qshd->kshd", prob_low, d_attn, preferred_element_type=jnp.float32)
    key_sums = lax.psum_scatter(
        jnp.concatenate(
            [
                key_part.reshape(ctx_dev * lax.axis_size("seq"), streams, model_width),
                value_part.reshape(ctx_dev * lax.axis_size("seq"), streams, model_width),
            ],
            -1,
        ).astype(jnp.bfloat16),
        "seq",
        scatter_dimension=0,
        tiled=True,
    ).astype(jnp.float32)
    d_keys = key_sums[..., :model_width].astype(jnp.bfloat16)
    d_values = key_sums[..., model_width:].astype(jnp.bfloat16)
    d_content = (
        jnp.einsum("shqk,kshd->qshd", d_scores, keys_heads, preferred_element_type=jnp.float32)
        * score_scale
    )
    d_rotated = (
        jnp.einsum("shqk,kf->qshf", d_scores, pos_table, preferred_element_type=jnp.float32)
        * score_scale
    )
    lead_part = d_rotated[..., :half_width]
    tail_part = d_rotated[..., half_width:]
    d_mixed = jnp.concatenate(
        [
            lead_part * query_sin - tail_part * query_cos,
            lead_part * query_cos + tail_part * query_sin,
        ],
        -1,
    ).astype(jnp.bfloat16)
    d_query_pos = jnp.einsum(
        "qshf,fhd->qshd", d_mixed, rel_heads, preferred_element_type=jnp.float32
    )
    grad_w_rel = jnp.einsum(
        "qshf,qshd->fhd", d_mixed, query_position, preferred_element_type=jnp.float32
    ).reshape(model_width, model_width)
    grad_bias_content = jnp.sum(d_content, (0, 1)).reshape(model_width)
    grad_bias_position = jnp.sum(d_query_pos, (0, 1)).reshape(model_width)
    d_queries = (
        (d_content + d_query_pos).reshape(seg_dev, streams, model_width).astype(jnp.bfloat16)
    )
    grad_w_query = jnp.einsum(
        "rsd,rse->de", seg_normed, d_queries, preferred_element_type=jnp.float32
    )
    grad_w_key = jnp.einsum("rsd,rse->de", normed_low, d_keys, preferred_element_type=jnp.float32)
    grad_w_value = jnp.einsum(
        "rsd,rse->de", normed_low, d_values, preferred_element_type=jnp.float32
    )
    d_from_kv = jnp.einsum(
        "rse,de->rsd", d_keys, w_key, preferred_element_type=jnp.float32
    ) + jnp.einsum("rse,de->rsd", d_values, w_value, preferred_element_type=jnp.float32)
    d_from_query = jnp.einsum("rse,de->rsd", d_queries, w_query, preferred_element_type=jnp.float32)
    d_normed = jnp.concatenate([d_from_kv[:split_at], d_from_kv[split_at:] + d_from_query], 0)
    _, norm_one_back = jax.vjp(layer_norm, context, gain_first, shift_first)
    d_context, grad_gain_first, grad_shift_first = norm_one_back(d_normed)
    grad_inputs = (d_hidden + d_context[split_at:]).astype(jnp.bfloat16)
    new_rows = memory_all.shape[0] // RATE
    windows = memory_all[: new_rows * RATE].reshape(new_rows, RATE, streams, model_width)
    new_compressed = (
        jnp.einsum("rtsd,tde->rse", windows, w_comp, preferred_element_type=jnp.float32) + comp_bias
    ).astype(jnp.bfloat16)
    grad_w_comp = jnp.einsum(
        "rtsd,rse->tde", windows, grad_comp, preferred_element_type=jnp.float32
    )
    grad_comp_bias = jnp.sum(grad_comp.astype(jnp.float32), (0, 1))
    (
        grad_w_query,
        grad_w_key,
        grad_w_value,
        grad_w_rel,
        grad_w_out,
        grad_bias_content,
        grad_bias_position,
        grad_gain_first,
        grad_shift_first,
        grad_gain_second,
        grad_shift_second,
        grad_bias_down,
    ) = lax.psum(
        (
            grad_w_query,
            grad_w_key,
            grad_w_value,
            grad_w_rel,
            grad_w_out,
            grad_bias_content,
            grad_bias_position,
            grad_gain_first,
            grad_shift_first,
            grad_gain_second,
            grad_shift_second,
            grad_bias_down,
        ),
        ("dp", "seq"),
    )
    grad_w_up, grad_bias_up, grad_w_down, grad_w_comp, grad_comp_bias = (
        lax.psum(grad_w_up.astype(jnp.bfloat16), "dp").astype(jnp.float32),
        lax.psum(grad_bias_up.astype(jnp.bfloat16), "dp").astype(jnp.float32),
        lax.psum(grad_w_down.astype(jnp.bfloat16), "dp").astype(jnp.float32),
        lax.psum(grad_w_comp.astype(jnp.bfloat16), "dp").astype(jnp.float32),
        lax.psum(grad_comp_bias.astype(jnp.bfloat16), "dp").astype(jnp.float32),
    )
    return (
        output,
        grad_inputs,
        new_compressed,
        grad_gain_first,
        grad_shift_first,
        grad_w_query,
        grad_w_key,
        grad_w_value,
        grad_w_rel,
        grad_bias_content,
        grad_bias_position,
        grad_w_out,
        grad_gain_second,
        grad_shift_second,
        grad_w_up,
        grad_bias_up,
        grad_w_down,
        grad_bias_down,
        grad_w_comp,
        grad_comp_bias,
    )


BF16 = jnp.bfloat16
F32 = jnp.float32
ATTEND_PARTS = 2
BACK_PARTS = 1
CALLS = (2, 2, 2, 2)
MIB = 1024 * 1024
SHORT = pl.CostEstimate(flops=1024, bytes_accessed=1024, transcendentals=0)


def contract(left, right, left_dim, right_dim):
    return lax.dot_general(
        left, right, (((left_dim,), (right_dim,)), ((), ())), preferred_element_type=F32
    )


def bit_of(axis, distance):
    return (lax.axis_index(axis) // distance) % 2


def swap(rows, axis, distance):
    count = lax.axis_size(axis)
    return lax.ppermute(rows, axis, [(i, i ^ distance) for i in range(count)])


def after(value, *others):
    return lax.optimization_barrier((value, *others))[0]


def pick(rows, which, dim):
    return lax.dynamic_index_in_dim(rows, which, dim, keepdims=False)


def halve(rows, step, dim=0):
    bit = bit_of(*step)
    got = swap(pick(rows, 1 - bit, dim).astype(BF16), *step)
    return pick(rows, bit, dim).astype(F32) + got.astype(F32)


def double(rows, step, dim=0):
    got = swap(rows, *step)
    second = bit_of(*step) == 1
    return jnp.stack([jnp.where(second, got, rows), jnp.where(second, rows, got)], dim)


def bits_below(count):
    return [1 << i for i in range(count.bit_length() - 1)]


def token(value):
    return (value[(0,) * value.ndim].astype(F32) * 0.0).astype(jnp.int32)


def to_streams(rows, count, order=0):
    me = lax.axis_index("seq")
    block = rows.shape[1]
    whole = jnp.zeros((count * block, rows.shape[2]), rows.dtype)
    for shift in range(count):
        part = pick(rows, (me + shift) % count + order, 0)
        if shift:
            part = lax.ppermute(part, "seq", [(i, (i + shift) % count) for i in range(count)])
        whole = lax.dynamic_update_slice_in_dim(whole, part, (me - shift) % count * block, 0)
    return whole


def by_stream(rows):
    return jnp.swapaxes(rows, 0, 1)


def attend_kernel(
    len_ref, qc_ref, qp_ref, k_ref, v_ref, rel_ref, table_ref, cos_ref, sin_ref, *rest
):
    p_ref, o_ref = rest[-2:]
    rows = qc_ref.shape[0] // ATTEND_PARTS
    keys = k_ref.shape[0]
    half = cos_ref.shape[1]
    split = CMEM + MEM
    for part in range(ATTEND_PARTS):
        at = slice(part * rows, (part + 1) * rows)
        mixed = contract(qp_ref[at], rel_ref[...], 1, 1)
        lead, tail = mixed[:, :half], mixed[:, half:]
        cos, sin = cos_ref[at], sin_ref[at]
        rotated = jnp.concatenate(
            [(lead * sin + tail * cos).astype(BF16), (tail * sin - lead * cos).astype(BF16)], 1
        )
        scores = contract(qc_ref[at], k_ref[...], 1, 1) + contract(rotated, table_ref[...], 1, 1)
        row_ids = part * rows + lax.broadcasted_iota(jnp.int32, (rows, keys - split), 0)
        col_ids = lax.broadcasted_iota(jnp.int32, (rows, keys - split), 1)
        visible = (col_ids <= row_ids) & (col_ids < len_ref[0])
        past = scores[:, :split]
        own = jnp.where(visible, scores[:, split:], -1e30)
        top = jnp.maximum(jnp.max(past, 1, keepdims=True), jnp.max(own, 1, keepdims=True))
        factor = math.log2(math.e) / math.sqrt(DH)
        past = jnp.exp2((past - top) * factor)
        own = jnp.exp2((own - top) * factor)
        total = jnp.sum(past, 1, keepdims=True) + jnp.sum(own, 1, keepdims=True)
        scale = 1.0 / total
        prob = jnp.concatenate([(past * scale).astype(BF16), (own * scale).astype(BF16)], 1)
        p_ref[0, at] = prob
        o_ref[at] = jnp.dot(prob, v_ref[...], preferred_element_type=F32).astype(BF16)


def attend(heads, length, content, position, keys, values, w_rel, table, cos, sin, first=(), into=()):
    seg, width = content.shape
    total = keys.shape[0]
    block = seg
    start, count = heads.start, len(heads)
    head = lambda h, q: (0, start + h)
    rows = lambda h, q: (q, start + h)
    whole = pl.BlockSpec(memory_space=pl.ANY)
    operands = [length, content, position, keys, values, w_rel, table, cos, sin]
    aliases = {len(operands) + i: i for i in range(len(into))}
    operands += [*into, *first]
    return pl.pallas_call(
        attend_kernel,
        grid=(count, seg // block),
        in_specs=[
            pl.BlockSpec(memory_space=pltpu.SMEM),
            pl.BlockSpec((block, DH), rows),
            pl.BlockSpec((block, DH), rows),
            pl.BlockSpec((total, DH), head),
            pl.BlockSpec((total, DH), head),
            pl.BlockSpec((width, DH), head),
            pl.BlockSpec((total, width), lambda h, q: (0, 0)),
            pl.BlockSpec((block, width // 2), lambda h, q: (q, 0)),
            pl.BlockSpec((block, width // 2), lambda h, q: (q, 0)),
        ]
        + [whole] * (len(into) + len(first)),
        out_specs=[
            pl.BlockSpec((1, block, total), lambda h, q: (start + h, q, 0)),
            pl.BlockSpec((block, DH), rows),
        ],
        out_shape=[
            jax.ShapeDtypeStruct((H, seg, total), BF16),
            jax.ShapeDtypeStruct((seg, width), BF16),
        ],
        input_output_aliases=aliases,
        compiler_params=pltpu.CompilerParams(vmem_limit_bytes=52 * MIB),
        cost_estimate=SHORT,
        name="attend",
    )(*operands)


def attend_back_kernel(
    with_sums,
    bits_ref,
    p_ref,
    da_ref,
    qc_ref,
    qp_ref,
    k_ref,
    v_ref,
    rel_ref,
    wq_ref,
    wk_ref,
    wv_ref,
    normed_ref,
    table_ref,
    cos_ref,
    sin_ref,
    *rest,
):
    keep_ref, give_ref, rows_ref, along_ref, shift_ref, bias_ref = rest[-6:]
    head = pl.program_id(0)
    scale = 1.0 / math.sqrt(DH)
    half = cos_ref.shape[1]
    seg = da_ref.shape[0]
    past = k_ref.shape[0] - seg
    block = seg // BACK_PARTS
    dk_t = dv_t = drel_t = 0.0
    d_content_sum = d_position_sum = 0.0
    d_queries = []
    for part in range(BACK_PARTS):
        at = slice(part * block, (part + 1) * block)
        prob = p_ref[0, at]
        d_attn = da_ref[at]
        dv_t = dv_t + contract(d_attn, prob, 0, 0)
        d_prob = contract(d_attn, v_ref[...], 1, 1)
        prob_f = prob.astype(F32)
        weighted = prob_f * d_prob
        inner = jnp.sum(weighted, 1, keepdims=True)
        d_scores = (weighted - prob_f * inner).astype(BF16)
        dk_t = dk_t + contract(qc_ref[at], d_scores, 0, 0)
        d_content = jnp.dot(d_scores, k_ref[...], preferred_element_type=F32) * scale
        d_rotated = jnp.dot(d_scores, table_ref[...], preferred_element_type=F32)
        lead, tail = d_rotated[:, :half], d_rotated[:, half:]
        cos, sin = cos_ref[at] * scale, sin_ref[at] * scale
        d_mixed = jnp.concatenate(
            [(lead * sin - tail * cos).astype(BF16), (lead * cos + tail * sin).astype(BF16)], 1
        )
        d_position = jnp.dot(d_mixed, rel_ref[...], preferred_element_type=F32)
        drel_t = drel_t + contract(qp_ref[at], d_mixed, 0, 0)
        d_queries.append((d_content + d_position).astype(BF16))
        d_content_sum = d_content_sum + jnp.sum(d_content, 0, keepdims=True)
        d_position_sum = d_position_sum + jnp.sum(d_position, 0, keepdims=True)
    bias_ref[...] = jnp.concatenate([d_content_sum, d_position_sum], 0)

    d_query = jnp.concatenate(d_queries, 0)
    d_kv_t = jnp.concatenate([(dk_t * scale).astype(BF16), dv_t.astype(BF16)], 0)
    d_kv = d_kv_t[:, past:].T
    of_kv_t = jnp.dot(d_kv_t, normed_ref[...], preferred_element_type=F32)
    of_query_t = contract(d_query, normed_ref[past:, :], 0, 0)
    of_query, of_key, of_value = of_query_t.T, of_kv_t[:DH].T, of_kv_t[DH:].T
    mine = bits_ref[0] == 1
    for i, grad in enumerate((of_query, drel_t.T, of_key, of_value)):
        middle = grad.shape[0] // 2
        low, high = grad[:middle].astype(BF16), grad[middle:].astype(BF16)
        keep_ref[i] = jnp.where(mine, high, low)
        give_ref[i] = jnp.where(mine, low, high)
    own_rows = (
        contract(d_query, wq_ref[...], 1, 1)
        + contract(d_kv[:, :DH], wk_ref[...], 1, 1)
        + contract(d_kv[:, DH:], wv_ref[...], 1, 1)
    )
    wq = wq_ref[...].astype(F32)
    wk = wk_ref[...].astype(F32)
    wv = wv_ref[...].astype(F32)
    sums = jnp.sum(d_kv_t.astype(F32), 1, keepdims=True).T
    own_along = of_query * wq + of_key * wk + of_value * wv
    own_shift = (
        jnp.sum(d_query.astype(F32), 0, keepdims=True) * wq + sums[:, :DH] * wk + sums[:, DH:] * wv
    )

    @pl.when(head == 0)
    def _():
        before = rest[:3] if with_sums else None
        rows_ref[...] = own_rows + before[0][...] if with_sums else own_rows
        along_ref[...] = own_along + before[1][...] if with_sums else own_along
        shift_ref[...] = own_shift + before[2][...] if with_sums else own_shift

    @pl.when(head > 0)
    def _():
        rows_ref[...] += own_rows
        along_ref[...] += own_along
        shift_ref[...] += own_shift


def attend_back(
    start,
    count,
    heads,
    bits,
    prob,
    d_attn,
    content,
    position,
    keys,
    values,
    w_rel,
    w_query,
    w_key,
    w_value,
    normed,
    table,
    cos,
    sin,
    sums=(),
    into=(),
    first=(),
):
    seg, width = content.shape
    total = keys.shape[0]
    block = seg
    column = lambda h: (0, start + h)
    rows = lambda h: (0, start + h)
    fixed = lambda h: (0, 0)
    whole = pl.BlockSpec(memory_space=pl.ANY)
    operands = [bits, prob, d_attn, content, position, keys, values, w_rel]
    operands += [w_query, w_key, w_value, normed, table, cos, sin]
    aliases = {}
    sum_specs = [
        pl.BlockSpec((seg, width), fixed),
        pl.BlockSpec((width, DH), fixed),
        pl.BlockSpec((width, DH), fixed),
    ]
    for i in range(len(sums)):
        aliases[len(operands) + i] = 2 + i
    operands += [*sums]
    for i in range(len(into)):
        aliases[len(operands) + i] = i
    operands += [*into, *first]
    half = jax.ShapeDtypeStruct(into[0].shape if into else (4, width // 2, len(heads) * DH), BF16)
    half_spec = pl.BlockSpec((4, width // 2, DH), lambda h: (0, 0, start - heads.start + h))
    return pl.pallas_call(
        functools.partial(attend_back_kernel, bool(sums)),
        grid=(count,),
        in_specs=[
            pl.BlockSpec(memory_space=pltpu.SMEM),
            pl.BlockSpec((1, block, total), lambda h: (start + h, 0, 0)),
            pl.BlockSpec((block, DH), rows),
            pl.BlockSpec((block, DH), rows),
            pl.BlockSpec((block, DH), rows),
            pl.BlockSpec((total, DH), column),
            pl.BlockSpec((total, DH), column),
            pl.BlockSpec((width, DH), column),
            pl.BlockSpec((width, DH), column),
            pl.BlockSpec((width, DH), column),
            pl.BlockSpec((width, DH), column),
            pl.BlockSpec(memory_space=pltpu.VMEM),
            pl.BlockSpec(memory_space=pltpu.VMEM),
            pl.BlockSpec(memory_space=pltpu.VMEM),
            pl.BlockSpec(memory_space=pltpu.VMEM),
        ]
        + sum_specs[: len(sums)]
        + [whole] * (len(into) + len(first)),
        out_specs=[half_spec, half_spec] + sum_specs + [pl.BlockSpec((2, DH), lambda h: (0, h))],
        out_shape=[
            half,
            half,
            jax.ShapeDtypeStruct((seg, width), F32),
            jax.ShapeDtypeStruct((width, DH), F32),
            jax.ShapeDtypeStruct((width, DH), F32),
            jax.ShapeDtypeStruct((2, count * DH), F32),
        ],
        input_output_aliases=aliases,
        compiler_params=pltpu.CompilerParams(vmem_limit_bytes=52 * MIB),
        cost_estimate=SHORT,
        name="attend_back",
    )(*operands)


def in_vmem():
    return pl.BlockSpec(memory_space=pltpu.VMEM)


def norm_kernel(count, owners_ref, *refs):
    parts, (gain_ref, shift_ref), (normed_ref, rows_ref) = refs[:count], refs[count : count + 2], refs[-2:]
    block = rows_ref.shape[1]
    for i, part in enumerate(parts):
        owner = owners_ref[i]
        for kind in range(3):
            low = part[kind * block : (kind + 1) * block]
            values = low.astype(F32)
            center = values - jnp.mean(values, -1, keepdims=True)
            spread = jnp.mean(center * center, -1, keepdims=True)
            normed = center * lax.rsqrt(spread + 1e-05) * gain_ref[...] + shift_ref[...]
            normed_ref[kind, owner] = normed.astype(BF16)
            if kind == 2:
                rows_ref[owner] = low


def norm_context(parts, owners, gain, shift, after=()):
    rows, width = parts[0].shape
    block = rows // 3
    normed, inputs = pl.pallas_call(
        functools.partial(norm_kernel, len(parts)),
        in_specs=[pl.BlockSpec(memory_space=pltpu.SMEM)] + [in_vmem()] * (len(parts) + 2)
        + [pl.BlockSpec(memory_space=pl.ANY)] * len(after),
        out_specs=[in_vmem(), in_vmem()],
        out_shape=[
            jax.ShapeDtypeStruct((3, len(parts), block, width), BF16),
            jax.ShapeDtypeStruct((len(parts), block, width), BF16),
        ],
        compiler_params=pltpu.CompilerParams(vmem_limit_bytes=48 * MIB),
        cost_estimate=SHORT,
        name="norm_context",
    )(owners, *parts, gain.reshape(1, -1), shift.reshape(1, -1), *after)
    return normed.reshape(-1, width), inputs.reshape(-1, width)


def place_kernel(count, owners_ref, *refs):
    for i, part in enumerate(refs[:count]):
        refs[-1][owners_ref[i]] = part[...]


def place_rows(parts, owners, after=()):
    rows, width = parts[0].shape
    return pl.pallas_call(
        functools.partial(place_kernel, len(parts)),
        in_specs=[pl.BlockSpec(memory_space=pltpu.SMEM)]
        + [in_vmem()] * len(parts)
        + [pl.BlockSpec(memory_space=pl.ANY)] * len(after),
        out_specs=in_vmem(),
        out_shape=jax.ShapeDtypeStruct((len(parts), rows, width), parts[0].dtype),
        cost_estimate=SHORT,
        name="place_rows",
    )(owners, *parts, *after)


def hold(values, *others):
    whole = pl.BlockSpec(memory_space=pl.ANY)
    return pl.pallas_call(
        lambda *refs: None,
        in_specs=[whole] * (len(values) + len(others)),
        out_specs=[whole] * len(values),
        out_shape=[jax.ShapeDtypeStruct(v.shape, v.dtype) for v in values],
        input_output_aliases={i: i for i in range(len(values))},
        cost_estimate=SHORT,
        name="hold",
    )(*values, *others)


def copy_kernel(rows_ref, *refs):
    refs[-1][...] = rows_ref[...]


def copy_after(rows, *others):
    return pl.pallas_call(
        copy_kernel,
        in_specs=[in_vmem()] + [pl.BlockSpec(memory_space=pl.ANY)] * len(others),
        out_specs=in_vmem(),
        out_shape=jax.ShapeDtypeStruct(rows.shape, rows.dtype),
        cost_estimate=SHORT,
        name="copy_after",
    )(rows, *others)


def out_grad_kernel(bits_ref, left_ref, right_ref, keep_ref, give_ref):
    mine = bits_ref[0] == 1
    grad = contract(left_ref[...], right_ref[...], 0, 0)
    middle, columns = keep_ref.shape[1:]
    for i in range(2):
        part = grad[:, i * columns : (i + 1) * columns]
        low, high = part[:middle].astype(BF16), part[middle:].astype(BF16)
        keep_ref[i] = jnp.where(mine, high, low)
        give_ref[i] = jnp.where(mine, low, high)


def out_grad(bits, left, right):
    width = right.shape[1]
    half = jax.ShapeDtypeStruct((6, width // 2, width // 2), BF16)
    spec = pl.BlockSpec((2, width // 2, width // 2), lambda i: (2, 0, 0))
    whole = pl.BlockSpec(left.shape, lambda i: (0, 0))
    return pl.pallas_call(
        out_grad_kernel,
        grid=(1,),
        in_specs=[pl.BlockSpec(memory_space=pltpu.SMEM), whole, whole],
        out_specs=[spec, spec],
        out_shape=[half, half],
        compiler_params=pltpu.CompilerParams(vmem_limit_bytes=48 * MIB),
        cost_estimate=SHORT,
        name="out_grad",
    )(bits, left, right)


def finish_kernel(bits_ref, own_ref, got_ref, *refs):
    outs = refs[-5:]
    own = pl.program_id(0) == bits_ref[0]

    def write(ref):
        for i in range(4):
            outs[i][...] = ref[i].astype(F32)
        if ref.shape[0] > 4:
            half = ref.shape[2]
            outs[4][:, :half] = ref[4].astype(F32)
            outs[4][:, half:] = ref[5].astype(F32)

    pl.when(own)(lambda: write(own_ref))
    pl.when(jnp.logical_not(own))(lambda: write(got_ref))


def finish(bits, column, columns, own, got, results):
    count, rows, width = own.shape
    fixed = pl.BlockSpec(own.shape, lambda i: (0, 0, 0))
    block = pl.BlockSpec((rows, width), lambda i: (i, column))
    last = pl.BlockSpec((rows, columns * width), lambda i: (i, 0))
    out = jax.ShapeDtypeStruct((2 * rows, columns * width), F32)
    if count == 4:
        out_specs, before = [block] * 4, results[:4]
    else:
        out_specs, before = [block] * 4 + [last], results
    sums = pl.pallas_call(
        finish_kernel if count > 4 else lambda *refs: finish_kernel(*refs, None),
        grid=(2,),
        in_specs=[pl.BlockSpec(memory_space=pltpu.SMEM), fixed, fixed]
        + [pl.BlockSpec(memory_space=pl.ANY)] * len(before),
        out_specs=out_specs,
        out_shape=[out] * len(out_specs),
        input_output_aliases={3 + i: i for i in range(len(before))},
        compiler_params=pltpu.CompilerParams(vmem_limit_bytes=48 * MIB),
        cost_estimate=SHORT,
        name="finish",
    )(bits, own, got, *before)
    return list(sums) + list(results[len(sums) :])


class Chain:
    def __init__(self, moves, keeps, gives):
        self.moves, self.keeps, self.gives = list(moves), keeps, gives
        self.join = False
        self.got = None


def parts_of(move):
    return len(move[1])


def split_rows(rows, pre):
    lead, count, columns = rows.shape
    return rows.reshape(lead, pre, 2, count // (2 * pre), columns)


def first_halves(rows, move):
    keeps, gives = [], []
    size = rows.shape[0] // parts_of(move)
    for i, (step, pre) in enumerate(move[1]):
        cells = split_rows(rows[i * size : (i + 1) * size], pre)
        bit = bit_of(*step)
        flat = (size, -1, rows.shape[2])
        keeps.append(pick(cells, bit, 2).reshape(flat))
        gives.append(pick(cells, 1 - bit, 2).reshape(flat))
    return keeps, gives


def round_of(chains, bits, bit_names, after=(), through=()):
    operands, plans, out_shape = [], [], []
    for chain in chains:
        kind, cuts = chain.moves.pop(0)
        nexts = chain.moves[0] if chain.moves else None
        got = chain.got or [[swap(give, *step)] for give, (step, _) in zip(chain.gives, cuts)]
        chain.got = None
        held = chain.keeps if kind == "halve" else chain.gives
        leads, columns = [h.shape[0] for h in held], held[0].shape[2]
        total = sum(leads)
        next_kind, next_cuts = nexts if nexts else ("end", [None])
        size = total // len(next_cuts)
        ins, views = [], []
        for i, (h, g) in enumerate(zip(held, got)):
            base = sum(leads[:i])
            if kind == "double":
                cells = max(pre for _, pre in cuts)
                view = (h.shape[0], cells, h.shape[1] // cells, columns)
                bit = (bit_names.index(cuts[i][0]), cuts[i][1])
            elif next_kind == "halve":
                cells = max([2 * pre for _, pre in next_cuts] + [len(g) for g in got])
                view = (h.shape[0], cells, h.shape[1] // cells, columns)
                bit = None
            else:
                view = h.shape
                bit = None
            ins.append((len(operands), base, bit, view, len(g)))
            operands += [h.reshape(view)]
            operands += [r.reshape(view[0], -1, *view[2:]) if len(g) > 1 else r.reshape(view) for r in g]
        rows = held[0].shape[1]
        outs = []
        for j, cut in enumerate(next_cuts):
            if next_kind == "halve":
                cells = ins[0][3][1]
                shape = (size, cells // 2, rows // cells, columns)
                outs.append((len(out_shape), bit_names.index(cut[0]), cut[1]))
                out_shape += [jax.ShapeDtypeStruct(shape, BF16)] * 2
            else:
                if kind == "double":
                    cells = ins[0][3][1]
                    shape = (size, cells * 2, rows // cells, columns)
                    if chain.join and next_kind == "end":
                        shape = (1, cells * 2, rows // cells, size * columns)
                else:
                    shape = (size, rows, columns)
                outs.append((len(out_shape), None, None))
                out_shape += [jax.ShapeDtypeStruct(shape, held[0].dtype)]
        plans.append((kind, next_kind, size, ins, outs))

    def kernel(bits_ref, *refs):
        inputs, results = refs[: len(operands)], refs[len(refs) - len(out_shape) - len(through) :]
        for kind, next_kind, size, ins, outs in plans:
            for at, base, bit, view, count in ins:
                held_ref, got_ref = inputs[at], inputs[at + 1]
                got_refs = inputs[at + 1 : at + 1 + count]
                for i in range(view[0]):
                    where, which = divmod(base + i, size)
                    out, out_bit, out_pre = outs[where]
                    if kind == "double":
                        mine = bits_ref[bit[0]]
                        run = view[1] // bit[1]
                        for cell in range(view[1]):
                            for side, ref in ((mine, held_ref), (1 - mine, got_ref)):
                                place = (cell // run * 2 + side) * run + cell % run
                                if results[out].shape[3] == ref.shape[3]:
                                    results[out][which, place] = ref[i, cell]
                                else:
                                    wide = slice(which * ref.shape[3], (which + 1) * ref.shape[3])
                                    results[out][0, place, :, wide] = ref[i, cell]
                    elif next_kind == "halve":
                        mine = bits_ref[out_bit]
                        run = view[1] // (2 * out_pre)
                        for cell in range(view[1] // 2):
                            if count > 1:
                                sums = []
                                for side in range(2):
                                    place = (cell // run * 2 + side) * run + cell % run
                                    piece, rest = divmod(place * count, view[1])
                                    more = got_refs[piece][i, rest // count].astype(F32)
                                    sums.append(held_ref[i, place].astype(F32) + more)
                                high = mine == 1
                                results[out][which, cell] = jnp.where(high, sums[1], sums[0]).astype(BF16)
                                results[out + 1][which, cell] = jnp.where(high, *sums).astype(BF16)
                                continue
                            for side, slot in ((mine, out), (1 - mine, out + 1)):
                                place = (cell // run * 2 + side) * run + cell % run
                                results[slot][which, cell] = (
                                    held_ref[i, place].astype(F32) + got_ref[i, place].astype(F32)
                                ).astype(BF16)
                    else:
                        results[out][which] = (held_ref[i].astype(F32) + got_ref[i].astype(F32)).astype(
                            results[out].dtype
                        )

    in_vmem = pl.BlockSpec(memory_space=pltpu.VMEM)
    results = pl.pallas_call(
        kernel,
        in_specs=[pl.BlockSpec(memory_space=pltpu.SMEM)]
        + [in_vmem] * len(operands)
        + [pl.BlockSpec(memory_space=pl.ANY)] * (len(through) + len(after)),
        out_specs=[in_vmem] * len(out_shape) + [pl.BlockSpec(memory_space=pl.ANY)] * len(through),
        out_shape=out_shape + [jax.ShapeDtypeStruct(r.shape, r.dtype) for r in through],
        input_output_aliases={
            1 + len(operands) + i: len(out_shape) + i for i in range(len(through))
        },
        compiler_params=pltpu.CompilerParams(vmem_limit_bytes=48 * MIB),
        cost_estimate=SHORT,
        name="add_and_split",
    )(bits, *operands, *through, *after)
    for chain, (kind, next_kind, size, ins, outs) in zip(chains, plans):
        flat = lambda r: r.reshape(r.shape[0], -1, r.shape[-1])
        if next_kind == "halve":
            chain.keeps = [flat(results[o]) for o, _, _ in outs]
            chain.gives = [flat(results[o + 1]) for o, _, _ in outs]
        else:
            chain.keeps = []
            chain.gives = [flat(results[o]) for o, _, _ in outs]
    return results[len(out_shape) :]


def input_grad_kernel(targets_ref, d_rows_ref, x_ref, d_hidden_ref, gain_ref, *outs):
    block = outs[0].shape[0]
    for i, out in enumerate(outs):
        at = pl.ds(pl.multiple_of(targets_ref[i] * block, block), block)
        values = x_ref[at, :].astype(F32)
        center = values - jnp.mean(values, -1, keepdims=True)
        spread = jnp.mean(center * center, -1, keepdims=True)
        inverse = lax.rsqrt(spread + 1e-05)
        unit = center * inverse
        grad = d_rows_ref[at, :] * gain_ref[...]
        mean = jnp.mean(grad, -1, keepdims=True)
        along = jnp.mean(grad * unit, -1, keepdims=True)
        out[...] = (d_hidden_ref[at, :] + inverse * (grad - mean - unit * along)).astype(BF16)


def input_grad(targets, d_rows, rows, d_hidden, gain, count):
    block = jax.ShapeDtypeStruct((rows.shape[0] // count, rows.shape[1]), BF16)
    return pl.pallas_call(
        input_grad_kernel,
        in_specs=[pl.BlockSpec(memory_space=pltpu.SMEM)] + [in_vmem()] * 4,
        out_specs=[in_vmem()] * count,
        out_shape=[block] * count,
        compiler_params=pltpu.CompilerParams(vmem_limit_bytes=48 * MIB),
        cost_estimate=SHORT,
        name="input_grad",
    )(targets, d_rows, rows, d_hidden, gain.reshape(1, -1))


def widen_kernel(rows_ref, out_ref):
    out_ref[...] = rows_ref[...].astype(F32)


def widen_flip_kernel(rows_ref, out_ref):
    out_ref[...] = rows_ref[...].astype(F32).T


def widen(rows, flip=False):
    count, width = rows.shape
    block = count // 4
    out = pl.BlockSpec((width, block), lambda i: (0, i)) if flip else pl.BlockSpec((block, width), lambda i: (i, 0))
    return pl.pallas_call(
        widen_flip_kernel if flip else widen_kernel,
        grid=(4,),
        in_specs=[pl.BlockSpec((block, width), lambda i: (i, 0))],
        out_specs=out,
        out_shape=jax.ShapeDtypeStruct((width, count) if flip else (count, width), F32),
        compiler_params=pltpu.CompilerParams(vmem_limit_bytes=48 * MIB),
        cost_estimate=SHORT,
        name="widen",
    )(rows)


def own_streams_plan(
    inputs,
    memory,
    compressed,
    seg_len,
    gain_first,
    shift_first,
    w_query,
    w_key,
    w_value,
    w_rel,
    bias_content,
    bias_position,
    w_out,
    gain_second,
    shift_second,
    w_up,
    bias_up,
    w_down,
    bias_down,
    w_comp,
    comp_bias,
    grad_out,
    grad_comp,
):
    seq_parts = lax.axis_size("seq")
    dp_parts = lax.axis_size("dp")
    me = lax.axis_index("seq")
    seg_dev, streams, width = inputs.shape
    seg = seg_dev * seq_parts
    split = CMEM + MEM
    hidden_dev = w_down.shape[0]

    core = ("dp", 1)
    wide = [("dp", d) for d in reversed(bits_below(dp_parts)[1:])]
    line = [("seq", d) for d in bits_below(seq_parts)]
    there = list(range(len(wide)))
    back = there[::-1]
    core_bit = bit_of(*core)

    bit_names = [core] + wide + line
    bits = jnp.stack([bit_of(*name) for name in bit_names]).astype(jnp.int32)
    wide_in = [[(wide[i], 1), (wide[j], 1 << j)] for i, j in zip(there, back)]
    line_in = [[(step, 1 << i)] for i, step in enumerate(reversed(line))][::-1]
    core_cut, line_cuts, wide_cuts = [(core, 1)], [[(s, 1)] for s in line], [[(s, 1)] for s in wide]

    def moves_of(cuts, collected):
        return [("halve", c) for c in cuts] + [("double", c) for c in reversed(collected)]

    piece = hidden_dev // dp_parts
    place = lax.axis_index("dp")

    def gathered(rows):
        rows = jnp.swapaxes(rows.reshape(piece, 2, width // 2), 0, 1)
        chain = Chain(moves_of([], wide_in + line_in), [], [rows])
        chain.join = True
        return chain

    up_piece = lax.dynamic_slice_in_dim(w_up, place * piece, piece, 1).T
    up_chain = gathered(up_piece)
    round_of([up_chain], bits, bit_names)
    for step in line[:-1]:
        round_of([up_chain], bits, bit_names)
    order_two = token(up_chain.gives[0])

    key_cos, key_sin = sinusoids(jnp.arange(split + seg, dtype=jnp.int32))
    table = jnp.concatenate([key_cos, key_sin], -1).astype(BF16)
    cos, sin = key_cos[split:], key_sin[split:]

    owners = jnp.stack([(me - shift) % seq_parts for shift in range(seq_parts)]).astype(jnp.int32)

    def send(parts):
        return [parts[0]] + [
            lax.ppermute(part, "seq", [(i, (i + shift) % seq_parts) for i in range(seq_parts)])
            for shift, part in enumerate(parts)
            if shift
        ]

    def parts_for(rows, order=0):
        return [pick(rows, (me + shift) % seq_parts + order, 0) for shift in range(seq_parts)]

    def from_streams(parts):
        return by_stream(place_rows(send(parts), owners))

    blocks = [by_stream(rows) for rows in (compressed, memory, inputs)]
    parts = send(parts_for(jnp.concatenate(blocks, 1)))
    down_piece = lax.dynamic_slice_in_dim(w_down, place * piece + order_two, piece, 0)
    down_chain = gathered(down_piece)
    go_parts = parts_for(by_stream(grad_out))
    memory_rows = by_stream(memory)
    idle = [*up_chain.gives, *down_chain.gives, table, cos, sin, *go_parts, memory_rows]
    normed, x_rows = norm_context(parts, owners, gain_first, shift_first, idle)
    length = lax.dynamic_slice_in_dim(seg_len, me, 1)
    round_of([up_chain], bits, bit_names, [normed])
    order = token(normed)
    bias_all = lax.dynamic_slice_in_dim(bias_up.reshape(-1, 2, piece), core_bit + order, 1, 1)
    bias_all = bias_all.reshape(1, -1)

    seg_normed = normed[split:]
    queries = jnp.dot(seg_normed, w_query, preferred_element_type=F32)
    keys = jnp.dot(normed, w_key, preferred_element_type=F32).astype(BF16)
    values = jnp.dot(normed, w_value, preferred_element_type=F32).astype(BF16)
    content = (queries + bias_content).astype(BF16)
    position = (queries + bias_position).astype(BF16)
    given = (length, content, position, keys, values, w_rel, table, cos, sin)
    round_of([down_chain], bits, bit_names, [normed])
    round_of([down_chain], bits, bit_names, [values])
    memory_rows = copy_after(memory_rows, down_chain.gives[0])
    memory_all = lax.all_gather(memory_rows, "seq", axis=1, tiled=True)
    prob, attn_out = attend(range(H // 2), *given, first=down_chain.gives)
    prob, attn_out = round_of([up_chain, down_chain], bits, bit_names, [], [prob, attn_out])
    while up_chain.moves:
        round_of([up_chain], bits, bit_names, [attn_out])
    up_half = up_chain.gives[0][0]
    bias_all = double(bias_all, line[-1], 0)
    prob, attn_out = attend(
        range(H // 2, H), *given, first=down_chain.gives + [bias_all], into=[prob, attn_out]
    )
    (attn_out,) = round_of([down_chain], bits, bit_names, [], [attn_out])
    while down_chain.moves:
        round_of([down_chain], bits, bit_names)
    down_half = down_chain.gives[0][0]
    for i, step in enumerate(line[-2::-1]):
        bias_all = double(bias_all, step, i + 1)
    bias_half = jnp.swapaxes(bias_all.reshape(seq_parts, -1, piece), 0, 1).reshape(-1).astype(F32)
    x_f = x_rows.astype(F32)
    hidden = x_f + jnp.dot(attn_out, w_out, preferred_element_type=F32)
    normed_two = layer_norm(hidden, gain_second, shift_second).astype(BF16)

    pair_normed = double(normed_two, core).reshape(-1, width)
    pre_act = contract(pair_normed, up_half, 1, 1) + bias_half
    activated = gelu_tanh(pre_act).astype(BF16)
    go_rows = place_rows(send(go_parts), owners, [activated, memory_all]).reshape(seg, width)
    pair_grad = double(go_rows, core).reshape(-1, width)
    ffn_rows = jnp.dot(activated, down_half, preferred_element_type=F32)
    ffn_rows = halve(ffn_rows.reshape(2, seg, width), core)
    output = (hidden + ffn_rows + bias_down).astype(BF16)
    output_parts = parts_for(output.reshape(seq_parts, seg_dev, width))
    groups_of = [list(range(c, dp_parts, 2)) for c in range(2)]

    def over_rows(grad):
        return lax.psum_scatter(grad, "dp", axis_index_groups=groups_of, tiled=True)

    down_sum = over_rows(contract(activated, pair_grad, 0, 0).astype(BF16))
    d_activated = contract(pair_grad, down_half, 1, 1)
    _, gelu_back = jax.vjp(gelu_tanh, pre_act)
    d_pre = gelu_back(d_activated)[0].astype(BF16)
    d_normed_two = jnp.dot(d_pre, up_half, preferred_element_type=F32)
    d_normed_two = halve(d_normed_two.reshape(2, seg, width), core)
    up_sum = over_rows(contract(d_pre, pair_normed, 0, 0).astype(BF16))
    grad_bias_half = jnp.sum(d_pre.astype(F32), 0)

    go_f = go_rows.astype(F32)
    _, norm_two_back = jax.vjp(layer_norm, hidden, gain_second, shift_second)
    d_hidden_ffn, grad_gain_second, grad_shift_second = norm_two_back(d_normed_two)
    d_hidden = go_f + d_hidden_ffn
    grad_bias_down = jnp.sum(go_f, 0)
    d_branch = d_hidden.astype(BF16)
    d_attn = contract(d_branch, w_out, 1, 1).astype(BF16)

    half_heads = H // 2
    group_moves = moves_of([core_cut] + wide_in + line_cuts, [core_cut] + wide_in + line_cuts)
    groups, biases, head_sums = [], [], []
    output_rows = send(output_parts)

    first, start = [], 0
    for call, heads in enumerate(CALLS):
        base = start // half_heads * half_heads
        group_heads = range(base, base + half_heads)
        if start == 0:
            halves = out_grad(bits, attn_out, d_branch)
        elif start == base:
            halves = []
        *halves, d_rows, along, shift_part, bias_part = attend_back(
            start, heads, group_heads, bits, prob, d_attn, content, position, keys, values,
            w_rel, w_query, w_key, w_value, normed, table, cos, sin, head_sums, halves, first,
        )
        start += heads
        passing = [*halves, d_rows, along, shift_part, bias_part]
        if call == 0:
            down_sum, *passing = hold([down_sum, *passing])
            down_sum = lax.psum_scatter(down_sum, "seq", tiled=True)
            first = output_parts[1:]
        elif call == 1:
            output_rows = place_rows(output_rows, owners, [bias_part])
            up_sum, *passing = hold([up_sum, *passing], output_rows)
            up_sum = lax.psum_scatter(up_sum, "seq", tiled=True)
            first = []
        elif call == 2:
            passing = round_of(groups, bits, bit_names, [], passing)
            first = [g for c in groups for g in c.gives]
        else:
            down_sum, *passing = round_of(groups, bits, bit_names, [], [down_sum, *passing])
            down_sum = lax.all_gather(down_sum, "dp", tiled=True)
        *halves, d_rows, along, shift_part, bias_part = passing
        head_sums = [d_rows, along, shift_part]
        biases.append(bias_part)
        if start == group_heads.stop:
            groups.append(Chain(group_moves, [halves[0]], [halves[1]]))
            first += [halves[1]]
    output = by_stream(output_rows)

    def compress(memory_all):
        new_rows = memory_all.shape[1] // RATE
        windows = memory_all[:, : new_rows * RATE].reshape(streams, new_rows, RATE, width)
        made = jnp.einsum("srtd,tde->rse", windows, w_comp, preferred_element_type=F32)
        grad = jnp.einsum("srtd,rse->tde", windows, grad_comp, preferred_element_type=F32)
        grad = grad.astype(BF16).reshape(1, -1, grad.shape[2])
        moves = moves_of([core_cut] + wide_cuts, [core_cut] + wide_cuts)
        return (made + comp_bias).astype(BF16), Chain(moves, *first_halves(grad, moves[0]))

    grad_comp_bias = jnp.sum(grad_comp.astype(F32), (0, 1))
    targets = jnp.stack([(me + shift) % seq_parts for shift in range(seq_parts)]).astype(jnp.int32)
    input_parts = input_grad(targets, d_rows, x_rows, d_hidden, gain_first, seq_parts)
    input_rows = send(input_parts)

    grad_shift_first = jnp.sum(shift_part, 1)
    grad_gain_first = (jnp.sum(along, 1) - shift_first * grad_shift_first) / gain_first
    vectors = jnp.concatenate(
        [
            jnp.concatenate(biases, 1).reshape(-1),
            grad_gain_first,
            grad_shift_first,
            grad_gain_second,
            grad_shift_second,
            grad_bias_down,
        ]
    )
    count = vectors.shape[0]
    hidden_sums = jnp.zeros((2, grad_bias_half.shape[0]), F32)
    hidden_sums = lax.dynamic_update_slice(hidden_sums, grad_bias_half[None], (core_bit, 0))
    comp_sums = jnp.zeros((seq_parts, grad_comp_bias.shape[0]), F32)
    comp_sums = lax.dynamic_update_slice(comp_sums, grad_comp_bias[None], (me, 0))
    vectors = jnp.concatenate([vectors, hidden_sums.reshape(-1), comp_sums.reshape(-1)])
    vector = Chain([("add", [(name, 1)]) for name in bit_names], [], [vectors.reshape(1, -1, DH)])

    one, two = groups
    def finished(column, group, results):
        own = group.gives[0]
        return finish(bits, column, len(groups), own, swap(own, *core), results)

    turn, results = 0, []
    pinned = {
        1: input_parts,
        2: [input_rows[1]],
        5: [*input_rows[2:-1]],
        6: [input_rows[-1]],
    }
    comp = None
    while len(two.moves) > 1 or vector.moves:
        active = [one, two] + [comp] * (turn > 0) + [vector] * (turn > 2)
        active = [c for c in active if len(c.moves) > (c in groups)]
        fence = pinned.get(turn, [])
        if turn == 7:
            grad_inputs = by_stream(place_rows(input_rows, owners))
            fence = [grad_inputs]
        if turn == 8:
            results = finished(0, one, results)
            grad_w_comp = widen(comp.gives[0][0]).reshape(w_comp.shape)
            fence = [*fence, *results, grad_w_comp]
        through = [up_sum, memory_all] if turn == 0 else []
        through = round_of(active, bits, bit_names, fence, through)
        if turn == 0:
            up_sum = lax.all_gather(through[0], "dp", tiled=True)
            new_compressed, comp = compress(through[1])
            pinned[3] = [new_compressed, output]
            grad_w_down, grad_w_up = widen(down_sum), widen(up_sum, True)
            pinned[4] = [grad_w_down]
            pinned[5] = [*pinned[5], grad_w_up]
        turn += 1
    vectors = vector.gives[0].reshape(-1)

    results = finished(1, two, results)
    grad_w_query, grad_w_rel, grad_w_key, grad_w_value, grad_w_out = results

    totals = vectors[:count].reshape(-1, width)
    hidden_sums = vectors[count : count + hidden_sums.size].reshape(
        [2, 1 << len(wide)] + [2] * len(line) + [piece]
    )
    for step in reversed(line):
        hidden_sums = pick(hidden_sums, bit_of(*step), 2)
    grad_bias_up = jnp.swapaxes(hidden_sums, 0, 1).reshape(-1)
    comp_sums = vectors[count + grad_bias_half.size * 2 :].reshape(comp_sums.shape)
    grad_comp_bias = pick(comp_sums, me, 0)

    return (
        output,
        grad_inputs,
        new_compressed,
        totals[2],
        totals[3],
        grad_w_query,
        grad_w_key,
        grad_w_value,
        grad_w_rel,
        totals[0],
        totals[1],
        grad_w_out,
        totals[4],
        totals[5],
        grad_w_up,
        grad_bias_up,
        grad_w_down,
        totals[6],
        grad_w_comp,
        grad_comp_bias,
    )


def on_device(*arrays):
    streams = arrays[0].shape[1]
    dp_parts, seq_parts = lax.axis_size("dp"), lax.axis_size("seq")
    fits = streams == seq_parts and seq_parts > 1 and dp_parts >= 4
    powers = (seq_parts & (seq_parts - 1)) == 0 and (dp_parts & (dp_parts - 1)) == 0
    plan = own_streams_plan if fits and powers else split_rows_plan
    return plan(*arrays)


def solution(mesh):
    in_specs = (
        P("seq", "dp", None),
        P("seq", "dp", None),
        P("seq", "dp", None),
        P("dp"),
        P(),
        P(),
        P(),
        P(),
        P(),
        P(),
        P(),
        P(),
        P(),
        P(),
        P(),
        P(None, "seq"),
        P("seq"),
        P("seq", None),
        P(),
        P(None, None, "seq"),
        P("seq"),
        P("seq", "dp", None),
        P(None, "dp", "seq"),
    )
    out_specs = (
        P("seq", "dp", None),
        P("seq", "dp", None),
        P(None, "dp", "seq"),
        P(),
        P(),
        P(),
        P(),
        P(),
        P(),
        P(),
        P(),
        P(),
        P(),
        P(),
        P(None, "seq"),
        P("seq"),
        P("seq", None),
        P(),
        P(None, None, "seq"),
        P("seq"),
    )
    return jax.shard_map(
        on_device, mesh=mesh, in_specs=in_specs, out_specs=out_specs, check_vma=False
    )
```

```python
import functools
import math

import jax
import jax.numpy as jnp
from jax import lax
from jax.experimental import pallas as pl
from jax.experimental.pallas import tpu as pltpu
from jax.sharding import PartitionSpec as P

D = 1024
H = 8
DH = 128
MEM = 512
CMEM = 512
RATE = 3


def layer_norm(values, gain, shift):
    center = values - jnp.mean(values, -1, keepdims=True)
    spread = jnp.mean(center * center, -1, keepdims=True)
    return center * lax.rsqrt(spread + 1e-05) * gain + shift


def gelu_tanh(values):
    return jax.nn.gelu(values, approximate=True)


def sinusoids(positions):
    half_width = D // 2
    frequency = jnp.exp(jnp.arange(half_width, dtype=jnp.float32) * (-2.0 * math.log(10000.0) / D))
    angles = positions.astype(jnp.float32)[:, None] * frequency[None, :]
    return (jnp.cos(angles), jnp.sin(angles))


def key_positions(seq_parts, cmem_dev, mem_dev, seg_dev):
    ctx_dev = cmem_dev + mem_dev + seg_dev
    row_ids = jnp.arange(ctx_dev * seq_parts, dtype=jnp.int32)
    device_ids = row_ids // ctx_dev
    local_ids = row_ids % ctx_dev
    in_cmem = device_ids * cmem_dev + local_ids
    in_mem = CMEM + device_ids * mem_dev + (local_ids - cmem_dev)
    in_seg = CMEM + MEM + device_ids * seg_dev + (local_ids - cmem_dev - mem_dev)
    return jnp.where(
        local_ids < cmem_dev, in_cmem, jnp.where(local_ids < cmem_dev + mem_dev, in_mem, in_seg)
    )


def rotate_rows(position_rows, rel_heads, row_sin, row_cos, half_width):
    mixed = jnp.einsum(
        "qshd,fhd->qshf", position_rows, rel_heads, preferred_element_type=jnp.float32
    )
    first_half = mixed[..., :half_width]
    second_half = mixed[..., half_width:]
    return jnp.concatenate(
        [
            first_half * row_sin + second_half * row_cos,
            second_half * row_sin - first_half * row_cos,
        ],
        -1,
    ).astype(jnp.bfloat16)


def split_rows_plan(
    inputs,
    memory,
    compressed,
    seg_len,
    gain_first,
    shift_first,
    w_query,
    w_key,
    w_value,
    w_rel,
    bias_content,
    bias_position,
    w_out,
    gain_second,
    shift_second,
    w_up,
    bias_up,
    w_down,
    bias_down,
    w_comp,
    comp_bias,
    grad_out,
    grad_comp,
):
    seq_parts = lax.axis_size("seq")
    my_index = lax.axis_index("seq")
    seg_dev, streams, model_width = inputs.shape
    mem_dev = memory.shape[0]
    cmem_dev = compressed.shape[0]
    split_at = cmem_dev + mem_dev
    ctx_dev = split_at + seg_dev
    total_keys = ctx_dev * seq_parts
    half_width = model_width // 2
    score_scale = 1.0 / math.sqrt(DH)
    key_pos = key_positions(seq_parts, cmem_dev, mem_dev, seg_dev)
    key_cos, key_sin = sinusoids(key_pos)
    pos_table = jnp.concatenate([key_cos, key_sin], -1).astype(jnp.bfloat16)
    query_rows = my_index * seg_dev + jnp.arange(seg_dev, dtype=jnp.int32)
    query_cos, query_sin = sinusoids(CMEM + MEM + query_rows)
    query_cos = query_cos[:, None, None, :]
    query_sin = query_sin[:, None, None, :]
    key_seg = key_pos - (CMEM + MEM)
    visible = (key_seg[None, None, :] < 0) | (
        key_seg[None, None, :] <= query_rows[None, :, None]
    ) & (key_seg[None, None, :] < seg_len[:, None, None])
    x_in = inputs.astype(jnp.float32)
    context = jnp.concatenate([compressed, memory, inputs], 0).astype(jnp.float32)
    normed = layer_norm(context, gain_first, shift_first)
    normed_low = normed.astype(jnp.bfloat16)
    seg_normed = normed_low[split_at:]
    queries = jnp.dot(seg_normed, w_query, preferred_element_type=jnp.float32)
    keys_low = jnp.dot(normed_low, w_key, preferred_element_type=jnp.float32).astype(jnp.bfloat16)
    values_low = jnp.dot(normed_low, w_value, preferred_element_type=jnp.float32).astype(
        jnp.bfloat16
    )
    query_content = (queries + bias_content).astype(jnp.bfloat16).reshape(seg_dev, streams, H, DH)
    query_position = (queries + bias_position).astype(jnp.bfloat16).reshape(seg_dev, streams, H, DH)
    rel_heads = w_rel.reshape(model_width, H, DH)
    rotated = rotate_rows(query_position, rel_heads, query_sin, query_cos, half_width)
    keys_all, values_all, memory_all = (
        lax.all_gather(keys_low, "seq", axis=0, tiled=True),
        lax.all_gather(values_low, "seq", axis=0, tiled=True),
        lax.all_gather(memory, "seq", axis=0, tiled=True),
    )

    def scores_of(keys_gathered):
        content = jnp.einsum(
            "qshd,kshd->shqk",
            query_content,
            keys_gathered.reshape(total_keys, streams, H, DH),
            preferred_element_type=jnp.float32,
        )
        placed = jnp.einsum("qshf,kf->shqk", rotated, pos_table, preferred_element_type=jnp.float32)
        return jnp.where(visible[:, None], (content + placed) * score_scale, -1e30)

    scores = scores_of(keys_all)
    row_max = jnp.max(scores, -1, keepdims=True)
    exp_scores = jnp.exp(scores - row_max)
    row_total = jnp.sum(exp_scores, -1, keepdims=True)
    attn_prob = (exp_scores / row_total).astype(jnp.bfloat16)
    log_total = row_max + jnp.log(row_total)
    attended = jnp.einsum(
        "shqk,kshd->qshd",
        attn_prob,
        values_all.reshape(total_keys, streams, H, DH),
        preferred_element_type=jnp.float32,
    )
    attn_out = attended.reshape(seg_dev, streams, model_width).astype(jnp.bfloat16)
    hidden = x_in + jnp.dot(attn_out, w_out, preferred_element_type=jnp.float32)
    normed_two = layer_norm(hidden, gain_second, shift_second).astype(jnp.bfloat16)
    normed_all = lax.all_gather(normed_two, "seq", axis=0, tiled=True)
    pre_act = jnp.dot(normed_all, w_up, preferred_element_type=jnp.float32) + bias_up.astype(
        jnp.float32
    )
    activated = gelu_tanh(pre_act).astype(jnp.bfloat16)
    row_piece = activated
    ffn_result = lax.psum_scatter(
        jnp.dot(row_piece, w_down, preferred_element_type=jnp.float32).astype(jnp.bfloat16),
        "seq",
        scatter_dimension=0,
        tiled=True,
    ).astype(jnp.float32)
    output = (hidden + ffn_result + bias_down).astype(jnp.bfloat16)
    grad_all = lax.all_gather(grad_out, "seq", axis=0, tiled=True)
    d_activated = jnp.einsum("rsd,fd->rsf", grad_all, w_down, preferred_element_type=jnp.float32)
    _, gelu_back = jax.vjp(gelu_tanh, pre_act)
    d_pre = gelu_back(d_activated)[0].astype(jnp.bfloat16)
    grad_w_down = jnp.einsum("rsf,rsd->fd", activated, grad_all, preferred_element_type=jnp.float32)
    grad_w_up = jnp.einsum("rsd,rsf->df", normed_all, d_pre, preferred_element_type=jnp.float32)
    grad_bias_up = jnp.sum(d_pre.astype(jnp.float32), (0, 1))
    row_piece = d_pre
    d_normed_two = lax.psum_scatter(
        jnp.einsum("rsf,df->rsd", row_piece, w_up, preferred_element_type=jnp.float32).astype(
            jnp.bfloat16
        ),
        "seq",
        scatter_dimension=0,
        tiled=True,
    ).astype(jnp.float32)
    _, norm_two_back = jax.vjp(layer_norm, hidden, gain_second, shift_second)
    d_hidden_ffn, grad_gain_second, grad_shift_second = norm_two_back(d_normed_two)
    grad_rows_f = grad_out.astype(jnp.float32)
    d_hidden = grad_rows_f + d_hidden_ffn
    grad_bias_down = jnp.sum(grad_rows_f, (0, 1))
    d_branch = d_hidden.astype(jnp.bfloat16)
    grad_w_out = jnp.einsum("rsd,rse->de", attn_out, d_branch, preferred_element_type=jnp.float32)
    d_attn = (
        jnp.einsum("rse,de->rsd", d_branch, w_out, preferred_element_type=jnp.float32)
        .astype(jnp.bfloat16)
        .reshape(seg_dev, streams, H, DH)
    )
    keys_back, values_back = (
        lax.all_gather(keys_low, "seq", axis=0, tiled=True),
        lax.all_gather(values_low, "seq", axis=0, tiled=True),
    )
    keys_heads = keys_back.reshape(total_keys, streams, H, DH)
    values_heads = values_back.reshape(total_keys, streams, H, DH)
    prob_full = jnp.exp(scores_of(keys_back) - log_total)
    prob_low = prob_full.astype(jnp.bfloat16)
    d_prob = jnp.einsum("qshd,kshd->shqk", d_attn, values_heads, preferred_element_type=jnp.float32)
    inner_sum = jnp.sum(d_prob * prob_full, -1, keepdims=True)
    d_scores = (prob_full * (d_prob - inner_sum)).astype(jnp.bfloat16)
    key_part = (
        jnp.einsum("shqk,qshd->kshd", d_scores, query_content, preferred_element_type=jnp.float32)
        * score_scale
    )
    value_part = jnp.einsum("shqk,qshd->kshd", prob_low, d_attn, preferred_element_type=jnp.float32)
    key_sums = lax.psum_scatter(
        jnp.concatenate(
            [
                key_part.reshape(ctx_dev * lax.axis_size("seq"), streams, model_width),
                value_part.reshape(ctx_dev * lax.axis_size("seq"), streams, model_width),
            ],
            -1,
        ).astype(jnp.bfloat16),
        "seq",
        scatter_dimension=0,
        tiled=True,
    ).astype(jnp.float32)
    d_keys = key_sums[..., :model_width].astype(jnp.bfloat16)
    d_values = key_sums[..., model_width:].astype(jnp.bfloat16)
    d_content = (
        jnp.einsum("shqk,kshd->qshd", d_scores, keys_heads, preferred_element_type=jnp.float32)
        * score_scale
    )
    d_rotated = (
        jnp.einsum("shqk,kf->qshf", d_scores, pos_table, preferred_element_type=jnp.float32)
        * score_scale
    )
    lead_part = d_rotated[..., :half_width]
    tail_part = d_rotated[..., half_width:]
    d_mixed = jnp.concatenate(
        [
            lead_part * query_sin - tail_part * query_cos,
            lead_part * query_cos + tail_part * query_sin,
        ],
        -1,
    ).astype(jnp.bfloat16)
    d_query_pos = jnp.einsum(
        "qshf,fhd->qshd", d_mixed, rel_heads, preferred_element_type=jnp.float32
    )
    grad_w_rel = jnp.einsum(
        "qshf,qshd->fhd", d_mixed, query_position, preferred_element_type=jnp.float32
    ).reshape(model_width, model_width)
    grad_bias_content = jnp.sum(d_content, (0, 1)).reshape(model_width)
    grad_bias_position = jnp.sum(d_query_pos, (0, 1)).reshape(model_width)
    d_queries = (
        (d_content + d_query_pos).reshape(seg_dev, streams, model_width).astype(jnp.bfloat16)
    )
    grad_w_query = jnp.einsum(
        "rsd,rse->de", seg_normed, d_queries, preferred_element_type=jnp.float32
    )
    grad_w_key = jnp.einsum("rsd,rse->de", normed_low, d_keys, preferred_element_type=jnp.float32)
    grad_w_value = jnp.einsum(
        "rsd,rse->de", normed_low, d_values, preferred_element_type=jnp.float32
    )
    d_from_kv = jnp.einsum(
        "rse,de->rsd", d_keys, w_key, preferred_element_type=jnp.float32
    ) + jnp.einsum("rse,de->rsd", d_values, w_value, preferred_element_type=jnp.float32)
    d_from_query = jnp.einsum("rse,de->rsd", d_queries, w_query, preferred_element_type=jnp.float32)
    d_normed = jnp.concatenate([d_from_kv[:split_at], d_from_kv[split_at:] + d_from_query], 0)
    _, norm_one_back = jax.vjp(layer_norm, context, gain_first, shift_first)
    d_context, grad_gain_first, grad_shift_first = norm_one_back(d_normed)
    grad_inputs = (d_hidden + d_context[split_at:]).astype(jnp.bfloat16)
    new_rows = memory_all.shape[0] // RATE
    windows = memory_all[: new_rows * RATE].reshape(new_rows, RATE, streams, model_width)
    new_compressed = (
        jnp.einsum("rtsd,tde->rse", windows, w_comp, preferred_element_type=jnp.float32) + comp_bias
    ).astype(jnp.bfloat16)
    grad_w_comp = jnp.einsum(
        "rtsd,rse->tde", windows, grad_comp, preferred_element_type=jnp.float32
    )
    grad_comp_bias = jnp.sum(grad_comp.astype(jnp.float32), (0, 1))
    (
        grad_w_query,
        grad_w_key,
        grad_w_value,
        grad_w_rel,
        grad_w_out,
        grad_bias_content,
        grad_bias_position,
        grad_gain_first,
        grad_shift_first,
        grad_gain_second,
        grad_shift_second,
        grad_bias_down,
    ) = lax.psum(
        (
            grad_w_query,
            grad_w_key,
            grad_w_value,
            grad_w_rel,
            grad_w_out,
            grad_bias_content,
            grad_bias_position,
            grad_gain_first,
            grad_shift_first,
            grad_gain_second,
            grad_shift_second,
            grad_bias_down,
        ),
        ("dp", "seq"),
    )
    grad_w_up, grad_bias_up, grad_w_down, grad_w_comp, grad_comp_bias = (
        lax.psum(grad_w_up.astype(jnp.bfloat16), "dp").astype(jnp.float32),
        lax.psum(grad_bias_up.astype(jnp.bfloat16), "dp").astype(jnp.float32),
        lax.psum(grad_w_down.astype(jnp.bfloat16), "dp").astype(jnp.float32),
        lax.psum(grad_w_comp.astype(jnp.bfloat16), "dp").astype(jnp.float32),
        lax.psum(grad_comp_bias.astype(jnp.bfloat16), "dp").astype(jnp.float32),
    )
    return (
        output,
        grad_inputs,
        new_compressed,
        grad_gain_first,
        grad_shift_first,
        grad_w_query,
        grad_w_key,
        grad_w_value,
        grad_w_rel,
        grad_bias_content,
        grad_bias_position,
        grad_w_out,
        grad_gain_second,
        grad_shift_second,
        grad_w_up,
        grad_bias_up,
        grad_w_down,
        grad_bias_down,
        grad_w_comp,
        grad_comp_bias,
    )


BF16 = jnp.bfloat16
F32 = jnp.float32
ATTEND_PARTS = 2
BACK_PARTS = 1
CALLS = (2, 2, 2, 2)
MIB = 1024 * 1024
SHORT = pl.CostEstimate(flops=1024, bytes_accessed=1024, transcendentals=0)


def contract(left, right, left_dim, right_dim):
    return lax.dot_general(
        left, right, (((left_dim,), (right_dim,)), ((), ())), preferred_element_type=F32
    )


def bit_of(axis, distance):
    return (lax.axis_index(axis) // distance) % 2


def swap(rows, axis, distance):
    count = lax.axis_size(axis)
    return lax.ppermute(rows, axis, [(i, i ^ distance) for i in range(count)])


def after(value, *others):
    return lax.optimization_barrier((value, *others))[0]


def pick(rows, which, dim):
    return lax.dynamic_index_in_dim(rows, which, dim, keepdims=False)


def halve(rows, step, dim=0):
    bit = bit_of(*step)
    got = swap(pick(rows, 1 - bit, dim).astype(BF16), *step)
    return pick(rows, bit, dim).astype(F32) + got.astype(F32)


def double(rows, step, dim=0):
    got = swap(rows, *step)
    second = bit_of(*step) == 1
    return jnp.stack([jnp.where(second, got, rows), jnp.where(second, rows, got)], dim)


def bits_below(count):
    return [1 << i for i in range(count.bit_length() - 1)]


def token(value):
    return (value[(0,) * value.ndim].astype(F32) * 0.0).astype(jnp.int32)


def to_streams(rows, count, order=0):
    me = lax.axis_index("seq")
    block = rows.shape[1]
    whole = jnp.zeros((count * block, rows.shape[2]), rows.dtype)
    for shift in range(count):
        part = pick(rows, (me + shift) % count + order, 0)
        if shift:
            part = lax.ppermute(part, "seq", [(i, (i + shift) % count) for i in range(count)])
        whole = lax.dynamic_update_slice_in_dim(whole, part, (me - shift) % count * block, 0)
    return whole


def by_stream(rows):
    return jnp.swapaxes(rows, 0, 1)


def attend_kernel(
    len_ref, qc_ref, qp_ref, k_ref, v_ref, rel_ref, table_ref, cos_ref, sin_ref, *rest
):
    p_ref, o_ref = rest[-2:]
    rows = qc_ref.shape[0] // ATTEND_PARTS
    keys = k_ref.shape[0]
    half = cos_ref.shape[1]
    split = CMEM + MEM
    for part in range(ATTEND_PARTS):
        at = slice(part * rows, (part + 1) * rows)
        mixed = contract(qp_ref[at], rel_ref[...], 1, 1)
        lead, tail = mixed[:, :half], mixed[:, half:]
        cos, sin = cos_ref[at], sin_ref[at]
        rotated = jnp.concatenate(
            [(lead * sin + tail * cos).astype(BF16), (tail * sin - lead * cos).astype(BF16)], 1
        )
        scores = contract(qc_ref[at], k_ref[...], 1, 1) + contract(rotated, table_ref[...], 1, 1)
        row_ids = part * rows + lax.broadcasted_iota(jnp.int32, (rows, keys - split), 0)
        col_ids = lax.broadcasted_iota(jnp.int32, (rows, keys - split), 1)
        visible = (col_ids <= row_ids) & (col_ids < len_ref[0])
        past = scores[:, :split]
        own = jnp.where(visible, scores[:, split:], -1e30)
        top = jnp.maximum(jnp.max(past, 1, keepdims=True), jnp.max(own, 1, keepdims=True))
        factor = math.log2(math.e) / math.sqrt(DH)
        past = jnp.exp2((past - top) * factor)
        own = jnp.exp2((own - top) * factor)
        total = jnp.sum(past, 1, keepdims=True) + jnp.sum(own, 1, keepdims=True)
        scale = 1.0 / total
        prob = jnp.concatenate([(past * scale).astype(BF16), (own * scale).astype(BF16)], 1)
        p_ref[0, at] = prob
        o_ref[at] = jnp.dot(prob, v_ref[...], preferred_element_type=F32).astype(BF16)


def attend(heads, length, content, position, keys, values, w_rel, table, cos, sin, first=(), into=()):
    seg, width = content.shape
    total = keys.shape[0]
    block = seg
    start, count = heads.start, len(heads)
    head = lambda h, q: (0, start + h)
    rows = lambda h, q: (q, start + h)
    whole = pl.BlockSpec(memory_space=pl.ANY)
    operands = [length, content, position, keys, values, w_rel, table, cos, sin]
    aliases = {len(operands) + i: i for i in range(len(into))}
    operands += [*into, *first]
    return pl.pallas_call(
        attend_kernel,
        grid=(count, seg // block),
        in_specs=[
            pl.BlockSpec(memory_space=pltpu.SMEM),
            pl.BlockSpec((block, DH), rows),
            pl.BlockSpec((block, DH), rows),
            pl.BlockSpec((total, DH), head),
            pl.BlockSpec((total, DH), head),
            pl.BlockSpec((width, DH), head),
            pl.BlockSpec((total, width), lambda h, q: (0, 0)),
            pl.BlockSpec((block, width // 2), lambda h, q: (q, 0)),
            pl.BlockSpec((block, width // 2), lambda h, q: (q, 0)),
        ]
        + [whole] * (len(into) + len(first)),
        out_specs=[
            pl.BlockSpec((1, block, total), lambda h, q: (start + h, q, 0)),
            pl.BlockSpec((block, DH), rows),
        ],
        out_shape=[
            jax.ShapeDtypeStruct((H, seg, total), BF16),
            jax.ShapeDtypeStruct((seg, width), BF16),
        ],
        input_output_aliases=aliases,
        compiler_params=pltpu.CompilerParams(vmem_limit_bytes=52 * MIB),
        cost_estimate=SHORT,
        name="attend",
    )(*operands)


def attend_back_kernel(
    with_sums,
    bits_ref,
    p_ref,
    da_ref,
    qc_ref,
    qp_ref,
    k_ref,
    v_ref,
    rel_ref,
    wq_ref,
    wk_ref,
    wv_ref,
    normed_ref,
    table_ref,
    cos_ref,
    sin_ref,
    *rest,
):
    keep_ref, give_ref, rows_ref, along_ref, shift_ref, bias_ref = rest[-6:]
    head = pl.program_id(0)
    scale = 1.0 / math.sqrt(DH)
    half = cos_ref.shape[1]
    seg = da_ref.shape[0]
    past = k_ref.shape[0] - seg
    block = seg // BACK_PARTS
    dk_t = dv_t = drel_t = 0.0
    d_content_sum = d_position_sum = 0.0
    d_queries = []
    for part in range(BACK_PARTS):
        at = slice(part * block, (part + 1) * block)
        prob = p_ref[0, at]
        d_attn = da_ref[at]
        dv_t = dv_t + contract(d_attn, prob, 0, 0)
        d_prob = contract(d_attn, v_ref[...], 1, 1)
        prob_f = prob.astype(F32)
        weighted = prob_f * d_prob
        inner = jnp.sum(weighted, 1, keepdims=True)
        d_scores = (weighted - prob_f * inner).astype(BF16)
        dk_t = dk_t + contract(qc_ref[at], d_scores, 0, 0)
        d_content = jnp.dot(d_scores, k_ref[...], preferred_element_type=F32) * scale
        d_rotated = jnp.dot(d_scores, table_ref[...], preferred_element_type=F32)
        lead, tail = d_rotated[:, :half], d_rotated[:, half:]
        cos, sin = cos_ref[at] * scale, sin_ref[at] * scale
        d_mixed = jnp.concatenate(
            [(lead * sin - tail * cos).astype(BF16), (lead * cos + tail * sin).astype(BF16)], 1
        )
        d_position = jnp.dot(d_mixed, rel_ref[...], preferred_element_type=F32)
        drel_t = drel_t + contract(qp_ref[at], d_mixed, 0, 0)
        d_queries.append((d_content + d_position).astype(BF16))
        d_content_sum = d_content_sum + jnp.sum(d_content, 0, keepdims=True)
        d_position_sum = d_position_sum + jnp.sum(d_position, 0, keepdims=True)
    bias_ref[...] = jnp.concatenate([d_content_sum, d_position_sum], 0)

    d_query = jnp.concatenate(d_queries, 0)
    d_kv_t = jnp.concatenate([(dk_t * scale).astype(BF16), dv_t.astype(BF16)], 0)
    d_kv = d_kv_t[:, past:].T
    of_kv_t = jnp.dot(d_kv_t, normed_ref[...], preferred_element_type=F32)
    of_query_t = contract(d_query, normed_ref[past:, :], 0, 0)
    of_query, of_key, of_value = of_query_t.T, of_kv_t[:DH].T, of_kv_t[DH:].T
    mine = bits_ref[0] == 1
    for i, grad in enumerate((of_query, drel_t.T, of_key, of_value)):
        middle = grad.shape[0] // 2
        low, high = grad[:middle].astype(BF16), grad[middle:].astype(BF16)
        keep_ref[i] = jnp.where(mine, high, low)
        give_ref[i] = jnp.where(mine, low, high)
    own_rows = (
        contract(d_query, wq_ref[...], 1, 1)
        + contract(d_kv[:, :DH], wk_ref[...], 1, 1)
        + contract(d_kv[:, DH:], wv_ref[...], 1, 1)
    )
    wq = wq_ref[...].astype(F32)
    wk = wk_ref[...].astype(F32)
    wv = wv_ref[...].astype(F32)
    sums = jnp.sum(d_kv_t.astype(F32), 1, keepdims=True).T
    own_along = of_query * wq + of_key * wk + of_value * wv
    own_shift = (
        jnp.sum(d_query.astype(F32), 0, keepdims=True) * wq + sums[:, :DH] * wk + sums[:, DH:] * wv
    )

    @pl.when(head == 0)
    def _():
        rows_ref[...] = own_rows + rest[0][...] if with_sums else own_rows
        along_ref[...] = own_along
        shift_ref[...] = own_shift

    @pl.when(head > 0)
    def _():
        rows_ref[...] += own_rows
        along_ref[...] += own_along
        shift_ref[...] += own_shift


def attend_back(
    start,
    count,
    heads,
    bits,
    prob,
    d_attn,
    content,
    position,
    keys,
    values,
    w_rel,
    w_query,
    w_key,
    w_value,
    normed,
    table,
    cos,
    sin,
    sums=(),
    into=(),
    first=(),
):
    seg, width = content.shape
    total = keys.shape[0]
    block = seg
    column = lambda h: (0, start + h)
    rows = lambda h: (0, start + h)
    fixed = lambda h: (0, 0)
    whole = pl.BlockSpec(memory_space=pl.ANY)
    operands = [bits, prob, d_attn, content, position, keys, values, w_rel]
    operands += [w_query, w_key, w_value, normed, table, cos, sin]
    aliases = {}
    sum_specs = [
        pl.BlockSpec((seg, width), fixed),
        pl.BlockSpec((width, DH), fixed),
        pl.BlockSpec((width, DH), fixed),
    ]
    for i in range(len(sums)):
        aliases[len(operands) + i] = 2 + i
    operands += [*sums]
    for i in range(len(into)):
        aliases[len(operands) + i] = i
    operands += [*into, *first]
    half = jax.ShapeDtypeStruct(into[0].shape if into else (4, width // 2, len(heads) * DH), BF16)
    half_spec = pl.BlockSpec((4, width // 2, DH), lambda h: (0, 0, start - heads.start + h))
    return pl.pallas_call(
        functools.partial(attend_back_kernel, bool(sums)),
        grid=(count,),
        in_specs=[
            pl.BlockSpec(memory_space=pltpu.SMEM),
            pl.BlockSpec((1, block, total), lambda h: (start + h, 0, 0)),
            pl.BlockSpec((block, DH), rows),
            pl.BlockSpec((block, DH), rows),
            pl.BlockSpec((block, DH), rows),
            pl.BlockSpec((total, DH), column),
            pl.BlockSpec((total, DH), column),
            pl.BlockSpec((width, DH), column),
            pl.BlockSpec((width, DH), column),
            pl.BlockSpec((width, DH), column),
            pl.BlockSpec((width, DH), column),
            pl.BlockSpec(memory_space=pltpu.VMEM),
            pl.BlockSpec(memory_space=pltpu.VMEM),
            pl.BlockSpec(memory_space=pltpu.VMEM),
            pl.BlockSpec(memory_space=pltpu.VMEM),
        ]
        + sum_specs[: len(sums)]
        + [whole] * (len(into) + len(first)),
        out_specs=[half_spec, half_spec] + sum_specs + [pl.BlockSpec((2, DH), lambda h: (0, h))],
        out_shape=[
            half,
            half,
            jax.ShapeDtypeStruct((seg, width), F32),
            jax.ShapeDtypeStruct((width, DH), F32),
            jax.ShapeDtypeStruct((width, DH), F32),
            jax.ShapeDtypeStruct((2, count * DH), F32),
        ],
        input_output_aliases=aliases,
        compiler_params=pltpu.CompilerParams(vmem_limit_bytes=52 * MIB),
        cost_estimate=SHORT,
        name="attend_back",
    )(*operands)


def in_vmem():
    return pl.BlockSpec(memory_space=pltpu.VMEM)


def norm_kernel(count, owners_ref, *refs):
    parts, (gain_ref, shift_ref), (normed_ref, rows_ref) = refs[:count], refs[count : count + 2], refs[-2:]
    block = rows_ref.shape[1]
    for i, part in enumerate(parts):
        owner = owners_ref[i]
        for kind in range(3):
            low = part[kind * block : (kind + 1) * block]
            values = low.astype(F32)
            center = values - jnp.mean(values, -1, keepdims=True)
            spread = jnp.mean(center * center, -1, keepdims=True)
            normed = center * lax.rsqrt(spread + 1e-05) * gain_ref[...] + shift_ref[...]
            normed_ref[kind, owner] = normed.astype(BF16)
            if kind == 2:
                rows_ref[owner] = low


def norm_context(parts, owners, gain, shift, after=()):
    rows, width = parts[0].shape
    block = rows // 3
    normed, inputs = pl.pallas_call(
        functools.partial(norm_kernel, len(parts)),
        in_specs=[pl.BlockSpec(memory_space=pltpu.SMEM)] + [in_vmem()] * (len(parts) + 2)
        + [pl.BlockSpec(memory_space=pl.ANY)] * len(after),
        out_specs=[in_vmem(), in_vmem()],
        out_shape=[
            jax.ShapeDtypeStruct((3, len(parts), block, width), BF16),
            jax.ShapeDtypeStruct((len(parts), block, width), BF16),
        ],
        compiler_params=pltpu.CompilerParams(vmem_limit_bytes=48 * MIB),
        cost_estimate=SHORT,
        name="norm_context",
    )(owners, *parts, gain.reshape(1, -1), shift.reshape(1, -1), *after)
    return normed.reshape(-1, width), inputs.reshape(-1, width)


def place_kernel(count, owners_ref, *refs):
    for i, part in enumerate(refs[:count]):
        refs[-1][owners_ref[i]] = part[...]


def place_rows(parts, owners, after=()):
    rows, width = parts[0].shape
    return pl.pallas_call(
        functools.partial(place_kernel, len(parts)),
        in_specs=[pl.BlockSpec(memory_space=pltpu.SMEM)]
        + [in_vmem()] * len(parts)
        + [pl.BlockSpec(memory_space=pl.ANY)] * len(after),
        out_specs=in_vmem(),
        out_shape=jax.ShapeDtypeStruct((len(parts), rows, width), parts[0].dtype),
        cost_estimate=SHORT,
        name="place_rows",
    )(owners, *parts, *after)


def hold(values, *others):
    whole = pl.BlockSpec(memory_space=pl.ANY)
    return pl.pallas_call(
        lambda *refs: None,
        in_specs=[whole] * (len(values) + len(others)),
        out_specs=[whole] * len(values),
        out_shape=[jax.ShapeDtypeStruct(v.shape, v.dtype) for v in values],
        input_output_aliases={i: i for i in range(len(values))},
        cost_estimate=SHORT,
        name="hold",
    )(*values, *others)


def copy_kernel(rows_ref, *refs):
    refs[-1][...] = rows_ref[...]


def copy_after(rows, *others):
    return pl.pallas_call(
        copy_kernel,
        in_specs=[in_vmem()] + [pl.BlockSpec(memory_space=pl.ANY)] * len(others),
        out_specs=in_vmem(),
        out_shape=jax.ShapeDtypeStruct(rows.shape, rows.dtype),
        cost_estimate=SHORT,
        name="copy_after",
    )(rows, *others)


def out_grad_kernel(bits_ref, left_ref, right_ref, keep_ref, give_ref):
    mine = bits_ref[0] == 1
    grad = contract(left_ref[...], right_ref[...], 0, 0)
    middle, columns = keep_ref.shape[1:]
    for i in range(2):
        part = grad[:, i * columns : (i + 1) * columns]
        low, high = part[:middle].astype(BF16), part[middle:].astype(BF16)
        keep_ref[i] = jnp.where(mine, high, low)
        give_ref[i] = jnp.where(mine, low, high)


def out_grad(bits, left, right):
    width = right.shape[1]
    half = jax.ShapeDtypeStruct((6, width // 2, width // 2), BF16)
    spec = pl.BlockSpec((2, width // 2, width // 2), lambda i: (2, 0, 0))
    whole = pl.BlockSpec(left.shape, lambda i: (0, 0))
    return pl.pallas_call(
        out_grad_kernel,
        grid=(1,),
        in_specs=[pl.BlockSpec(memory_space=pltpu.SMEM), whole, whole],
        out_specs=[spec, spec],
        out_shape=[half, half],
        compiler_params=pltpu.CompilerParams(vmem_limit_bytes=48 * MIB),
        cost_estimate=SHORT,
        name="out_grad",
    )(bits, left, right)


def finish_kernel(bits_ref, own_ref, got_ref, *refs):
    outs = refs[-5:]
    own = pl.program_id(0) == bits_ref[0]

    def write(ref):
        for i in range(4):
            outs[i][...] = ref[i].astype(F32)
        if ref.shape[0] > 4:
            half = ref.shape[2]
            outs[4][:, :half] = ref[4].astype(F32)
            outs[4][:, half:] = ref[5].astype(F32)

    pl.when(own)(lambda: write(own_ref))
    pl.when(jnp.logical_not(own))(lambda: write(got_ref))


def finish(bits, column, columns, own, got, results):
    count, rows, width = own.shape
    fixed = pl.BlockSpec(own.shape, lambda i: (0, 0, 0))
    block = pl.BlockSpec((rows, width), lambda i: (i, column))
    last = pl.BlockSpec((rows, columns * width), lambda i: (i, 0))
    out = jax.ShapeDtypeStruct((2 * rows, columns * width), F32)
    if count == 4:
        out_specs, before = [block] * 4, results[:4]
    else:
        out_specs, before = [block] * 4 + [last], results
    sums = pl.pallas_call(
        finish_kernel if count > 4 else lambda *refs: finish_kernel(*refs, None),
        grid=(2,),
        in_specs=[pl.BlockSpec(memory_space=pltpu.SMEM), fixed, fixed]
        + [pl.BlockSpec(memory_space=pl.ANY)] * len(before),
        out_specs=out_specs,
        out_shape=[out] * len(out_specs),
        input_output_aliases={3 + i: i for i in range(len(before))},
        compiler_params=pltpu.CompilerParams(vmem_limit_bytes=48 * MIB),
        cost_estimate=SHORT,
        name="finish",
    )(bits, own, got, *before)
    return list(sums) + list(results[len(sums) :])


class Chain:
    def __init__(self, moves, keeps, gives):
        self.moves, self.keeps, self.gives = list(moves), keeps, gives
        self.join = False
        self.got = None


def parts_of(move):
    return len(move[1])


def split_rows(rows, pre):
    lead, count, columns = rows.shape
    return rows.reshape(lead, pre, 2, count // (2 * pre), columns)


def first_halves(rows, move):
    keeps, gives = [], []
    size = rows.shape[0] // parts_of(move)
    for i, (step, pre) in enumerate(move[1]):
        cells = split_rows(rows[i * size : (i + 1) * size], pre)
        bit = bit_of(*step)
        flat = (size, -1, rows.shape[2])
        keeps.append(pick(cells, bit, 2).reshape(flat))
        gives.append(pick(cells, 1 - bit, 2).reshape(flat))
    return keeps, gives


def round_of(chains, bits, bit_names, after=(), through=()):
    operands, plans, out_shape = [], [], []
    for chain in chains:
        kind, cuts = chain.moves.pop(0)
        nexts = chain.moves[0] if chain.moves else None
        got = chain.got or [[swap(give, *step)] for give, (step, _) in zip(chain.gives, cuts)]
        chain.got = None
        held = chain.keeps if kind == "halve" else chain.gives
        leads, columns = [h.shape[0] for h in held], held[0].shape[2]
        total = sum(leads)
        next_kind, next_cuts = nexts if nexts else ("end", [None])
        size = total // len(next_cuts)
        ins, views = [], []
        for i, (h, g) in enumerate(zip(held, got)):
            base = sum(leads[:i])
            if kind == "double":
                cells = max(pre for _, pre in cuts)
                view = (h.shape[0], cells, h.shape[1] // cells, columns)
                bit = (bit_names.index(cuts[i][0]), cuts[i][1])
            elif next_kind == "halve":
                cells = max([2 * pre for _, pre in next_cuts] + [len(g) for g in got])
                view = (h.shape[0], cells, h.shape[1] // cells, columns)
                bit = None
            else:
                view = h.shape
                bit = None
            ins.append((len(operands), base, bit, view, len(g)))
            operands += [h.reshape(view)]
            operands += [r.reshape(view[0], -1, *view[2:]) if len(g) > 1 else r.reshape(view) for r in g]
        rows = held[0].shape[1]
        outs = []
        for j, cut in enumerate(next_cuts):
            if next_kind == "halve":
                cells = ins[0][3][1]
                shape = (size, cells // 2, rows // cells, columns)
                outs.append((len(out_shape), bit_names.index(cut[0]), cut[1]))
                out_shape += [jax.ShapeDtypeStruct(shape, BF16)] * 2
            else:
                if kind == "double":
                    cells = ins[0][3][1]
                    shape = (size, cells * 2, rows // cells, columns)
                    if chain.join and next_kind == "end":
                        shape = (1, cells * 2, rows // cells, size * columns)
                else:
                    shape = (size, rows, columns)
                outs.append((len(out_shape), None, None))
                out_shape += [jax.ShapeDtypeStruct(shape, held[0].dtype)]
        plans.append((kind, next_kind, size, ins, outs))

    def kernel(bits_ref, *refs):
        inputs, results = refs[: len(operands)], refs[len(refs) - len(out_shape) - len(through) :]
        for kind, next_kind, size, ins, outs in plans:
            for at, base, bit, view, count in ins:
                held_ref, got_ref = inputs[at], inputs[at + 1]
                got_refs = inputs[at + 1 : at + 1 + count]
                for i in range(view[0]):
                    where, which = divmod(base + i, size)
                    out, out_bit, out_pre = outs[where]
                    if kind == "double":
                        mine = bits_ref[bit[0]]
                        run = view[1] // bit[1]
                        for cell in range(view[1]):
                            for side, ref in ((mine, held_ref), (1 - mine, got_ref)):
                                place = (cell // run * 2 + side) * run + cell % run
                                if results[out].shape[3] == ref.shape[3]:
                                    results[out][which, place] = ref[i, cell]
                                else:
                                    wide = slice(which * ref.shape[3], (which + 1) * ref.shape[3])
                                    results[out][0, place, :, wide] = ref[i, cell]
                    elif next_kind == "halve":
                        mine = bits_ref[out_bit]
                        run = view[1] // (2 * out_pre)
                        for cell in range(view[1] // 2):
                            if count > 1:
                                sums = []
                                for side in range(2):
                                    place = (cell // run * 2 + side) * run + cell % run
                                    piece, rest = divmod(place * count, view[1])
                                    more = got_refs[piece][i, rest // count].astype(F32)
                                    sums.append(held_ref[i, place].astype(F32) + more)
                                high = mine == 1
                                results[out][which, cell] = jnp.where(high, sums[1], sums[0]).astype(BF16)
                                results[out + 1][which, cell] = jnp.where(high, *sums).astype(BF16)
                                continue
                            for side, slot in ((mine, out), (1 - mine, out + 1)):
                                place = (cell // run * 2 + side) * run + cell % run
                                results[slot][which, cell] = (
                                    held_ref[i, place].astype(F32) + got_ref[i, place].astype(F32)
                                ).astype(BF16)
                    else:
                        results[out][which] = (held_ref[i].astype(F32) + got_ref[i].astype(F32)).astype(
                            results[out].dtype
                        )

    in_vmem = pl.BlockSpec(memory_space=pltpu.VMEM)
    results = pl.pallas_call(
        kernel,
        in_specs=[pl.BlockSpec(memory_space=pltpu.SMEM)]
        + [in_vmem] * len(operands)
        + [pl.BlockSpec(memory_space=pl.ANY)] * (len(through) + len(after)),
        out_specs=[in_vmem] * len(out_shape) + [pl.BlockSpec(memory_space=pl.ANY)] * len(through),
        out_shape=out_shape + [jax.ShapeDtypeStruct(r.shape, r.dtype) for r in through],
        input_output_aliases={
            1 + len(operands) + i: len(out_shape) + i for i in range(len(through))
        },
        compiler_params=pltpu.CompilerParams(vmem_limit_bytes=48 * MIB),
        cost_estimate=SHORT,
        name="add_and_split",
    )(bits, *operands, *through, *after)
    for chain, (kind, next_kind, size, ins, outs) in zip(chains, plans):
        flat = lambda r: r.reshape(r.shape[0], -1, r.shape[-1])
        if next_kind == "halve":
            chain.keeps = [flat(results[o]) for o, _, _ in outs]
            chain.gives = [flat(results[o + 1]) for o, _, _ in outs]
        else:
            chain.keeps = []
            chain.gives = [flat(results[o]) for o, _, _ in outs]
    return results[len(out_shape) :]


def input_grad_kernel(targets_ref, d_rows_ref, x_ref, d_hidden_ref, gain_ref, *outs):
    block = outs[0].shape[0]
    for i, out in enumerate(outs):
        at = pl.ds(pl.multiple_of(targets_ref[i] * block, block), block)
        values = x_ref[at, :].astype(F32)
        center = values - jnp.mean(values, -1, keepdims=True)
        spread = jnp.mean(center * center, -1, keepdims=True)
        inverse = lax.rsqrt(spread + 1e-05)
        unit = center * inverse
        grad = d_rows_ref[at, :] * gain_ref[...]
        mean = jnp.mean(grad, -1, keepdims=True)
        along = jnp.mean(grad * unit, -1, keepdims=True)
        out[...] = (d_hidden_ref[at, :] + inverse * (grad - mean - unit * along)).astype(BF16)


def input_grad(targets, d_rows, rows, d_hidden, gain, count):
    block = jax.ShapeDtypeStruct((rows.shape[0] // count, rows.shape[1]), BF16)
    return pl.pallas_call(
        input_grad_kernel,
        in_specs=[pl.BlockSpec(memory_space=pltpu.SMEM)] + [in_vmem()] * 4,
        out_specs=[in_vmem()] * count,
        out_shape=[block] * count,
        compiler_params=pltpu.CompilerParams(vmem_limit_bytes=48 * MIB),
        cost_estimate=SHORT,
        name="input_grad",
    )(targets, d_rows, rows, d_hidden, gain.reshape(1, -1))


def widen_kernel(rows_ref, out_ref):
    out_ref[...] = rows_ref[...].astype(F32)


def widen_flip_kernel(rows_ref, out_ref):
    out_ref[...] = rows_ref[...].astype(F32).T


def widen(rows, flip=False):
    count, width = rows.shape
    block = count // 4
    out = pl.BlockSpec((width, block), lambda i: (0, i)) if flip else pl.BlockSpec((block, width), lambda i: (i, 0))
    return pl.pallas_call(
        widen_flip_kernel if flip else widen_kernel,
        grid=(4,),
        in_specs=[pl.BlockSpec((block, width), lambda i: (i, 0))],
        out_specs=out,
        out_shape=jax.ShapeDtypeStruct((width, count) if flip else (count, width), F32),
        compiler_params=pltpu.CompilerParams(vmem_limit_bytes=48 * MIB),
        cost_estimate=SHORT,
        name="widen",
    )(rows)


def compress_kernel(mem_ref, gc_ref, w_ref, bias_ref, new_ref, grad_ref, wide_ref, sum_ref):
    stream = pl.program_id(0)
    count = gc_ref.shape[1]
    rows = mem_ref.shape[1]
    blocks, depth, lanes = wide_ref.shape
    for i in range(blocks):
        wide_ref[i, :rows] = mem_ref[0, :, i * lanes : (i + 1) * lanes].astype(F32)
        wide_ref[i, rows:] = jnp.zeros((depth - rows, lanes), F32)
    made = jnp.zeros((count, gc_ref.shape[2]), F32) + bias_ref[...]
    for tap in range(RATE):
        taken = [wide_ref[i, pl.ds(tap, count, stride=RATE), :] for i in range(blocks)]
        window = jnp.concatenate(taken, 1).astype(BF16)
        made = made + jnp.dot(window, w_ref[tap], preferred_element_type=F32)
        part = contract(window, gc_ref[0], 0, 0)
        sum_ref[tap] = jnp.where(stream == 0, part, part + sum_ref[tap])
    new_ref[0] = made.astype(BF16)

    @pl.when(stream == pl.num_programs(0) - 1)
    def _():
        grad_ref[...] = sum_ref[...].astype(BF16)


def compress_rows(memory, grad, weights, bias):
    streams, rows, width = memory.shape
    count, columns = grad.shape[1:]
    return pl.pallas_call(
        compress_kernel,
        grid=(streams,),
        in_specs=[
            pl.BlockSpec((1, rows, width), lambda i: (i, 0, 0)),
            pl.BlockSpec((1, count, columns), lambda i: (i, 0, 0)),
            pl.BlockSpec(weights.shape, lambda i: (0, 0, 0)),
            pl.BlockSpec((1, columns), lambda i: (0, 0)),
        ],
        out_specs=[
            pl.BlockSpec((1, count, columns), lambda i: (i, 0, 0)),
            pl.BlockSpec(weights.shape, lambda i: (0, 0, 0)),
        ],
        out_shape=[
            jax.ShapeDtypeStruct((streams, count, columns), BF16),
            jax.ShapeDtypeStruct(weights.shape, BF16),
        ],
        scratch_shapes=[
            pltpu.VMEM((width // DH, RATE * count + 16, DH), F32),
            pltpu.VMEM(weights.shape, F32),
        ],
        compiler_params=pltpu.CompilerParams(vmem_limit_bytes=48 * MIB),
        cost_estimate=SHORT,
        name="compress_rows",
    )(memory, grad, weights, bias.reshape(1, -1))


def own_streams_plan(
    inputs,
    memory,
    compressed,
    seg_len,
    gain_first,
    shift_first,
    w_query,
    w_key,
    w_value,
    w_rel,
    bias_content,
    bias_position,
    w_out,
    gain_second,
    shift_second,
    w_up,
    bias_up,
    w_down,
    bias_down,
    w_comp,
    comp_bias,
    grad_out,
    grad_comp,
):
    seq_parts = lax.axis_size("seq")
    dp_parts = lax.axis_size("dp")
    me = lax.axis_index("seq")
    seg_dev, streams, width = inputs.shape
    seg = seg_dev * seq_parts
    split = CMEM + MEM
    hidden_dev = w_down.shape[0]

    core = ("dp", 1)
    wide = [("dp", d) for d in reversed(bits_below(dp_parts)[1:])]
    line = [("seq", d) for d in bits_below(seq_parts)]
    there = list(range(len(wide)))
    back = there[::-1]
    core_bit = bit_of(*core)

    bit_names = [core] + wide + line
    bits = jnp.stack([bit_of(*name) for name in bit_names]).astype(jnp.int32)
    wide_in = [[(wide[i], 1), (wide[j], 1 << j)] for i, j in zip(there, back)]
    line_in = [[(step, 1 << i)] for i, step in enumerate(reversed(line))][::-1]
    core_cut, line_cuts, wide_cuts = [(core, 1)], [[(s, 1)] for s in line], [[(s, 1)] for s in wide]

    def moves_of(cuts, collected):
        return [("halve", c) for c in cuts] + [("double", c) for c in reversed(collected)]

    piece = hidden_dev // dp_parts
    place = lax.axis_index("dp")

    def gathered(rows):
        rows = jnp.swapaxes(rows.reshape(piece, 2, width // 2), 0, 1)
        chain = Chain(moves_of([], wide_in + line_in), [], [rows])
        chain.join = True
        return chain

    up_piece = lax.dynamic_slice_in_dim(w_up, place * piece, piece, 1).T
    up_chain = gathered(up_piece)
    round_of([up_chain], bits, bit_names)
    for step in line[:-1]:
        round_of([up_chain], bits, bit_names)
    order_two = token(up_chain.gives[0])

    key_cos, key_sin = sinusoids(jnp.arange(split + seg, dtype=jnp.int32))
    table = jnp.concatenate([key_cos, key_sin], -1).astype(BF16)
    cos, sin = key_cos[split:], key_sin[split:]

    owners = jnp.stack([(me - shift) % seq_parts for shift in range(seq_parts)]).astype(jnp.int32)

    def send(parts):
        return [parts[0]] + [
            lax.ppermute(part, "seq", [(i, (i + shift) % seq_parts) for i in range(seq_parts)])
            for shift, part in enumerate(parts)
            if shift
        ]

    def parts_for(rows, order=0):
        return [pick(rows, (me + shift) % seq_parts + order, 0) for shift in range(seq_parts)]

    def from_streams(parts):
        return by_stream(place_rows(send(parts), owners))

    blocks = [by_stream(rows) for rows in (compressed, memory, inputs)]
    parts = send(parts_for(jnp.concatenate(blocks, 1)))
    down_piece = lax.dynamic_slice_in_dim(w_down, place * piece + order_two, piece, 0)
    down_chain = gathered(down_piece)
    go_parts = parts_for(by_stream(grad_out))
    memory_rows = by_stream(memory)
    idle = [*up_chain.gives, *down_chain.gives, table, cos, sin, *go_parts, memory_rows]
    normed, x_rows = norm_context(parts, owners, gain_first, shift_first, idle)
    length = lax.dynamic_slice_in_dim(seg_len, me, 1)
    round_of([up_chain], bits, bit_names, [normed])
    order = token(normed)
    bias_all = lax.dynamic_slice_in_dim(bias_up.reshape(-1, 2, piece), core_bit + order, 1, 1)
    bias_all = bias_all.reshape(1, -1)

    seg_normed = normed[split:]
    queries = jnp.dot(seg_normed, w_query, preferred_element_type=F32)
    keys = jnp.dot(normed, w_key, preferred_element_type=F32).astype(BF16)
    values = jnp.dot(normed, w_value, preferred_element_type=F32).astype(BF16)
    content = (queries + bias_content).astype(BF16)
    position = (queries + bias_position).astype(BF16)
    given = (length, content, position, keys, values, w_rel, table, cos, sin)
    round_of([down_chain], bits, bit_names, [normed])
    round_of([down_chain], bits, bit_names, [values])
    memory_rows = copy_after(memory_rows, down_chain.gives[0])
    memory_all = lax.all_gather(memory_rows, "seq", axis=1, tiled=True)
    prob, attn_out = attend(range(H // 2), *given, first=down_chain.gives)
    prob, attn_out = round_of([up_chain, down_chain], bits, bit_names, [], [prob, attn_out])
    while up_chain.moves:
        round_of([up_chain], bits, bit_names, [attn_out])
    up_half = up_chain.gives[0][0]
    bias_all = double(bias_all, line[-1], 0)
    prob, attn_out = attend(
        range(H // 2, H), *given, first=down_chain.gives + [bias_all], into=[prob, attn_out]
    )
    (attn_out,) = round_of([down_chain], bits, bit_names, [], [attn_out])
    while down_chain.moves:
        round_of([down_chain], bits, bit_names)
    down_half = down_chain.gives[0][0]
    for i, step in enumerate(line[-2::-1]):
        bias_all = double(bias_all, step, i + 1)
    bias_half = jnp.swapaxes(bias_all.reshape(seq_parts, -1, piece), 0, 1).reshape(-1).astype(F32)
    x_f = x_rows.astype(F32)
    hidden = x_f + jnp.dot(attn_out, w_out, preferred_element_type=F32)
    normed_two = layer_norm(hidden, gain_second, shift_second).astype(BF16)

    pair_normed = double(normed_two, core).reshape(-1, width)
    pre_act = contract(pair_normed, up_half, 1, 1) + bias_half
    activated = gelu_tanh(pre_act).astype(BF16)
    go_rows = place_rows(send(go_parts), owners, [activated, memory_all]).reshape(seg, width)
    pair_grad = double(go_rows, core).reshape(-1, width)
    ffn_rows = jnp.dot(activated, down_half, preferred_element_type=F32)
    ffn_rows = halve(ffn_rows.reshape(2, seg, width), core)
    output = (hidden + ffn_rows + bias_down).astype(BF16)
    output_parts = parts_for(output.reshape(seq_parts, seg_dev, width))
    groups_of = [list(range(c, dp_parts, 2)) for c in range(2)]

    def over_rows(grad):
        return lax.psum_scatter(grad, "dp", axis_index_groups=groups_of, tiled=True)

    down_sum = over_rows(contract(activated, pair_grad, 0, 0).astype(BF16))
    d_activated = contract(pair_grad, down_half, 1, 1)
    _, gelu_back = jax.vjp(gelu_tanh, pre_act)
    d_pre = gelu_back(d_activated)[0].astype(BF16)
    d_normed_two = jnp.dot(d_pre, up_half, preferred_element_type=F32)
    d_normed_two = halve(d_normed_two.reshape(2, seg, width), core)
    up_sum = over_rows(contract(d_pre, pair_normed, 0, 0).astype(BF16))
    grad_bias_half = jnp.sum(d_pre.astype(F32), 0)

    go_f = go_rows.astype(F32)
    _, norm_two_back = jax.vjp(layer_norm, hidden, gain_second, shift_second)
    d_hidden_ffn, grad_gain_second, grad_shift_second = norm_two_back(d_normed_two)
    d_hidden = go_f + d_hidden_ffn
    grad_bias_down = jnp.sum(go_f, 0)
    d_branch = d_hidden.astype(BF16)
    d_attn = contract(d_branch, w_out, 1, 1).astype(BF16)

    half_heads = H // 2
    group_moves = moves_of([core_cut] + wide_in + line_cuts, [core_cut] + wide_in + line_cuts)
    groups, biases, head_sums = [], [], []
    output_rows = send(output_parts)

    first, start, alongs, shifts = [], 0, [], []
    for call, heads in enumerate(CALLS):
        base = start // half_heads * half_heads
        group_heads = range(base, base + half_heads)
        if start == 0:
            halves = out_grad(bits, attn_out, d_branch)
        elif start == base:
            halves = []
        *halves, d_rows, along, shift_part, bias_part = attend_back(
            start, heads, group_heads, bits, prob, d_attn, content, position, keys, values,
            w_rel, w_query, w_key, w_value, normed, table, cos, sin, head_sums, halves, first,
        )
        start += heads
        passing = [*halves, d_rows, along, shift_part, bias_part]
        if call == 0:
            down_sum, *passing = hold([down_sum, *passing])
            down_sum = lax.psum_scatter(down_sum, "seq", tiled=True)
            first = output_parts[1:]
        elif call == 1:
            output_rows = place_rows(output_rows, owners, [bias_part])
            up_sum, *passing = hold([up_sum, *passing], output_rows)
            up_sum = lax.psum_scatter(up_sum, "seq", tiled=True)
            first = []
        elif call == 2:
            passing = round_of(groups, bits, bit_names, [], passing)
            first = [g for c in groups for g in c.gives]
        else:
            down_sum, *passing = round_of(groups, bits, bit_names, [], [down_sum, *passing])
            down_sum = lax.all_gather(down_sum, "dp", tiled=True)
        *halves, d_rows, along, shift_part, bias_part = passing
        head_sums = [d_rows]
        alongs.append(along)
        shifts.append(shift_part)
        biases.append(bias_part)
        if start == group_heads.stop:
            groups.append(Chain(group_moves, [halves[0]], [halves[1]]))
            first += [halves[1]]
    output = by_stream(output_rows)

    def compress(memory_all):
        new_rows = grad_comp.shape[0]
        padded = jnp.pad(by_stream(grad_comp), ((0, 0), (0, -new_rows % 16), (0, 0)))
        made, grad = compress_rows(memory_all, padded, w_comp, comp_bias)
        grad = grad.reshape(1, -1, grad.shape[2])
        moves = moves_of([core_cut] + wide_cuts, [core_cut] + wide_cuts)
        return by_stream(made)[:new_rows], Chain(moves, *first_halves(grad, moves[0]))

    grad_comp_bias = jnp.sum(grad_comp.astype(F32), (0, 1))
    targets = jnp.stack([(me + shift) % seq_parts for shift in range(seq_parts)]).astype(jnp.int32)
    input_parts = input_grad(targets, d_rows, x_rows, d_hidden, gain_first, seq_parts)
    input_rows = send(input_parts)

    grad_shift_first = jnp.sum(sum(shifts), 1)
    grad_gain_first = (jnp.sum(sum(alongs), 1) - shift_first * grad_shift_first) / gain_first
    vectors = jnp.concatenate(
        [
            jnp.concatenate(biases, 1).reshape(-1),
            grad_gain_first,
            grad_shift_first,
            grad_gain_second,
            grad_shift_second,
            grad_bias_down,
        ]
    )
    count = vectors.shape[0]
    hidden_sums = jnp.zeros((2, grad_bias_half.shape[0]), F32)
    hidden_sums = lax.dynamic_update_slice(hidden_sums, grad_bias_half[None], (core_bit, 0))
    comp_sums = jnp.zeros((seq_parts, grad_comp_bias.shape[0]), F32)
    comp_sums = lax.dynamic_update_slice(comp_sums, grad_comp_bias[None], (me, 0))
    vectors = jnp.concatenate([vectors, hidden_sums.reshape(-1), comp_sums.reshape(-1)])
    vector = Chain([("add", [(name, 1)]) for name in bit_names], [], [vectors.reshape(1, -1, DH)])

    one, two = groups
    def finished(column, group, results):
        own = group.gives[0]
        return finish(bits, column, len(groups), own, swap(own, *core), results)

    turn, results = 0, []
    pinned = {
        1: input_parts,
        2: [input_rows[1]],
        6: [input_rows[-1]],
        7: [*input_rows[2:-1]],
    }
    comp = None
    while len(two.moves) > 1 or vector.moves:
        active = [one, two] + [comp] * (turn > 1) + [vector] * (turn > 2)
        active = [c for c in active if len(c.moves) > (c in groups)]
        fence = pinned.get(turn, [])
        if turn == 8:
            results = finished(0, one, results)
            grad_w_comp = widen(comp.gives[0][0]).reshape(w_comp.shape)
            grad_inputs = by_stream(place_rows(input_rows, owners))
            fence = [*fence, *results, grad_w_comp, grad_inputs]
        through = [up_sum, memory_all] if turn == 0 else []
        through = round_of(active, bits, bit_names, fence, through)
        if turn == 0:
            up_sum = lax.all_gather(through[0], "dp", tiled=True)
            new_compressed, comp = compress(through[1])
            pinned[2] = [*pinned[2], new_compressed]
            pinned[3] = [output]
            grad_w_down, grad_w_up = widen(down_sum), widen(up_sum, True)
            pinned[4] = [grad_w_down]
            pinned[5] = [grad_w_up]
        turn += 1
    vectors = vector.gives[0].reshape(-1)

    results = finished(1, two, results)
    grad_w_query, grad_w_rel, grad_w_key, grad_w_value, grad_w_out = results

    totals = vectors[:count].reshape(-1, width)
    hidden_sums = vectors[count : count + hidden_sums.size].reshape(
        [2, 1 << len(wide)] + [2] * len(line) + [piece]
    )
    for step in reversed(line):
        hidden_sums = pick(hidden_sums, bit_of(*step), 2)
    grad_bias_up = jnp.swapaxes(hidden_sums, 0, 1).reshape(-1)
    comp_sums = vectors[count + grad_bias_half.size * 2 :].reshape(comp_sums.shape)
    grad_comp_bias = pick(comp_sums, me, 0)

    return (
        output,
        grad_inputs,
        new_compressed,
        totals[2],
        totals[3],
        grad_w_query,
        grad_w_key,
        grad_w_value,
        grad_w_rel,
        totals[0],
        totals[1],
        grad_w_out,
        totals[4],
        totals[5],
        grad_w_up,
        grad_bias_up,
        grad_w_down,
        totals[6],
        grad_w_comp,
        grad_comp_bias,
    )


def on_device(*arrays):
    streams = arrays[0].shape[1]
    dp_parts, seq_parts = lax.axis_size("dp"), lax.axis_size("seq")
    fits = streams == seq_parts and seq_parts > 1 and dp_parts >= 4
    powers = (seq_parts & (seq_parts - 1)) == 0 and (dp_parts & (dp_parts - 1)) == 0
    plan = own_streams_plan if fits and powers else split_rows_plan
    return plan(*arrays)


def solution(mesh):
    in_specs = (
        P("seq", "dp", None),
        P("seq", "dp", None),
        P("seq", "dp", None),
        P("dp"),
        P(),
        P(),
        P(),
        P(),
        P(),
        P(),
        P(),
        P(),
        P(),
        P(),
        P(),
        P(None, "seq"),
        P("seq"),
        P("seq", None),
        P(),
        P(None, None, "seq"),
        P("seq"),
        P("seq", "dp", None),
        P(None, "dp", "seq"),
    )
    out_specs = (
        P("seq", "dp", None),
        P("seq", "dp", None),
        P(None, "dp", "seq"),
        P(),
        P(),
        P(),
        P(),
        P(),
        P(),
        P(),
        P(),
        P(),
        P(),
        P(),
        P(None, "seq"),
        P("seq"),
        P("seq", None),
        P(),
        P(None, None, "seq"),
        P("seq"),
    )
    return jax.shard_map(
        on_device, mesh=mesh, in_specs=in_specs, out_specs=out_specs, check_vma=False
    )
```

```python
import functools
import math

import jax
import jax.numpy as jnp
from jax import lax
from jax.experimental import pallas as pl
from jax.experimental.pallas import tpu as pltpu
from jax.sharding import PartitionSpec as P

D = 1024
H = 8
DH = 128
MEM = 512
CMEM = 512
RATE = 3


def layer_norm(values, gain, shift):
    center = values - jnp.mean(values, -1, keepdims=True)
    spread = jnp.mean(center * center, -1, keepdims=True)
    return center * lax.rsqrt(spread + 1e-05) * gain + shift


def gelu_tanh(values):
    return jax.nn.gelu(values, approximate=True)


def sinusoids(positions):
    half_width = D // 2
    frequency = jnp.exp(jnp.arange(half_width, dtype=jnp.float32) * (-2.0 * math.log(10000.0) / D))
    angles = positions.astype(jnp.float32)[:, None] * frequency[None, :]
    return (jnp.cos(angles), jnp.sin(angles))


def key_positions(seq_parts, cmem_dev, mem_dev, seg_dev):
    ctx_dev = cmem_dev + mem_dev + seg_dev
    row_ids = jnp.arange(ctx_dev * seq_parts, dtype=jnp.int32)
    device_ids = row_ids // ctx_dev
    local_ids = row_ids % ctx_dev
    in_cmem = device_ids * cmem_dev + local_ids
    in_mem = CMEM + device_ids * mem_dev + (local_ids - cmem_dev)
    in_seg = CMEM + MEM + device_ids * seg_dev + (local_ids - cmem_dev - mem_dev)
    return jnp.where(
        local_ids < cmem_dev, in_cmem, jnp.where(local_ids < cmem_dev + mem_dev, in_mem, in_seg)
    )


def rotate_rows(position_rows, rel_heads, row_sin, row_cos, half_width):
    mixed = jnp.einsum(
        "qshd,fhd->qshf", position_rows, rel_heads, preferred_element_type=jnp.float32
    )
    first_half = mixed[..., :half_width]
    second_half = mixed[..., half_width:]
    return jnp.concatenate(
        [
            first_half * row_sin + second_half * row_cos,
            second_half * row_sin - first_half * row_cos,
        ],
        -1,
    ).astype(jnp.bfloat16)


def split_rows_plan(
    inputs,
    memory,
    compressed,
    seg_len,
    gain_first,
    shift_first,
    w_query,
    w_key,
    w_value,
    w_rel,
    bias_content,
    bias_position,
    w_out,
    gain_second,
    shift_second,
    w_up,
    bias_up,
    w_down,
    bias_down,
    w_comp,
    comp_bias,
    grad_out,
    grad_comp,
):
    seq_parts = lax.axis_size("seq")
    my_index = lax.axis_index("seq")
    seg_dev, streams, model_width = inputs.shape
    mem_dev = memory.shape[0]
    cmem_dev = compressed.shape[0]
    split_at = cmem_dev + mem_dev
    ctx_dev = split_at + seg_dev
    total_keys = ctx_dev * seq_parts
    half_width = model_width // 2
    score_scale = 1.0 / math.sqrt(DH)
    key_pos = key_positions(seq_parts, cmem_dev, mem_dev, seg_dev)
    key_cos, key_sin = sinusoids(key_pos)
    pos_table = jnp.concatenate([key_cos, key_sin], -1).astype(jnp.bfloat16)
    query_rows = my_index * seg_dev + jnp.arange(seg_dev, dtype=jnp.int32)
    query_cos, query_sin = sinusoids(CMEM + MEM + query_rows)
    query_cos = query_cos[:, None, None, :]
    query_sin = query_sin[:, None, None, :]
    key_seg = key_pos - (CMEM + MEM)
    visible = (key_seg[None, None, :] < 0) | (
        key_seg[None, None, :] <= query_rows[None, :, None]
    ) & (key_seg[None, None, :] < seg_len[:, None, None])
    x_in = inputs.astype(jnp.float32)
    context = jnp.concatenate([compressed, memory, inputs], 0).astype(jnp.float32)
    normed = layer_norm(context, gain_first, shift_first)
    normed_low = normed.astype(jnp.bfloat16)
    seg_normed = normed_low[split_at:]
    queries = jnp.dot(seg_normed, w_query, preferred_element_type=jnp.float32)
    keys_low = jnp.dot(normed_low, w_key, preferred_element_type=jnp.float32).astype(jnp.bfloat16)
    values_low = jnp.dot(normed_low, w_value, preferred_element_type=jnp.float32).astype(
        jnp.bfloat16
    )
    query_content = (queries + bias_content).astype(jnp.bfloat16).reshape(seg_dev, streams, H, DH)
    query_position = (queries + bias_position).astype(jnp.bfloat16).reshape(seg_dev, streams, H, DH)
    rel_heads = w_rel.reshape(model_width, H, DH)
    rotated = rotate_rows(query_position, rel_heads, query_sin, query_cos, half_width)
    keys_all, values_all, memory_all = (
        lax.all_gather(keys_low, "seq", axis=0, tiled=True),
        lax.all_gather(values_low, "seq", axis=0, tiled=True),
        lax.all_gather(memory, "seq", axis=0, tiled=True),
    )

    def scores_of(keys_gathered):
        content = jnp.einsum(
            "qshd,kshd->shqk",
            query_content,
            keys_gathered.reshape(total_keys, streams, H, DH),
            preferred_element_type=jnp.float32,
        )
        placed = jnp.einsum("qshf,kf->shqk", rotated, pos_table, preferred_element_type=jnp.float32)
        return jnp.where(visible[:, None], (content + placed) * score_scale, -1e30)

    scores = scores_of(keys_all)
    row_max = jnp.max(scores, -1, keepdims=True)
    exp_scores = jnp.exp(scores - row_max)
    row_total = jnp.sum(exp_scores, -1, keepdims=True)
    attn_prob = (exp_scores / row_total).astype(jnp.bfloat16)
    log_total = row_max + jnp.log(row_total)
    attended = jnp.einsum(
        "shqk,kshd->qshd",
        attn_prob,
        values_all.reshape(total_keys, streams, H, DH),
        preferred_element_type=jnp.float32,
    )
    attn_out = attended.reshape(seg_dev, streams, model_width).astype(jnp.bfloat16)
    hidden = x_in + jnp.dot(attn_out, w_out, preferred_element_type=jnp.float32)
    normed_two = layer_norm(hidden, gain_second, shift_second).astype(jnp.bfloat16)
    normed_all = lax.all_gather(normed_two, "seq", axis=0, tiled=True)
    pre_act = jnp.dot(normed_all, w_up, preferred_element_type=jnp.float32) + bias_up.astype(
        jnp.float32
    )
    activated = gelu_tanh(pre_act).astype(jnp.bfloat16)
    row_piece = activated
    ffn_result = lax.psum_scatter(
        jnp.dot(row_piece, w_down, preferred_element_type=jnp.float32).astype(jnp.bfloat16),
        "seq",
        scatter_dimension=0,
        tiled=True,
    ).astype(jnp.float32)
    output = (hidden + ffn_result + bias_down).astype(jnp.bfloat16)
    grad_all = lax.all_gather(grad_out, "seq", axis=0, tiled=True)
    d_activated = jnp.einsum("rsd,fd->rsf", grad_all, w_down, preferred_element_type=jnp.float32)
    _, gelu_back = jax.vjp(gelu_tanh, pre_act)
    d_pre = gelu_back(d_activated)[0].astype(jnp.bfloat16)
    grad_w_down = jnp.einsum("rsf,rsd->fd", activated, grad_all, preferred_element_type=jnp.float32)
    grad_w_up = jnp.einsum("rsd,rsf->df", normed_all, d_pre, preferred_element_type=jnp.float32)
    grad_bias_up = jnp.sum(d_pre.astype(jnp.float32), (0, 1))
    row_piece = d_pre
    d_normed_two = lax.psum_scatter(
        jnp.einsum("rsf,df->rsd", row_piece, w_up, preferred_element_type=jnp.float32).astype(
            jnp.bfloat16
        ),
        "seq",
        scatter_dimension=0,
        tiled=True,
    ).astype(jnp.float32)
    _, norm_two_back = jax.vjp(layer_norm, hidden, gain_second, shift_second)
    d_hidden_ffn, grad_gain_second, grad_shift_second = norm_two_back(d_normed_two)
    grad_rows_f = grad_out.astype(jnp.float32)
    d_hidden = grad_rows_f + d_hidden_ffn
    grad_bias_down = jnp.sum(grad_rows_f, (0, 1))
    d_branch = d_hidden.astype(jnp.bfloat16)
    grad_w_out = jnp.einsum("rsd,rse->de", attn_out, d_branch, preferred_element_type=jnp.float32)
    d_attn = (
        jnp.einsum("rse,de->rsd", d_branch, w_out, preferred_element_type=jnp.float32)
        .astype(jnp.bfloat16)
        .reshape(seg_dev, streams, H, DH)
    )
    keys_back, values_back = (
        lax.all_gather(keys_low, "seq", axis=0, tiled=True),
        lax.all_gather(values_low, "seq", axis=0, tiled=True),
    )
    keys_heads = keys_back.reshape(total_keys, streams, H, DH)
    values_heads = values_back.reshape(total_keys, streams, H, DH)
    prob_full = jnp.exp(scores_of(keys_back) - log_total)
    prob_low = prob_full.astype(jnp.bfloat16)
    d_prob = jnp.einsum("qshd,kshd->shqk", d_attn, values_heads, preferred_element_type=jnp.float32)
    inner_sum = jnp.sum(d_prob * prob_full, -1, keepdims=True)
    d_scores = (prob_full * (d_prob - inner_sum)).astype(jnp.bfloat16)
    key_part = (
        jnp.einsum("shqk,qshd->kshd", d_scores, query_content, preferred_element_type=jnp.float32)
        * score_scale
    )
    value_part = jnp.einsum("shqk,qshd->kshd", prob_low, d_attn, preferred_element_type=jnp.float32)
    key_sums = lax.psum_scatter(
        jnp.concatenate(
            [
                key_part.reshape(ctx_dev * lax.axis_size("seq"), streams, model_width),
                value_part.reshape(ctx_dev * lax.axis_size("seq"), streams, model_width),
            ],
            -1,
        ).astype(jnp.bfloat16),
        "seq",
        scatter_dimension=0,
        tiled=True,
    ).astype(jnp.float32)
    d_keys = key_sums[..., :model_width].astype(jnp.bfloat16)
    d_values = key_sums[..., model_width:].astype(jnp.bfloat16)
    d_content = (
        jnp.einsum("shqk,kshd->qshd", d_scores, keys_heads, preferred_element_type=jnp.float32)
        * score_scale
    )
    d_rotated = (
        jnp.einsum("shqk,kf->qshf", d_scores, pos_table, preferred_element_type=jnp.float32)
        * score_scale
    )
    lead_part = d_rotated[..., :half_width]
    tail_part = d_rotated[..., half_width:]
    d_mixed = jnp.concatenate(
        [
            lead_part * query_sin - tail_part * query_cos,
            lead_part * query_cos + tail_part * query_sin,
        ],
        -1,
    ).astype(jnp.bfloat16)
    d_query_pos = jnp.einsum(
        "qshf,fhd->qshd", d_mixed, rel_heads, preferred_element_type=jnp.float32
    )
    grad_w_rel = jnp.einsum(
        "qshf,qshd->fhd", d_mixed, query_position, preferred_element_type=jnp.float32
    ).reshape(model_width, model_width)
    grad_bias_content = jnp.sum(d_content, (0, 1)).reshape(model_width)
    grad_bias_position = jnp.sum(d_query_pos, (0, 1)).reshape(model_width)
    d_queries = (
        (d_content + d_query_pos).reshape(seg_dev, streams, model_width).astype(jnp.bfloat16)
    )
    grad_w_query = jnp.einsum(
        "rsd,rse->de", seg_normed, d_queries, preferred_element_type=jnp.float32
    )
    grad_w_key = jnp.einsum("rsd,rse->de", normed_low, d_keys, preferred_element_type=jnp.float32)
    grad_w_value = jnp.einsum(
        "rsd,rse->de", normed_low, d_values, preferred_element_type=jnp.float32
    )
    d_from_kv = jnp.einsum(
        "rse,de->rsd", d_keys, w_key, preferred_element_type=jnp.float32
    ) + jnp.einsum("rse,de->rsd", d_values, w_value, preferred_element_type=jnp.float32)
    d_from_query = jnp.einsum("rse,de->rsd", d_queries, w_query, preferred_element_type=jnp.float32)
    d_normed = jnp.concatenate([d_from_kv[:split_at], d_from_kv[split_at:] + d_from_query], 0)
    _, norm_one_back = jax.vjp(layer_norm, context, gain_first, shift_first)
    d_context, grad_gain_first, grad_shift_first = norm_one_back(d_normed)
    grad_inputs = (d_hidden + d_context[split_at:]).astype(jnp.bfloat16)
    new_rows = memory_all.shape[0] // RATE
    windows = memory_all[: new_rows * RATE].reshape(new_rows, RATE, streams, model_width)
    new_compressed = (
        jnp.einsum("rtsd,tde->rse", windows, w_comp, preferred_element_type=jnp.float32) + comp_bias
    ).astype(jnp.bfloat16)
    grad_w_comp = jnp.einsum(
        "rtsd,rse->tde", windows, grad_comp, preferred_element_type=jnp.float32
    )
    grad_comp_bias = jnp.sum(grad_comp.astype(jnp.float32), (0, 1))
    (
        grad_w_query,
        grad_w_key,
        grad_w_value,
        grad_w_rel,
        grad_w_out,
        grad_bias_content,
        grad_bias_position,
        grad_gain_first,
        grad_shift_first,
        grad_gain_second,
        grad_shift_second,
        grad_bias_down,
    ) = lax.psum(
        (
            grad_w_query,
            grad_w_key,
            grad_w_value,
            grad_w_rel,
            grad_w_out,
            grad_bias_content,
            grad_bias_position,
            grad_gain_first,
            grad_shift_first,
            grad_gain_second,
            grad_shift_second,
            grad_bias_down,
        ),
        ("dp", "seq"),
    )
    grad_w_up, grad_bias_up, grad_w_down, grad_w_comp, grad_comp_bias = (
        lax.psum(grad_w_up.astype(jnp.bfloat16), "dp").astype(jnp.float32),
        lax.psum(grad_bias_up.astype(jnp.bfloat16), "dp").astype(jnp.float32),
        lax.psum(grad_w_down.astype(jnp.bfloat16), "dp").astype(jnp.float32),
        lax.psum(grad_w_comp.astype(jnp.bfloat16), "dp").astype(jnp.float32),
        lax.psum(grad_comp_bias.astype(jnp.bfloat16), "dp").astype(jnp.float32),
    )
    return (
        output,
        grad_inputs,
        new_compressed,
        grad_gain_first,
        grad_shift_first,
        grad_w_query,
        grad_w_key,
        grad_w_value,
        grad_w_rel,
        grad_bias_content,
        grad_bias_position,
        grad_w_out,
        grad_gain_second,
        grad_shift_second,
        grad_w_up,
        grad_bias_up,
        grad_w_down,
        grad_bias_down,
        grad_w_comp,
        grad_comp_bias,
    )


BF16 = jnp.bfloat16
F32 = jnp.float32
ATTEND_PARTS = 2
BACK_PARTS = 1
CALLS = (2, 2, 2, 2)
MIB = 1024 * 1024
SHORT = pl.CostEstimate(flops=1024, bytes_accessed=1024, transcendentals=0)


def contract(left, right, left_dim, right_dim):
    return lax.dot_general(
        left, right, (((left_dim,), (right_dim,)), ((), ())), preferred_element_type=F32
    )


def bit_of(axis, distance):
    return (lax.axis_index(axis) // distance) % 2


def swap(rows, axis, distance):
    count = lax.axis_size(axis)
    return lax.ppermute(rows, axis, [(i, i ^ distance) for i in range(count)])


def after(value, *others):
    return lax.optimization_barrier((value, *others))[0]


def pick(rows, which, dim):
    return lax.dynamic_index_in_dim(rows, which, dim, keepdims=False)


def halve(rows, step, dim=0):
    bit = bit_of(*step)
    got = swap(pick(rows, 1 - bit, dim).astype(BF16), *step)
    return pick(rows, bit, dim).astype(F32) + got.astype(F32)


def double(rows, step, dim=0):
    got = swap(rows, *step)
    second = bit_of(*step) == 1
    return jnp.stack([jnp.where(second, got, rows), jnp.where(second, rows, got)], dim)


def bits_below(count):
    return [1 << i for i in range(count.bit_length() - 1)]


def token(value):
    return (value[(0,) * value.ndim].astype(F32) * 0.0).astype(jnp.int32)


def to_streams(rows, count, order=0):
    me = lax.axis_index("seq")
    block = rows.shape[1]
    whole = jnp.zeros((count * block, rows.shape[2]), rows.dtype)
    for shift in range(count):
        part = pick(rows, (me + shift) % count + order, 0)
        if shift:
            part = lax.ppermute(part, "seq", [(i, (i + shift) % count) for i in range(count)])
        whole = lax.dynamic_update_slice_in_dim(whole, part, (me - shift) % count * block, 0)
    return whole


def by_stream(rows):
    return jnp.swapaxes(rows, 0, 1)


def attend_kernel(
    len_ref, qc_ref, qp_ref, k_ref, v_ref, rel_ref, table_ref, cos_ref, sin_ref, *rest
):
    p_ref, o_ref = rest[-2:]
    rows = qc_ref.shape[0] // ATTEND_PARTS
    keys = k_ref.shape[0]
    half = cos_ref.shape[1]
    split = CMEM + MEM
    for part in range(ATTEND_PARTS):
        at = slice(part * rows, (part + 1) * rows)
        mixed = contract(qp_ref[at], rel_ref[...], 1, 1)
        lead, tail = mixed[:, :half], mixed[:, half:]
        cos, sin = cos_ref[at], sin_ref[at]
        rotated = jnp.concatenate(
            [(lead * sin + tail * cos).astype(BF16), (tail * sin - lead * cos).astype(BF16)], 1
        )
        scores = contract(qc_ref[at], k_ref[...], 1, 1) + contract(rotated, table_ref[...], 1, 1)
        row_ids = part * rows + lax.broadcasted_iota(jnp.int32, (rows, keys - split), 0)
        col_ids = lax.broadcasted_iota(jnp.int32, (rows, keys - split), 1)
        visible = (col_ids <= row_ids) & (col_ids < len_ref[0])
        past = scores[:, :split]
        own = jnp.where(visible, scores[:, split:], -1e30)
        top = jnp.maximum(jnp.max(past, 1, keepdims=True), jnp.max(own, 1, keepdims=True))
        factor = math.log2(math.e) / math.sqrt(DH)
        past = jnp.exp2((past - top) * factor)
        own = jnp.exp2((own - top) * factor)
        total = jnp.sum(past, 1, keepdims=True) + jnp.sum(own, 1, keepdims=True)
        scale = 1.0 / total
        prob = jnp.concatenate([(past * scale).astype(BF16), (own * scale).astype(BF16)], 1)
        p_ref[0, at] = prob
        o_ref[at] = jnp.dot(prob, v_ref[...], preferred_element_type=F32).astype(BF16)


def attend(heads, length, content, position, keys, values, w_rel, table, cos, sin, first=(), into=()):
    seg, width = content.shape
    total = keys.shape[0]
    block = seg
    start, count = heads.start, len(heads)
    head = lambda h, q: (0, start + h)
    rows = lambda h, q: (q, start + h)
    whole = pl.BlockSpec(memory_space=pl.ANY)
    operands = [length, content, position, keys, values, w_rel, table, cos, sin]
    aliases = {len(operands) + i: i for i in range(len(into))}
    operands += [*into, *first]
    return pl.pallas_call(
        attend_kernel,
        grid=(count, seg // block),
        in_specs=[
            pl.BlockSpec(memory_space=pltpu.SMEM),
            pl.BlockSpec((block, DH), rows),
            pl.BlockSpec((block, DH), rows),
            pl.BlockSpec((total, DH), head),
            pl.BlockSpec((total, DH), head),
            pl.BlockSpec((width, DH), head),
            pl.BlockSpec((total, width), lambda h, q: (0, 0)),
            pl.BlockSpec((block, width // 2), lambda h, q: (q, 0)),
            pl.BlockSpec((block, width // 2), lambda h, q: (q, 0)),
        ]
        + [whole] * (len(into) + len(first)),
        out_specs=[
            pl.BlockSpec((1, block, total), lambda h, q: (start + h, q, 0)),
            pl.BlockSpec((block, DH), rows),
        ],
        out_shape=[
            jax.ShapeDtypeStruct((H, seg, total), BF16),
            jax.ShapeDtypeStruct((seg, width), BF16),
        ],
        input_output_aliases=aliases,
        compiler_params=pltpu.CompilerParams(vmem_limit_bytes=52 * MIB),
        cost_estimate=SHORT,
        name="attend",
    )(*operands)


def attend_back_kernel(
    with_sums,
    bits_ref,
    p_ref,
    da_ref,
    qc_ref,
    qp_ref,
    k_ref,
    v_ref,
    rel_ref,
    wq_ref,
    wk_ref,
    wv_ref,
    normed_ref,
    table_ref,
    cos_ref,
    sin_ref,
    *rest,
):
    keep_ref, give_ref, rows_ref, along_ref, shift_ref, bias_ref = rest[-6:]
    head = pl.program_id(0)
    scale = 1.0 / math.sqrt(DH)
    half = cos_ref.shape[1]
    seg = da_ref.shape[0]
    past = k_ref.shape[0] - seg
    block = seg // BACK_PARTS
    dk_t = dv_t = drel_t = 0.0
    d_content_sum = d_position_sum = 0.0
    d_queries = []
    for part in range(BACK_PARTS):
        at = slice(part * block, (part + 1) * block)
        prob = p_ref[0, at]
        d_attn = da_ref[at]
        dv_t = dv_t + contract(d_attn, prob, 0, 0)
        d_prob = contract(d_attn, v_ref[...], 1, 1)
        prob_f = prob.astype(F32)
        weighted = prob_f * d_prob
        inner = jnp.sum(weighted, 1, keepdims=True)
        d_scores = (weighted - prob_f * inner).astype(BF16)
        dk_t = dk_t + contract(qc_ref[at], d_scores, 0, 0)
        d_content = jnp.dot(d_scores, k_ref[...], preferred_element_type=F32) * scale
        d_rotated = jnp.dot(d_scores, table_ref[...], preferred_element_type=F32)
        lead, tail = d_rotated[:, :half], d_rotated[:, half:]
        cos, sin = cos_ref[at] * scale, sin_ref[at] * scale
        d_mixed = jnp.concatenate(
            [(lead * sin - tail * cos).astype(BF16), (lead * cos + tail * sin).astype(BF16)], 1
        )
        d_position = jnp.dot(d_mixed, rel_ref[...], preferred_element_type=F32)
        drel_t = drel_t + contract(qp_ref[at], d_mixed, 0, 0)
        d_queries.append((d_content + d_position).astype(BF16))
        d_content_sum = d_content_sum + jnp.sum(d_content, 0, keepdims=True)
        d_position_sum = d_position_sum + jnp.sum(d_position, 0, keepdims=True)
    bias_ref[...] = jnp.concatenate([d_content_sum, d_position_sum], 0)

    d_query = jnp.concatenate(d_queries, 0)
    d_kv_t = jnp.concatenate([(dk_t * scale).astype(BF16), dv_t.astype(BF16)], 0)
    d_kv = d_kv_t[:, past:].T
    of_kv_t = jnp.dot(d_kv_t, normed_ref[...], preferred_element_type=F32)
    of_query_t = contract(d_query, normed_ref[past:, :], 0, 0)
    of_query, of_key, of_value = of_query_t.T, of_kv_t[:DH].T, of_kv_t[DH:].T
    mine = bits_ref[0] == 1
    for i, grad in enumerate((of_query, drel_t.T, of_key, of_value)):
        middle = grad.shape[0] // 2
        low, high = grad[:middle].astype(BF16), grad[middle:].astype(BF16)
        keep_ref[i] = jnp.where(mine, high, low)
        give_ref[i] = jnp.where(mine, low, high)
    own_rows = (
        contract(d_query, wq_ref[...], 1, 1)
        + contract(d_kv[:, :DH], wk_ref[...], 1, 1)
        + contract(d_kv[:, DH:], wv_ref[...], 1, 1)
    )
    wq = wq_ref[...].astype(F32)
    wk = wk_ref[...].astype(F32)
    wv = wv_ref[...].astype(F32)
    sums = jnp.sum(d_kv_t.astype(F32), 1, keepdims=True).T
    own_along = of_query * wq + of_key * wk + of_value * wv
    own_shift = (
        jnp.sum(d_query.astype(F32), 0, keepdims=True) * wq + sums[:, :DH] * wk + sums[:, DH:] * wv
    )

    @pl.when(head == 0)
    def _():
        rows_ref[...] = own_rows + rest[0][...] if with_sums else own_rows
        along_ref[...] = own_along
        shift_ref[...] = own_shift

    @pl.when(head > 0)
    def _():
        rows_ref[...] += own_rows
        along_ref[...] += own_along
        shift_ref[...] += own_shift


def attend_back(
    start,
    count,
    heads,
    bits,
    prob,
    d_attn,
    content,
    position,
    keys,
    values,
    w_rel,
    w_query,
    w_key,
    w_value,
    normed,
    table,
    cos,
    sin,
    sums=(),
    into=(),
    first=(),
):
    seg, width = content.shape
    total = keys.shape[0]
    block = seg
    column = lambda h: (0, start + h)
    rows = lambda h: (0, start + h)
    fixed = lambda h: (0, 0)
    whole = pl.BlockSpec(memory_space=pl.ANY)
    operands = [bits, prob, d_attn, content, position, keys, values, w_rel]
    operands += [w_query, w_key, w_value, normed, table, cos, sin]
    aliases = {}
    sum_specs = [
        pl.BlockSpec((seg, width), fixed),
        pl.BlockSpec((width, DH), fixed),
        pl.BlockSpec((width, DH), fixed),
    ]
    for i in range(len(sums)):
        aliases[len(operands) + i] = 2 + i
    operands += [*sums]
    for i in range(len(into)):
        aliases[len(operands) + i] = i
    operands += [*into, *first]
    half = jax.ShapeDtypeStruct(into[0].shape if into else (4, width // 2, len(heads) * DH), BF16)
    half_spec = pl.BlockSpec((4, width // 2, DH), lambda h: (0, 0, start - heads.start + h))
    return pl.pallas_call(
        functools.partial(attend_back_kernel, bool(sums)),
        grid=(count,),
        in_specs=[
            pl.BlockSpec(memory_space=pltpu.SMEM),
            pl.BlockSpec((1, block, total), lambda h: (start + h, 0, 0)),
            pl.BlockSpec((block, DH), rows),
            pl.BlockSpec((block, DH), rows),
            pl.BlockSpec((block, DH), rows),
            pl.BlockSpec((total, DH), column),
            pl.BlockSpec((total, DH), column),
            pl.BlockSpec((width, DH), column),
            pl.BlockSpec((width, DH), column),
            pl.BlockSpec((width, DH), column),
            pl.BlockSpec((width, DH), column),
            pl.BlockSpec(memory_space=pltpu.VMEM),
            pl.BlockSpec(memory_space=pltpu.VMEM),
            pl.BlockSpec(memory_space=pltpu.VMEM),
            pl.BlockSpec(memory_space=pltpu.VMEM),
        ]
        + sum_specs[: len(sums)]
        + [whole] * (len(into) + len(first)),
        out_specs=[half_spec, half_spec] + sum_specs + [pl.BlockSpec((2, DH), lambda h: (0, h))],
        out_shape=[
            half,
            half,
            jax.ShapeDtypeStruct((seg, width), F32),
            jax.ShapeDtypeStruct((width, DH), F32),
            jax.ShapeDtypeStruct((width, DH), F32),
            jax.ShapeDtypeStruct((2, count * DH), F32),
        ],
        input_output_aliases=aliases,
        compiler_params=pltpu.CompilerParams(vmem_limit_bytes=52 * MIB),
        cost_estimate=SHORT,
        name="attend_back",
    )(*operands)


def in_vmem():
    return pl.BlockSpec(memory_space=pltpu.VMEM)


def norm_kernel(count, owners_ref, *refs):
    parts, (gain_ref, shift_ref), (normed_ref, rows_ref) = refs[:count], refs[count : count + 2], refs[-2:]
    block = rows_ref.shape[1]
    for i, part in enumerate(parts):
        owner = owners_ref[i]
        for kind in range(3):
            low = part[kind * block : (kind + 1) * block]
            values = low.astype(F32)
            center = values - jnp.mean(values, -1, keepdims=True)
            spread = jnp.mean(center * center, -1, keepdims=True)
            normed = center * lax.rsqrt(spread + 1e-05) * gain_ref[...] + shift_ref[...]
            normed_ref[kind, owner] = normed.astype(BF16)
            if kind == 2:
                rows_ref[owner] = low


def norm_context(parts, owners, gain, shift, after=()):
    rows, width = parts[0].shape
    block = rows // 3
    normed, inputs = pl.pallas_call(
        functools.partial(norm_kernel, len(parts)),
        in_specs=[pl.BlockSpec(memory_space=pltpu.SMEM)] + [in_vmem()] * (len(parts) + 2)
        + [pl.BlockSpec(memory_space=pl.ANY)] * len(after),
        out_specs=[in_vmem(), in_vmem()],
        out_shape=[
            jax.ShapeDtypeStruct((3, len(parts), block, width), BF16),
            jax.ShapeDtypeStruct((len(parts), block, width), BF16),
        ],
        compiler_params=pltpu.CompilerParams(vmem_limit_bytes=48 * MIB),
        cost_estimate=SHORT,
        name="norm_context",
    )(owners, *parts, gain.reshape(1, -1), shift.reshape(1, -1), *after)
    return normed.reshape(-1, width), inputs.reshape(-1, width)


def place_kernel(count, owners_ref, *refs):
    for i, part in enumerate(refs[:count]):
        refs[-1][owners_ref[i]] = part[...]


def place_rows(parts, owners, after=()):
    rows, width = parts[0].shape
    return pl.pallas_call(
        functools.partial(place_kernel, len(parts)),
        in_specs=[pl.BlockSpec(memory_space=pltpu.SMEM)]
        + [in_vmem()] * len(parts)
        + [pl.BlockSpec(memory_space=pl.ANY)] * len(after),
        out_specs=in_vmem(),
        out_shape=jax.ShapeDtypeStruct((len(parts), rows, width), parts[0].dtype),
        cost_estimate=SHORT,
        name="place_rows",
    )(owners, *parts, *after)


def hold(values, *others):
    whole = pl.BlockSpec(memory_space=pl.ANY)
    return pl.pallas_call(
        lambda *refs: None,
        in_specs=[whole] * (len(values) + len(others)),
        out_specs=[whole] * len(values),
        out_shape=[jax.ShapeDtypeStruct(v.shape, v.dtype) for v in values],
        input_output_aliases={i: i for i in range(len(values))},
        cost_estimate=SHORT,
        name="hold",
    )(*values, *others)


def copy_kernel(rows_ref, *refs):
    refs[-1][...] = rows_ref[...]


def copy_after(rows, *others):
    return pl.pallas_call(
        copy_kernel,
        in_specs=[in_vmem()] + [pl.BlockSpec(memory_space=pl.ANY)] * len(others),
        out_specs=in_vmem(),
        out_shape=jax.ShapeDtypeStruct(rows.shape, rows.dtype),
        cost_estimate=SHORT,
        name="copy_after",
    )(rows, *others)


def out_grad_kernel(bits_ref, left_ref, right_ref, keep_ref, give_ref):
    mine = bits_ref[0] == 1
    grad = contract(left_ref[...], right_ref[...], 0, 0)
    middle, columns = keep_ref.shape[1:]
    for i in range(2):
        part = grad[:, i * columns : (i + 1) * columns]
        low, high = part[:middle].astype(BF16), part[middle:].astype(BF16)
        keep_ref[i] = jnp.where(mine, high, low)
        give_ref[i] = jnp.where(mine, low, high)


def out_grad(bits, left, right):
    width = right.shape[1]
    half = jax.ShapeDtypeStruct((6, width // 2, width // 2), BF16)
    spec = pl.BlockSpec((2, width // 2, width // 2), lambda i: (2, 0, 0))
    whole = pl.BlockSpec(left.shape, lambda i: (0, 0))
    return pl.pallas_call(
        out_grad_kernel,
        grid=(1,),
        in_specs=[pl.BlockSpec(memory_space=pltpu.SMEM), whole, whole],
        out_specs=[spec, spec],
        out_shape=[half, half],
        compiler_params=pltpu.CompilerParams(vmem_limit_bytes=48 * MIB),
        cost_estimate=SHORT,
        name="out_grad",
    )(bits, left, right)


def finish_kernel(bits_ref, own_ref, got_ref, *refs):
    outs = refs[-5:]
    own = pl.program_id(0) == bits_ref[0]

    def write(ref):
        for i in range(4):
            outs[i][...] = ref[i].astype(F32)
        if ref.shape[0] > 4:
            half = ref.shape[2]
            outs[4][:, :half] = ref[4].astype(F32)
            outs[4][:, half:] = ref[5].astype(F32)

    pl.when(own)(lambda: write(own_ref))
    pl.when(jnp.logical_not(own))(lambda: write(got_ref))


def finish(bits, column, columns, own, got, results):
    count, rows, width = own.shape
    fixed = pl.BlockSpec(own.shape, lambda i: (0, 0, 0))
    block = pl.BlockSpec((rows, width), lambda i: (i, column))
    last = pl.BlockSpec((rows, columns * width), lambda i: (i, 0))
    out = jax.ShapeDtypeStruct((2 * rows, columns * width), F32)
    if count == 4:
        out_specs, before = [block] * 4, results[:4]
    else:
        out_specs, before = [block] * 4 + [last], results
    sums = pl.pallas_call(
        finish_kernel if count > 4 else lambda *refs: finish_kernel(*refs, None),
        grid=(2,),
        in_specs=[pl.BlockSpec(memory_space=pltpu.SMEM), fixed, fixed]
        + [pl.BlockSpec(memory_space=pl.ANY)] * len(before),
        out_specs=out_specs,
        out_shape=[out] * len(out_specs),
        input_output_aliases={3 + i: i for i in range(len(before))},
        compiler_params=pltpu.CompilerParams(vmem_limit_bytes=48 * MIB),
        cost_estimate=SHORT,
        name="finish",
    )(bits, own, got, *before)
    return list(sums) + list(results[len(sums) :])


class Chain:
    def __init__(self, moves, keeps, gives):
        self.moves, self.keeps, self.gives = list(moves), keeps, gives
        self.join = False
        self.got = None


def parts_of(move):
    return len(move[1])


def split_rows(rows, pre):
    lead, count, columns = rows.shape
    return rows.reshape(lead, pre, 2, count // (2 * pre), columns)


def first_halves(rows, move):
    keeps, gives = [], []
    size = rows.shape[0] // parts_of(move)
    for i, (step, pre) in enumerate(move[1]):
        cells = split_rows(rows[i * size : (i + 1) * size], pre)
        bit = bit_of(*step)
        flat = (size, -1, rows.shape[2])
        keeps.append(pick(cells, bit, 2).reshape(flat))
        gives.append(pick(cells, 1 - bit, 2).reshape(flat))
    return keeps, gives


def round_of(chains, bits, bit_names, after=(), through=()):
    operands, plans, out_shape = [], [], []
    for chain in chains:
        kind, cuts = chain.moves.pop(0)
        nexts = chain.moves[0] if chain.moves else None
        got = chain.got or [[swap(give, *step)] for give, (step, _) in zip(chain.gives, cuts)]
        chain.got = None
        held = chain.keeps if kind == "halve" else chain.gives
        leads, columns = [h.shape[0] for h in held], held[0].shape[2]
        total = sum(leads)
        next_kind, next_cuts = nexts if nexts else ("end", [None])
        size = total // len(next_cuts)
        ins, views = [], []
        for i, (h, g) in enumerate(zip(held, got)):
            base = sum(leads[:i])
            if kind == "double":
                cells = max(pre for _, pre in cuts)
                view = (h.shape[0], cells, h.shape[1] // cells, columns)
                bit = (bit_names.index(cuts[i][0]), cuts[i][1])
            elif next_kind == "halve":
                cells = max([2 * pre for _, pre in next_cuts] + [len(g) for g in got])
                view = (h.shape[0], cells, h.shape[1] // cells, columns)
                bit = None
            else:
                view = h.shape
                bit = None
            ins.append((len(operands), base, bit, view, len(g)))
            operands += [h.reshape(view)]
            operands += [r.reshape(view[0], -1, *view[2:]) if len(g) > 1 else r.reshape(view) for r in g]
        rows = held[0].shape[1]
        outs = []
        for j, cut in enumerate(next_cuts):
            if next_kind == "halve":
                cells = ins[0][3][1]
                shape = (size, cells // 2, rows // cells, columns)
                outs.append((len(out_shape), bit_names.index(cut[0]), cut[1]))
                out_shape += [jax.ShapeDtypeStruct(shape, BF16)] * 2
            else:
                if kind == "double":
                    cells = ins[0][3][1]
                    shape = (size, cells * 2, rows // cells, columns)
                    if chain.join and next_kind == "end":
                        shape = (1, cells * 2, rows // cells, size * columns)
                else:
                    shape = (size, rows, columns)
                outs.append((len(out_shape), None, None))
                out_shape += [jax.ShapeDtypeStruct(shape, held[0].dtype)]
        plans.append((kind, next_kind, size, ins, outs))

    def kernel(bits_ref, *refs):
        inputs, results = refs[: len(operands)], refs[len(refs) - len(out_shape) - len(through) :]
        for kind, next_kind, size, ins, outs in plans:
            for at, base, bit, view, count in ins:
                held_ref, got_ref = inputs[at], inputs[at + 1]
                got_refs = inputs[at + 1 : at + 1 + count]
                for i in range(view[0]):
                    where, which = divmod(base + i, size)
                    out, out_bit, out_pre = outs[where]
                    if kind == "double":
                        mine = bits_ref[bit[0]]
                        run = view[1] // bit[1]
                        for cell in range(view[1]):
                            for side, ref in ((mine, held_ref), (1 - mine, got_ref)):
                                place = (cell // run * 2 + side) * run + cell % run
                                if results[out].shape[3] == ref.shape[3]:
                                    results[out][which, place] = ref[i, cell]
                                else:
                                    wide = slice(which * ref.shape[3], (which + 1) * ref.shape[3])
                                    results[out][0, place, :, wide] = ref[i, cell]
                    elif next_kind == "halve":
                        mine = bits_ref[out_bit]
                        run = view[1] // (2 * out_pre)
                        for cell in range(view[1] // 2):
                            if count > 1:
                                sums = []
                                for side in range(2):
                                    place = (cell // run * 2 + side) * run + cell % run
                                    piece, rest = divmod(place * count, view[1])
                                    more = got_refs[piece][i, rest // count].astype(F32)
                                    sums.append(held_ref[i, place].astype(F32) + more)
                                high = mine == 1
                                results[out][which, cell] = jnp.where(high, sums[1], sums[0]).astype(BF16)
                                results[out + 1][which, cell] = jnp.where(high, *sums).astype(BF16)
                                continue
                            for side, slot in ((mine, out), (1 - mine, out + 1)):
                                place = (cell // run * 2 + side) * run + cell % run
                                results[slot][which, cell] = (
                                    held_ref[i, place].astype(F32) + got_ref[i, place].astype(F32)
                                ).astype(BF16)
                    else:
                        results[out][which] = (held_ref[i].astype(F32) + got_ref[i].astype(F32)).astype(
                            results[out].dtype
                        )

    in_vmem = pl.BlockSpec(memory_space=pltpu.VMEM)
    results = pl.pallas_call(
        kernel,
        in_specs=[pl.BlockSpec(memory_space=pltpu.SMEM)]
        + [in_vmem] * len(operands)
        + [pl.BlockSpec(memory_space=pl.ANY)] * (len(through) + len(after)),
        out_specs=[in_vmem] * len(out_shape) + [pl.BlockSpec(memory_space=pl.ANY)] * len(through),
        out_shape=out_shape + [jax.ShapeDtypeStruct(r.shape, r.dtype) for r in through],
        input_output_aliases={
            1 + len(operands) + i: len(out_shape) + i for i in range(len(through))
        },
        compiler_params=pltpu.CompilerParams(vmem_limit_bytes=48 * MIB),
        cost_estimate=SHORT,
        name="add_and_split",
    )(bits, *operands, *through, *after)
    for chain, (kind, next_kind, size, ins, outs) in zip(chains, plans):
        flat = lambda r: r.reshape(r.shape[0], -1, r.shape[-1])
        if next_kind == "halve":
            chain.keeps = [flat(results[o]) for o, _, _ in outs]
            chain.gives = [flat(results[o + 1]) for o, _, _ in outs]
        else:
            chain.keeps = []
            chain.gives = [flat(results[o]) for o, _, _ in outs]
    return results[len(out_shape) :]


def input_grad_kernel(targets_ref, d_rows_ref, x_ref, d_hidden_ref, gain_ref, *outs):
    block = outs[0].shape[0]
    for i, out in enumerate(outs):
        at = pl.ds(pl.multiple_of(targets_ref[i] * block, block), block)
        values = x_ref[at, :].astype(F32)
        center = values - jnp.mean(values, -1, keepdims=True)
        spread = jnp.mean(center * center, -1, keepdims=True)
        inverse = lax.rsqrt(spread + 1e-05)
        unit = center * inverse
        grad = d_rows_ref[at, :] * gain_ref[...]
        mean = jnp.mean(grad, -1, keepdims=True)
        along = jnp.mean(grad * unit, -1, keepdims=True)
        out[...] = (d_hidden_ref[at, :] + inverse * (grad - mean - unit * along)).astype(BF16)


def input_grad(targets, d_rows, rows, d_hidden, gain, count):
    block = jax.ShapeDtypeStruct((rows.shape[0] // count, rows.shape[1]), BF16)
    return pl.pallas_call(
        input_grad_kernel,
        in_specs=[pl.BlockSpec(memory_space=pltpu.SMEM)] + [in_vmem()] * 4,
        out_specs=[in_vmem()] * count,
        out_shape=[block] * count,
        compiler_params=pltpu.CompilerParams(vmem_limit_bytes=48 * MIB),
        cost_estimate=SHORT,
        name="input_grad",
    )(targets, d_rows, rows, d_hidden, gain.reshape(1, -1))


def widen_kernel(rows_ref, out_ref):
    out_ref[...] = rows_ref[...].astype(F32)


def widen_flip_kernel(rows_ref, out_ref):
    out_ref[...] = rows_ref[...].astype(F32).T


def widen(rows, flip=False):
    count, width = rows.shape
    block = count // 4
    out = pl.BlockSpec((width, block), lambda i: (0, i)) if flip else pl.BlockSpec((block, width), lambda i: (i, 0))
    return pl.pallas_call(
        widen_flip_kernel if flip else widen_kernel,
        grid=(4,),
        in_specs=[pl.BlockSpec((block, width), lambda i: (i, 0))],
        out_specs=out,
        out_shape=jax.ShapeDtypeStruct((width, count) if flip else (count, width), F32),
        compiler_params=pltpu.CompilerParams(vmem_limit_bytes=48 * MIB),
        cost_estimate=SHORT,
        name="widen",
    )(rows)


def compress_kernel(mem_ref, gc_ref, w_ref, bias_ref, new_ref, grad_ref, wide_ref, sum_ref):
    stream = pl.program_id(0)
    count = gc_ref.shape[1]
    rows = mem_ref.shape[1]
    blocks, depth, lanes = wide_ref.shape
    for i in range(blocks):
        wide_ref[i, :rows] = mem_ref[0, :, i * lanes : (i + 1) * lanes].astype(F32)
        wide_ref[i, rows:] = jnp.zeros((depth - rows, lanes), F32)
    made = jnp.zeros((count, gc_ref.shape[2]), F32) + bias_ref[...]
    for tap in range(RATE):
        taken = [wide_ref[i, pl.ds(tap, count, stride=RATE), :] for i in range(blocks)]
        window = jnp.concatenate(taken, 1).astype(BF16)
        made = made + jnp.dot(window, w_ref[tap], preferred_element_type=F32)
        part = contract(window, gc_ref[0], 0, 0)
        sum_ref[tap] = jnp.where(stream == 0, part, part + sum_ref[tap])
    new_ref[0] = made.astype(BF16)

    @pl.when(stream == pl.num_programs(0) - 1)
    def _():
        grad_ref[...] = sum_ref[...].astype(BF16)


def compress_rows(memory, grad, weights, bias):
    streams, rows, width = memory.shape
    count, columns = grad.shape[1:]
    return pl.pallas_call(
        compress_kernel,
        grid=(streams,),
        in_specs=[
            pl.BlockSpec((1, rows, width), lambda i: (i, 0, 0)),
            pl.BlockSpec((1, count, columns), lambda i: (i, 0, 0)),
            pl.BlockSpec(weights.shape, lambda i: (0, 0, 0)),
            pl.BlockSpec((1, columns), lambda i: (0, 0)),
        ],
        out_specs=[
            pl.BlockSpec((1, count, columns), lambda i: (i, 0, 0)),
            pl.BlockSpec(weights.shape, lambda i: (0, 0, 0)),
        ],
        out_shape=[
            jax.ShapeDtypeStruct((streams, count, columns), BF16),
            jax.ShapeDtypeStruct(weights.shape, BF16),
        ],
        scratch_shapes=[
            pltpu.VMEM((width // DH, RATE * count + 16, DH), F32),
            pltpu.VMEM(weights.shape, F32),
        ],
        compiler_params=pltpu.CompilerParams(vmem_limit_bytes=48 * MIB),
        cost_estimate=SHORT,
        name="compress_rows",
    )(memory, grad, weights, bias.reshape(1, -1))


def own_streams_plan(
    inputs,
    memory,
    compressed,
    seg_len,
    gain_first,
    shift_first,
    w_query,
    w_key,
    w_value,
    w_rel,
    bias_content,
    bias_position,
    w_out,
    gain_second,
    shift_second,
    w_up,
    bias_up,
    w_down,
    bias_down,
    w_comp,
    comp_bias,
    grad_out,
    grad_comp,
):
    seq_parts = lax.axis_size("seq")
    dp_parts = lax.axis_size("dp")
    me = lax.axis_index("seq")
    seg_dev, streams, width = inputs.shape
    seg = seg_dev * seq_parts
    split = CMEM + MEM
    hidden_dev = w_down.shape[0]

    core = ("dp", 1)
    wide = [("dp", d) for d in reversed(bits_below(dp_parts)[1:])]
    line = [("seq", d) for d in bits_below(seq_parts)]
    there = list(range(len(wide)))
    back = there[::-1]
    core_bit = bit_of(*core)

    bit_names = [core] + wide + line
    bits = jnp.stack([bit_of(*name) for name in bit_names]).astype(jnp.int32)
    wide_in = [[(wide[i], 1), (wide[j], 1 << j)] for i, j in zip(there, back)]
    line_in = [[(step, 1 << i)] for i, step in enumerate(reversed(line))][::-1]
    core_cut, line_cuts, wide_cuts = [(core, 1)], [[(s, 1)] for s in line], [[(s, 1)] for s in wide]

    def moves_of(cuts, collected):
        return [("halve", c) for c in cuts] + [("double", c) for c in reversed(collected)]

    piece = hidden_dev // dp_parts
    place = lax.axis_index("dp")

    def gathered(rows):
        rows = jnp.swapaxes(rows.reshape(piece, 2, width // 2), 0, 1)
        chain = Chain(moves_of([], wide_in + line_in), [], [rows])
        chain.join = True
        return chain

    up_piece = lax.dynamic_slice_in_dim(w_up, place * piece, piece, 1).T
    up_chain = gathered(up_piece)
    round_of([up_chain], bits, bit_names)
    for step in line[:-1]:
        round_of([up_chain], bits, bit_names)
    order_two = token(up_chain.gives[0])

    key_cos, key_sin = sinusoids(jnp.arange(split + seg, dtype=jnp.int32))
    table = jnp.concatenate([key_cos, key_sin], -1).astype(BF16)
    cos, sin = key_cos[split:], key_sin[split:]

    owners = jnp.stack([(me - shift) % seq_parts for shift in range(seq_parts)]).astype(jnp.int32)

    def send(parts):
        return [parts[0]] + [
            lax.ppermute(part, "seq", [(i, (i + shift) % seq_parts) for i in range(seq_parts)])
            for shift, part in enumerate(parts)
            if shift
        ]

    def parts_for(rows, order=0):
        return [pick(rows, (me + shift) % seq_parts + order, 0) for shift in range(seq_parts)]

    def from_streams(parts):
        return by_stream(place_rows(send(parts), owners))

    blocks = [by_stream(rows) for rows in (compressed, memory, inputs)]
    parts = send(parts_for(jnp.concatenate(blocks, 1)))
    down_piece = lax.dynamic_slice_in_dim(w_down, place * piece + order_two, piece, 0)
    down_chain = gathered(down_piece)
    go_parts = parts_for(by_stream(grad_out))
    memory_rows = by_stream(memory)
    idle = [*up_chain.gives, *down_chain.gives, table, cos, sin, *go_parts, memory_rows]
    normed, x_rows = norm_context(parts, owners, gain_first, shift_first, idle)
    length = lax.dynamic_slice_in_dim(seg_len, me, 1)
    round_of([up_chain], bits, bit_names, [normed])
    order = token(normed)
    bias_all = lax.dynamic_slice_in_dim(bias_up.reshape(-1, 2, piece), core_bit + order, 1, 1)
    bias_all = bias_all.reshape(1, -1)

    seg_normed = normed[split:]
    queries = jnp.dot(seg_normed, w_query, preferred_element_type=F32)
    keys = jnp.dot(normed, w_key, preferred_element_type=F32).astype(BF16)
    values = jnp.dot(normed, w_value, preferred_element_type=F32).astype(BF16)
    content = (queries + bias_content).astype(BF16)
    position = (queries + bias_position).astype(BF16)
    given = (length, content, position, keys, values, w_rel, table, cos, sin)
    round_of([down_chain], bits, bit_names, [normed])
    round_of([down_chain], bits, bit_names, [values])
    memory_rows = copy_after(memory_rows, down_chain.gives[0])
    memory_all = lax.all_gather(memory_rows, "seq", axis=1, tiled=True)
    prob, attn_out = attend(range(H // 2), *given, first=down_chain.gives)
    prob, attn_out = round_of([up_chain, down_chain], bits, bit_names, [], [prob, attn_out])
    while up_chain.moves:
        round_of([up_chain], bits, bit_names, [attn_out])
    up_half = up_chain.gives[0][0]
    bias_all = double(bias_all, line[-1], 0)
    prob, attn_out = attend(
        range(H // 2, H), *given, first=down_chain.gives + [bias_all], into=[prob, attn_out]
    )
    (attn_out,) = round_of([down_chain], bits, bit_names, [], [attn_out])
    while down_chain.moves:
        round_of([down_chain], bits, bit_names)
    down_half = down_chain.gives[0][0]
    for i, step in enumerate(line[-2::-1]):
        bias_all = double(bias_all, step, i + 1)
    bias_half = jnp.swapaxes(bias_all.reshape(seq_parts, -1, piece), 0, 1).reshape(-1).astype(F32)
    x_f = x_rows.astype(F32)
    hidden = x_f + jnp.dot(attn_out, w_out, preferred_element_type=F32)
    normed_two = layer_norm(hidden, gain_second, shift_second).astype(BF16)

    pair_normed = double(normed_two, core).reshape(-1, width)
    pre_act = contract(pair_normed, up_half, 1, 1) + bias_half
    activated = gelu_tanh(pre_act).astype(BF16)
    go_rows = place_rows(send(go_parts), owners, [activated, memory_all]).reshape(seg, width)
    pair_grad = double(go_rows, core).reshape(-1, width)
    ffn_rows = jnp.dot(activated, down_half, preferred_element_type=F32)
    ffn_rows = halve(ffn_rows.reshape(2, seg, width), core)
    output = (hidden + ffn_rows + bias_down).astype(BF16)
    output_parts = parts_for(output.reshape(seq_parts, seg_dev, width))
    groups_of = [list(range(c, dp_parts, 2)) for c in range(2)]

    def over_rows(grad):
        return lax.psum_scatter(grad, "dp", axis_index_groups=groups_of, tiled=True)

    down_sum = over_rows(contract(activated, pair_grad, 0, 0).astype(BF16))
    d_activated = contract(pair_grad, down_half, 1, 1)
    _, gelu_back = jax.vjp(gelu_tanh, pre_act)
    d_pre = gelu_back(d_activated)[0].astype(BF16)
    d_normed_two = jnp.dot(d_pre, up_half, preferred_element_type=F32)
    d_normed_two = halve(d_normed_two.reshape(2, seg, width), core)
    up_sum = over_rows(contract(d_pre, pair_normed, 0, 0).astype(BF16))
    grad_bias_half = jnp.sum(d_pre.astype(F32), 0)

    go_f = go_rows.astype(F32)
    _, norm_two_back = jax.vjp(layer_norm, hidden, gain_second, shift_second)
    d_hidden_ffn, grad_gain_second, grad_shift_second = norm_two_back(d_normed_two)
    d_hidden = go_f + d_hidden_ffn
    grad_bias_down = jnp.sum(go_f, 0)
    d_branch = d_hidden.astype(BF16)
    d_attn = contract(d_branch, w_out, 1, 1).astype(BF16)

    half_heads = H // 2
    group_moves = moves_of([core_cut] + wide_in + line_cuts, [core_cut] + wide_in + line_cuts)
    groups, biases, head_sums = [], [], []
    output_rows = send(output_parts)

    first, start, alongs, shifts = [], 0, [], []
    for call, heads in enumerate(CALLS):
        base = start // half_heads * half_heads
        group_heads = range(base, base + half_heads)
        if start == 0:
            halves = out_grad(bits, attn_out, d_branch)
        elif start == base:
            halves = []
        *halves, d_rows, along, shift_part, bias_part = attend_back(
            start, heads, group_heads, bits, prob, d_attn, content, position, keys, values,
            w_rel, w_query, w_key, w_value, normed, table, cos, sin, head_sums, halves, first,
        )
        start += heads
        passing = [*halves, d_rows, along, shift_part, bias_part]
        if call == 0:
            down_sum, *passing = hold([down_sum, *passing])
            down_sum = lax.psum_scatter(down_sum, "seq", tiled=True)
            first = output_parts[1:]
        elif call == 1:
            output_rows = place_rows(output_rows, owners, [bias_part])
            up_sum, *passing = hold([up_sum, *passing], output_rows)
            up_sum = lax.psum_scatter(up_sum, "seq", tiled=True)
            first = []
        elif call == 2:
            passing = round_of(groups, bits, bit_names, [], passing)
            first = [g for c in groups for g in c.gives]
        else:
            down_sum, *passing = round_of(groups, bits, bit_names, [], [down_sum, *passing])
            down_sum = lax.all_gather(down_sum, "dp", tiled=True)
        *halves, d_rows, along, shift_part, bias_part = passing
        head_sums = [d_rows]
        alongs.append(along)
        shifts.append(shift_part)
        biases.append(bias_part)
        if start == group_heads.stop:
            groups.append(Chain(group_moves, [halves[0]], [halves[1]]))
            first += [halves[1]]
    output = by_stream(output_rows)

    def compress(memory_all):
        new_rows = grad_comp.shape[0]
        padded = jnp.pad(by_stream(grad_comp), ((0, 0), (0, -new_rows % 16), (0, 0)))
        made, grad = compress_rows(memory_all, padded, w_comp, comp_bias)
        grad = grad.reshape(1, -1, grad.shape[2])
        moves = moves_of([core_cut] + wide_cuts, [core_cut] + wide_cuts)
        return by_stream(made)[:new_rows], Chain(moves, *first_halves(grad, moves[0]))

    grad_comp_bias = jnp.sum(grad_comp.astype(F32), (0, 1))
    targets = jnp.stack([(me + shift) % seq_parts for shift in range(seq_parts)]).astype(jnp.int32)
    input_parts = input_grad(targets, d_rows, x_rows, d_hidden, gain_first, seq_parts)
    input_rows = send(input_parts)

    grad_shift_first = jnp.sum(sum(shifts), 1)
    grad_gain_first = (jnp.sum(sum(alongs), 1) - shift_first * grad_shift_first) / gain_first
    vectors = jnp.concatenate(
        [
            jnp.concatenate(biases, 1).reshape(-1),
            grad_gain_first,
            grad_shift_first,
            grad_gain_second,
            grad_shift_second,
            grad_bias_down,
        ]
    )
    count = vectors.shape[0]
    hidden_sums = jnp.zeros((2, grad_bias_half.shape[0]), F32)
    hidden_sums = lax.dynamic_update_slice(hidden_sums, grad_bias_half[None], (core_bit, 0))
    comp_sums = jnp.zeros((seq_parts, grad_comp_bias.shape[0]), F32)
    comp_sums = lax.dynamic_update_slice(comp_sums, grad_comp_bias[None], (me, 0))
    vectors = jnp.concatenate([vectors, hidden_sums.reshape(-1), comp_sums.reshape(-1)])
    vector = Chain([("add", [(name, 1)]) for name in bit_names], [], [vectors.reshape(1, -1, DH)])

    one, two = groups
    def finished(column, group, results):
        own = group.gives[0]
        return finish(bits, column, len(groups), own, swap(own, *core), results)

    turn, results = 0, []
    pinned = {
        1: input_parts,
        2: [input_rows[1]],
        6: [input_rows[-1]],
        7: [*input_rows[2:-1]],
    }
    comp = None
    while len(two.moves) > 1 or vector.moves:
        active = [one, two] + [comp] * (turn > 1) + [vector] * (turn > 1)
        active = [c for c in active if len(c.moves) > (c in groups)]
        fence = pinned.get(turn, [])
        if turn == 8:
            results = finished(0, one, results)
            grad_w_comp = widen(comp.gives[0][0]).reshape(w_comp.shape)
            grad_inputs = by_stream(place_rows(input_rows, owners))
            fence = [*fence, *results, grad_w_comp, grad_inputs]
        through = [up_sum, memory_all] if turn == 0 else []
        through = round_of(active, bits, bit_names, fence, through)
        if turn == 0:
            up_sum = lax.all_gather(through[0], "dp", tiled=True)
            new_compressed, comp = compress(through[1])
            pinned[2] = [*pinned[2], new_compressed]
            pinned[3] = [output]
            grad_w_down, grad_w_up = widen(down_sum), widen(up_sum, True)
            pinned[4] = [grad_w_down]
            pinned[5] = [grad_w_up]
        turn += 1
    vectors = vector.gives[0].reshape(-1)

    results = finished(1, two, results)
    grad_w_query, grad_w_rel, grad_w_key, grad_w_value, grad_w_out = results

    totals = vectors[:count].reshape(-1, width)
    hidden_sums = vectors[count : count + hidden_sums.size].reshape(
        [2, 1 << len(wide)] + [2] * len(line) + [piece]
    )
    for step in reversed(line):
        hidden_sums = pick(hidden_sums, bit_of(*step), 2)
    grad_bias_up = jnp.swapaxes(hidden_sums, 0, 1).reshape(-1)
    comp_sums = vectors[count + grad_bias_half.size * 2 :].reshape(comp_sums.shape)
    grad_comp_bias = pick(comp_sums, me, 0)

    return (
        output,
        grad_inputs,
        new_compressed,
        totals[2],
        totals[3],
        grad_w_query,
        grad_w_key,
        grad_w_value,
        grad_w_rel,
        totals[0],
        totals[1],
        grad_w_out,
        totals[4],
        totals[5],
        grad_w_up,
        grad_bias_up,
        grad_w_down,
        totals[6],
        grad_w_comp,
        grad_comp_bias,
    )


def on_device(*arrays):
    streams = arrays[0].shape[1]
    dp_parts, seq_parts = lax.axis_size("dp"), lax.axis_size("seq")
    fits = streams == seq_parts and seq_parts > 1 and dp_parts >= 4
    powers = (seq_parts & (seq_parts - 1)) == 0 and (dp_parts & (dp_parts - 1)) == 0
    plan = own_streams_plan if fits and powers else split_rows_plan
    return plan(*arrays)


def solution(mesh):
    in_specs = (
        P("seq", "dp", None),
        P("seq", "dp", None),
        P("seq", "dp", None),
        P("dp"),
        P(),
        P(),
        P(),
        P(),
        P(),
        P(),
        P(),
        P(),
        P(),
        P(),
        P(),
        P(None, "seq"),
        P("seq"),
        P("seq", None),
        P(),
        P(None, None, "seq"),
        P("seq"),
        P("seq", "dp", None),
        P(None, "dp", "seq"),
    )
    out_specs = (
        P("seq", "dp", None),
        P("seq", "dp", None),
        P(None, "dp", "seq"),
        P(),
        P(),
        P(),
        P(),
        P(),
        P(),
        P(),
        P(),
        P(),
        P(),
        P(),
        P(None, "seq"),
        P("seq"),
        P("seq", None),
        P(),
        P(None, None, "seq"),
        P("seq"),
    )
    return jax.shard_map(
        on_device, mesh=mesh, in_specs=in_specs, out_specs=out_specs, check_vma=False
    )
```
